32 devices in a mesh: seq: 4 (over y, x), fsdp: 8 (over z, core).
Axes of the slice: x: 2, y: 2, z: 4, core: 2. Of those that a mesh axis runs over, the one named last changes fastest.
Arguments:
- tokens: bfloat16 [8, 1024, 2048], P('fsdp', 'seq'), may hold values from -6 to 6
- positions: int32 [8, 1024], P('fsdp'), may hold values from 0 to 1023, as said below
- attn_gain: bfloat16 [2048], P(('seq', 'fsdp')), may hold values from 0.099609375 to 1.8984375
- query_weight: bfloat16 [2048, 2048], P(('seq', 'fsdp')), may hold values from -0.25 to 0.25
- key_weight: bfloat16 [2048, 256], P(('seq', 'fsdp')), may hold values from -0.125 to 0.125
- value_weight: bfloat16 [2048, 256], P(('seq', 'fsdp')), may hold values from -0.125 to 0.125
- output_weight: bfloat16 [2048, 2048], P(('seq', 'fsdp')), may hold values from -0.5 to 0.5
- ffn_gain: bfloat16 [2048], P(('seq', 'fsdp')), may hold values from 0.099609375 to 1.8984375
- gate_weight: bfloat16 [2048, 5632], P(('seq', 'fsdp')), may hold values from -0.125 to 0.125
- up_weight: bfloat16 [2048, 5632], P(('seq', 'fsdp')), may hold values from -0.125 to 0.125
- down_weight: bfloat16 [5632, 2048], P(('seq', 'fsdp')), may hold values from -0.078125 to 0.078125
- cotangent: bfloat16 [8, 1024, 2048], P('fsdp', 'seq'), may hold values from -6 to 6
Outputs:
- block_out: bfloat16 [8, 1024, 2048], P('fsdp', 'seq')
- grad_tokens: float32 [8, 1024, 2048], P('fsdp', 'seq')
- grad_attn_gain: float32 [2048], P(('seq', 'fsdp'))
- grad_query: float32 [2048, 2048], P(('seq', 'fsdp'))
- grad_key: float32 [2048, 256], P(('seq', 'fsdp'))
- grad_value: float32 [2048, 256], P(('seq', 'fsdp'))
- grad_output: float32 [2048, 2048], P(('seq', 'fsdp'))
- grad_ffn_gain: float32 [2048], P(('seq', 'fsdp'))
- grad_gate: float32 [2048, 5632], P(('seq', 'fsdp'))
- grad_up: float32 [2048, 5632], P(('seq', 'fsdp'))
- grad_down: float32 [5632, 2048], P(('seq', 'fsdp'))
The draws below stay inside these ranges and needn't reach their ends.
Inputs may be any that keep to these rules, and one draw needn't show every extreme that they name: Each sequence's positions are 0 to 1023, each once, in whole blocks of 256: entries j * 256 to (j + 1) * 256 - 1 hold i * 256 to (i + 1) * 256 - 1 in rising order for some i.
All inputs are finite; a program needn't handle non-finite values.
Results may differ from the reference program's by a relative error of at most 0.02.
Values may be sent and summed in bfloat16 or wider, within the bound.
No kernel may reach another device: no remote copies, remote signals or barrier semaphores. Data moves between devices by JAX's collectives and lax.ppermute only.
A program may use at most 384 MiB of HBM per device.

```python
import math
import jax
import jax.numpy as jnp
from jax import lax

D = 2048
HEADS = 32
KV_HEADS = 4
HEAD_DIM = 64
FF = 5632
STRETCH = 256
SEQUENCES = 8
LENGTH = 1024


def draw_positions(key, part):
    key = jax.random.fold_in(key, 11)
    block_count = LENGTH // STRETCH
    seq_keys = jax.random.split(key, SEQUENCES)
    orders = jax.vmap(lambda one_key: jax.random.permutation(one_key, block_count))(seq_keys)
    position_table = orders.astype(jnp.int32)[:, :, None] * STRETCH + jnp.arange(STRETCH, dtype=jnp.int32)[None, None, :]
    return position_table.reshape(SEQUENCES, LENGTH).astype(jnp.int32)


def block_levels(own_key, extent, pieces, least, top_value):
    def one(position, blocks):
        steps = jax.random.uniform(jax.random.fold_in(jax.random.fold_in(own_key, 6), position), (blocks,), jnp.float32, least / len(pieces), top_value / len(pieces))
        return jnp.repeat(jnp.exp(steps), extent[position] // blocks).reshape((-1,) + (1,) * (len(extent) - position - 1))

    gain = one(*pieces[0])
    for cut in pieces[1:]:
        gain = gain * one(*cut)
    return gain


def bell_draw(key, shape, width, bound, pieces=(), kind=jnp.bfloat16):
    factor_of = block_levels(key, shape, pieces, -0.22, 0.18) if pieces else 1.0
    array = jax.random.normal(key, shape, jnp.float32) * width * factor_of
    return jnp.minimum(jnp.maximum(array, -bound), bound).astype(kind)


def setup_inputs(seed: int = 0) -> dict:
    key_of = jax.random.split(jax.random.key(seed), 13)
    return {
        "tokens": bell_draw(key_of[0], (SEQUENCES, LENGTH, D), 1.0, 6.0, ((0, 8), (1, 4))),
        "positions": draw_positions(jax.random.fold_in(key_of[12], 71), 0),
        "attn_gain": jnp.clip(1.0 + 0.18 * jax.random.normal(key_of[2], (D,), jnp.float32), 0.099609375, 1.8984375).astype(jnp.bfloat16),
        "query_weight": bell_draw(key_of[3], (D, D), (D // 4) ** -0.5, 0.25, ((0, 32),)),
        "key_weight": bell_draw(key_of[4], (D, KV_HEADS * HEAD_DIM), D ** -0.5, 0.125, ((0, 32),)),
        "value_weight": bell_draw(key_of[5], (D, KV_HEADS * HEAD_DIM), D ** -0.5, 0.125, ((0, 32),)),
        "output_weight": bell_draw(key_of[6], (D, D), (D // 16) ** -0.5, 0.5, ((0, 32),)),
        "ffn_gain": jnp.clip(1.0 + 0.18 * jax.random.normal(key_of[7], (D,), jnp.float32), 0.099609375, 1.8984375).astype(jnp.bfloat16),
        "gate_weight": bell_draw(key_of[8], (D, FF), D ** -0.5, 0.125, ((0, 32),)),
        "up_weight": bell_draw(key_of[9], (D, FF), D ** -0.5, 0.125, ((0, 32),)),
        "down_weight": bell_draw(key_of[10], (FF, D), FF ** -0.5, 0.078125, ((0, 32),)),
        "cotangent": bell_draw(key_of[11], (SEQUENCES, LENGTH, D), 1.0, 6.0, ((0, 8), (1, 4))),
    }


@jax.custom_vjp
def low(v):
    return lax.optimization_barrier(v.astype(jnp.bfloat16)).astype(jnp.float32)

@jax.custom_vjp
def low_back(v):
    return v

def low_keep(v):
    return (low(v), None)

def low_pass(kept, grad):
    return (grad,)

def back_keep(v):
    return (v, None)

def back_low(kept, grad):
    return (low(grad),)
low.defvjp(low_keep, low_pass)
low_back.defvjp(back_keep, back_low)
EPSILON = 1e-05
MASK_FILL = -1e+30
HIGH = lax.Precision.HIGHEST

def rope_tables(where_at):
    half_dim = HEAD_DIM // 2
    frequency = 1.0 / 10000.0 ** (jnp.arange(half_dim, dtype=jnp.float32) * 2.0 / HEAD_DIM)
    angles = where_at.astype(jnp.float32)[:, None] * frequency[None, :]
    return (jnp.concatenate([jnp.cos(angles), jnp.cos(angles)], -1), jnp.concatenate([jnp.sin(angles), jnp.sin(angles)], -1))

def rotate(values, cosine, sine_table):
    half_dim = values.shape[-1] // 2
    turned = jnp.concatenate([-values[..., half_dim:], values[..., :half_dim]], -1)
    return values * cosine + turned * sine_table

def norm_rows(values):
    return values * lax.rsqrt(lax.optimization_barrier(jnp.mean(values * values, -1, keepdims=True)) + EPSILON)

def attend(block_data):
    query_rot, key_rot, value_rows, where_at = block_data
    seq_len = where_at.shape[0]
    group_size = HEADS // KV_HEADS
    query_heads = query_rot.reshape(seq_len, KV_HEADS, group_size, HEAD_DIM)
    scores = jnp.einsum('qkgd,jkd->kgqj', query_heads, key_rot, precision=HIGH) * (1.0 / math.sqrt(HEAD_DIM))
    scores = low_back(scores)
    allowed = where_at[None, :] <= where_at[:, None]
    scores = jnp.where(allowed[None, None], scores, MASK_FILL)
    probabilities = low(jax.nn.softmax(scores, axis=-1))
    mixed = jnp.einsum('kgqj,jkd->qkgd', probabilities, value_rows, precision=HIGH)
    return mixed.reshape(seq_len, HEADS * HEAD_DIM)

def reference(tokens, positions, attn_gain, query_weight, key_weight, value_weight, output_weight, ffn_gain, gate_weight, up_weight, down_weight, cotangent):

    def forward_pass(token_rows, gain_one, query_full, key_full, value_full, output_full, gain_two, gate_full, up_full, down_full):
        seq_count = token_rows.shape[0]
        seq_len = token_rows.shape[1]
        flat_rows = token_rows.reshape(seq_count * seq_len, D)
        normed_one = low(norm_rows(flat_rows) * gain_one)
        query_proj = low_back(jnp.dot(normed_one, query_full, precision=HIGH))
        key_proj = low_back(jnp.dot(normed_one, key_full, precision=HIGH))
        value_proj = low(low_back(jnp.dot(normed_one, value_full, precision=HIGH)))
        cosine, sine_table = rope_tables(positions.reshape(-1))
        query_rot = low(rotate(query_proj.reshape(-1, HEADS, HEAD_DIM), cosine[:, None], sine_table[:, None]))
        key_rot = low(rotate(key_proj.reshape(-1, KV_HEADS, HEAD_DIM), cosine[:, None], sine_table[:, None]))
        mixed = lax.map(jax.checkpoint(attend), (query_rot.reshape(seq_count, seq_len, HEADS, HEAD_DIM), key_rot.reshape(seq_count, seq_len, KV_HEADS, HEAD_DIM), value_proj.reshape(seq_count, seq_len, KV_HEADS, HEAD_DIM), positions))
        attended = low(low_back(mixed.reshape(-1, D)))
        middle = flat_rows + low_back(jnp.dot(attended, output_full, precision=HIGH))
        normed_two = low(norm_rows(middle) * gain_two)
        gate_rows = low_back(jnp.dot(normed_two, gate_full, precision=HIGH))
        up_rows = low_back(jnp.dot(normed_two, up_full, precision=HIGH))
        hidden = low(jax.nn.silu(gate_rows) * up_rows)
        result_rows = middle + low_back(jnp.dot(hidden, down_full, precision=HIGH))
        return result_rows.reshape(seq_count, seq_len, D)
    inputs = tuple((item.astype(jnp.float32) for item in (tokens, attn_gain, query_weight, key_weight, value_weight, output_weight, ffn_gain, gate_weight, up_weight, down_weight)))
    result_rows, pullback = jax.vjp(forward_pass, *inputs)
    gradient = pullback(cotangent.astype(jnp.float32))
    return (result_rows.astype(jnp.bfloat16), gradient[0], gradient[1], gradient[2], gradient[3], gradient[4], gradient[5], gradient[6], gradient[7], gradient[8], gradient[9])
```

```python
import functools
import math

import jax
import jax.numpy as jnp
from jax import lax
from jax.experimental import pallas as pl
from jax.experimental.pallas import tpu as pltpu
from jax.sharding import PartitionSpec as P

HEADS = 32
KV_HEADS = 4
HEAD_DIM = 64
HALF = HEAD_DIM // 2
GROUP = HEADS // KV_HEADS
EPSILON = 1e-05
SCALE = 1.0 / math.sqrt(HEAD_DIM)
LOW = jnp.bfloat16
FULL = jnp.float32


def dot(a, b, dims=((1,), (0,)), out=FULL):
    return lax.dot_general(a, b, (dims, ((), ())), preferred_element_type=out)


def rope_tables(where_at):
    frequency = 1.0 / 10000.0 ** (jnp.arange(HALF, dtype=FULL) * 2.0 / HEAD_DIM)
    angles = frequency[:, None] * where_at.astype(FULL)[None, :]
    return jnp.cos(angles), jnp.sin(angles)


def attend_kernel(heads, kvs, span, order_ref, rank_ref, qkv_ref, cos_ref, sin_ref,
                  qrot_ref, kv_ref, att_ref, mix_ref, lse_ref, keys_ref):
    count = cos_ref.shape[1] // span
    qw, kw = heads * HEAD_DIM, kvs * HEAD_DIM
    cosine, sine = cos_ref[...], sin_ref[...]

    def rotated(row):
        one, two = qkv_ref[row:row + HALF, :], qkv_ref[row + HALF:row + HEAD_DIM, :]
        return jnp.concatenate([one * cosine - two * sine, two * cosine + one * sine], 0)

    for h in range(heads):
        qrot_ref[h * HEAD_DIM:(h + 1) * HEAD_DIM, :] = rotated(h * HEAD_DIM).astype(LOW)
    for k in range(kvs):
        turned = rotated(qw + k * HEAD_DIM).astype(LOW)
        kv_ref[k * HEAD_DIM:(k + 1) * HEAD_DIM, :] = turned
        keys_ref[k] = (turned.astype(FULL) * SCALE).T.astype(LOW)
    kv_ref[kw:, :] = qkv_ref[qw + kw:, :].astype(LOW)

    def one_block(qb, _):
        cols = pl.ds(pl.multiple_of(qb * span, span), span)
        rank = rank_ref[qb]

        def step(at, state, diagonal):
            rows = pl.ds(pl.multiple_of(order_ref[at] * span, span), span)
            out = []
            for h in range(heads):
                top, total, mixed = state[h]
                k = h * kvs // heads
                scores = dot(keys_ref[k, rows, :], qrot_ref[h * HEAD_DIM:(h + 1) * HEAD_DIM, cols])
                if diagonal:
                    key_at = lax.broadcasted_iota(jnp.int32, (span, span), 0)
                    query_at = lax.broadcasted_iota(jnp.int32, (span, span), 1)
                    scores = jnp.where(key_at <= query_at, scores, -1e30)
                new_top = jnp.maximum(top, jnp.max(scores, 0, keepdims=True))
                weights = jnp.exp(scores - new_top)
                fade = jnp.exp(top - new_top)
                total = total * fade + jnp.sum(weights, 0, keepdims=True)
                values = kv_ref[kw + k * HEAD_DIM:kw + (k + 1) * HEAD_DIM, rows]
                mixed = mixed * fade + dot(values, weights.astype(LOW))
                out.append((new_top, total, mixed))
            return out

        start = [(jnp.full((1, span), -1e30, FULL), jnp.zeros((1, span), FULL),
                  jnp.zeros((HEAD_DIM, span), FULL)) for _ in range(heads)]
        state = lax.fori_loop(0, rank, lambda at, st: step(at, st, False), start)
        state = step(rank, state, True)
        for h in range(heads):
            top, total, mixed = state[h]
            mixed = mixed / total
            mix_ref[h * HEAD_DIM:(h + 1) * HEAD_DIM, cols] = mixed
            att_ref[h * HEAD_DIM:(h + 1) * HEAD_DIM, cols] = mixed.astype(LOW)
            lse_ref[h:h + 1, cols] = top + jnp.log(total)
        return 0

    lax.fori_loop(0, count, one_block, 0)


def attend(order, rank, qkv, cosine, sine, heads, kvs, span):
    tokens = qkv.shape[1]
    qw, kw = heads * HEAD_DIM, kvs * HEAD_DIM
    vmem = pl.BlockSpec(memory_space=pltpu.VMEM)
    smem = pl.BlockSpec(memory_space=pltpu.SMEM)
    return pl.pallas_call(
        functools.partial(attend_kernel, heads, kvs, span),
        out_shape=(
            jax.ShapeDtypeStruct((qw, tokens), LOW),
            jax.ShapeDtypeStruct((2 * kw, tokens), LOW),
            jax.ShapeDtypeStruct((qw, tokens), LOW),
            jax.ShapeDtypeStruct((qw, tokens), FULL),
            jax.ShapeDtypeStruct((heads, tokens), FULL),
        ),
        in_specs=[smem, smem, vmem, vmem, vmem],
        out_specs=(vmem,) * 5,
        scratch_shapes=[pltpu.VMEM((kvs, tokens, HEAD_DIM), LOW)],
        compiler_params=pltpu.CompilerParams(vmem_limit_bytes=40 << 20),
        cost_estimate=pl.CostEstimate(
            flops=4 * qw * tokens * tokens, bytes_accessed=12 * qw * tokens, transcendentals=heads * tokens * tokens
        ),
        name="attend",
    )(order, rank, qkv, cosine, sine)


def attend_back_kernel(heads, kvs, span, order_ref, rank_ref, qrot_ref, kv_ref, grad_ref, mix_ref, lse_ref,
                       cos_ref, sin_ref, out_ref, keys_ref, values_ref, delta_ref, dkv_ref):
    count = cos_ref.shape[1] // span
    qw, kw = heads * HEAD_DIM, kvs * HEAD_DIM
    for k in range(kvs):
        keys_ref[k] = (kv_ref[k * HEAD_DIM:(k + 1) * HEAD_DIM, :].astype(FULL) * SCALE).T.astype(LOW)
        values_ref[k] = kv_ref[kw + k * HEAD_DIM:kw + (k + 1) * HEAD_DIM, :].astype(FULL).T.astype(LOW)
    for h in range(heads):
        rows = slice(h * HEAD_DIM, (h + 1) * HEAD_DIM)
        delta_ref[h:h + 1, :] = jnp.sum(grad_ref[rows, :].astype(FULL) * mix_ref[rows, :], 0, keepdims=True)
    dkv_ref[...] = jnp.zeros_like(dkv_ref)

    def one_block(qb, _):
        cols = pl.ds(pl.multiple_of(qb * span, span), span)
        rank = rank_ref[qb]

        def step(at, state, diagonal):
            rows = pl.ds(pl.multiple_of(order_ref[at] * span, span), span)
            out = []
            dkeys = [None] * kvs
            dvalues = [None] * kvs
            for h in range(heads):
                k = h * kvs // heads
                mine = slice(h * HEAD_DIM, (h + 1) * HEAD_DIM)
                query = qrot_ref[mine, cols]
                grad = grad_ref[mine, cols]
                scores = dot(keys_ref[k, rows, :], query)
                weights = jnp.exp(scores - lse_ref[h:h + 1, cols])
                if diagonal:
                    key_at = lax.broadcasted_iota(jnp.int32, (span, span), 0)
                    query_at = lax.broadcasted_iota(jnp.int32, (span, span), 1)
                    weights = jnp.where(key_at <= query_at, weights, 0.0)
                grad_probs = dot(values_ref[k, rows, :], grad)
                grad_scores = (weights * (grad_probs - delta_ref[h:h + 1, cols])).astype(LOW)
                key_t = kv_ref[k * HEAD_DIM:(k + 1) * HEAD_DIM, rows]
                out.append(state[h] + dot(key_t, grad_scores))
                dk = dot(query, grad_scores, ((1,), (1,)))
                dv = dot(grad, weights.astype(LOW), ((1,), (1,)))
                dkeys[k] = dk if dkeys[k] is None else dkeys[k] + dk
                dvalues[k] = dv if dvalues[k] is None else dvalues[k] + dv
            for k in range(kvs):
                mine = slice(k * HEAD_DIM, (k + 1) * HEAD_DIM)
                dkv_ref[mine, rows] += dkeys[k]
                mine = slice(kw + k * HEAD_DIM, kw + (k + 1) * HEAD_DIM)
                dkv_ref[mine, rows] += dvalues[k]
            return out

        state = [jnp.zeros((HEAD_DIM, span), FULL) for _ in range(heads)]
        state = lax.fori_loop(0, rank, lambda at, st: step(at, st, False), state)
        state = step(rank, state, True)
        cosine, sine = cos_ref[:, cols], sin_ref[:, cols]
        for h in range(heads):
            one, two = state[h][:HALF] * SCALE, state[h][HALF:] * SCALE
            out_ref[h * HEAD_DIM:h * HEAD_DIM + HALF, cols] = (one * cosine + two * sine).astype(LOW)
            out_ref[h * HEAD_DIM + HALF:(h + 1) * HEAD_DIM, cols] = (two * cosine - one * sine).astype(LOW)
        return 0

    lax.fori_loop(0, count, one_block, 0)
    cosine, sine = cos_ref[...], sin_ref[...]
    for k in range(kvs):
        top = k * HEAD_DIM
        one, two = dkv_ref[top:top + HALF, :] * SCALE, dkv_ref[top + HALF:top + HEAD_DIM, :] * SCALE
        out_ref[qw + top:qw + top + HALF, :] = (one * cosine + two * sine).astype(LOW)
        out_ref[qw + top + HALF:qw + top + HEAD_DIM, :] = (two * cosine - one * sine).astype(LOW)
    out_ref[qw + kw:, :] = dkv_ref[kw:, :].astype(LOW)


def attend_back(order, rank, qrot, kv, grad, mix, lse, cosine, sine, heads, kvs, span):
    tokens = qrot.shape[1]
    qw, kw = heads * HEAD_DIM, kvs * HEAD_DIM
    vmem = pl.BlockSpec(memory_space=pltpu.VMEM)
    smem = pl.BlockSpec(memory_space=pltpu.SMEM)
    return pl.pallas_call(
        functools.partial(attend_back_kernel, heads, kvs, span),
        out_shape=jax.ShapeDtypeStruct((qw + 2 * kw, tokens), LOW),
        in_specs=[smem, smem] + [vmem] * 7,
        out_specs=vmem,
        scratch_shapes=[
            pltpu.VMEM((kvs, tokens, HEAD_DIM), LOW),
            pltpu.VMEM((kvs, tokens, HEAD_DIM), LOW),
            pltpu.VMEM((heads, tokens), FULL),
            pltpu.VMEM((2 * kw, tokens), FULL),
        ],
        compiler_params=pltpu.CompilerParams(vmem_limit_bytes=40 << 20),
        cost_estimate=pl.CostEstimate(
            flops=10 * qw * tokens * tokens, bytes_accessed=12 * qw * tokens, transcendentals=heads * tokens * tokens
        ),
        name="attend_back",
    )(order, rank, qrot, kv, grad, mix, lse, cosine, sine)


def layer(seq_size, fsdp_size, tokens, positions, attn_gain, query_weight, key_weight, value_weight, output_weight,
          ffn_gain, gate_weight, up_weight, down_weight, cotangent):
    span, width = tokens.shape[1:]
    heads = HEADS // seq_size
    kvs = max(1, KV_HEADS // seq_size)
    shared = max(1, seq_size // KV_HEADS)
    qw, kw = heads * HEAD_DIM, kvs * HEAD_DIM
    own_rows = query_weight.shape[0]
    hidden_own = gate_weight.shape[1] // seq_size
    here = lax.axis_index("seq")

    def swap(x, j):
        return lax.ppermute(x, "seq", [(i, i ^ j) for i in range(seq_size)])

    def seq_gather(x):
        if seq_size != 4:
            return jnp.concatenate([x] + [swap(x, j) for j in range(1, seq_size)], 0)
        half = x.shape[0] // 2
        a, b = x[:half], x[half:]
        ax, by = swap(a, 1), swap(b, 2)
        ay, bx = swap(a, 2), swap(b, 1)
        ad, bd = swap(ax, 2), swap(by, 1)
        return jnp.concatenate([a, b, ax, bx, ay, by, ad, bd], 0)

    def seq_scatter(x):
        blocks = [x[j * span:(j + 1) * span] for j in range(seq_size)]
        if seq_size != 4:
            total = blocks[0].astype(FULL)
            for j in range(1, seq_size):
                total = total + swap(blocks[j], j).astype(FULL)
            return total
        half = span // 2
        a, b = [blk[:half] for blk in blocks], [blk[half:] for blk in blocks]
        da, db = swap(a[3], 2), swap(b[3], 1)
        ya, xb = swap(a[2], 2), swap(b[1], 1)
        xa = swap((a[1].astype(FULL) + da.astype(FULL)).astype(LOW), 1)
        yb = swap((b[2].astype(FULL) + db.astype(FULL)).astype(LOW), 2)
        return jnp.concatenate([
            a[0].astype(FULL) + ya.astype(FULL) + xa.astype(FULL),
            b[0].astype(FULL) + xb.astype(FULL) + yb.astype(FULL),
        ], 0)

    def spread(pieces_for):
        got = [pieces_for(here)] + [swap(pieces_for(here ^ j), j) for j in range(1, seq_size)]
        stack = jnp.stack(got)
        return jnp.concatenate(
            [lax.dynamic_index_in_dim(stack, here ^ t, 0, False) for t in range(seq_size)], 0
        )

    def collect(x):
        blocks = x.reshape(seq_size, own_rows, x.shape[1])
        got = jnp.stack([lax.dynamic_index_in_dim(blocks, here, 0, False)] + [
            swap(lax.dynamic_index_in_dim(blocks, here ^ j, 0, False), j) for j in range(1, seq_size)
        ])
        return jnp.stack([lax.dynamic_index_in_dim(got, here ^ t, 0, False) for t in range(seq_size)])

    def fsdp_gather(x):
        return lax.all_gather(x, "fsdp", axis=0, tiled=True)

    def fsdp_scatter(x):
        return lax.psum_scatter(x, "fsdp", scatter_dimension=0, tiled=True)

    def shuffled(x):
        return x.reshape(span, seq_size, fsdp_size, own_rows).swapaxes(1, 2).reshape(span, width)

    def unshuffled(x):
        return x.reshape(span, fsdp_size, seq_size, own_rows).swapaxes(1, 2).reshape(span, width)

    gain_one, gain_two = attn_gain.astype(FULL)[:, None], ffn_gain.astype(FULL)[:, None]

    def with_gain(weight, gain):
        return (weight.astype(FULL) * gain).astype(LOW)

    query_low, key_low, value_low = (with_gain(w, gain_one) for w in (query_weight, key_weight, value_weight))
    gate_low, up_low = (with_gain(w, gain_two) for w in (gate_weight, up_weight))

    def qkv_for(t):
        first = (t * heads // GROUP) * HEAD_DIM
        return jnp.concatenate([
            lax.dynamic_slice_in_dim(query_low, t * qw, qw, 1),
            lax.dynamic_slice_in_dim(key_low, first, kw, 1),
            lax.dynamic_slice_in_dim(value_low, first, kw, 1),
        ], 1)

    def gate_up_for(t):
        return jnp.concatenate([
            lax.dynamic_slice_in_dim(gate_low, t * hidden_own, hidden_own, 1),
            lax.dynamic_slice_in_dim(up_low, t * hidden_own, hidden_own, 1),
        ], 1)

    token_rows = tokens[0].astype(FULL)
    inv_one = lax.rsqrt(jnp.mean(token_rows * token_rows, -1, keepdims=True) + EPSILON)
    scaled_one = token_rows * inv_one
    normed_one = seq_gather(shuffled(scaled_one.astype(LOW)))
    qkv_full = fsdp_gather(spread(qkv_for))
    output_full = fsdp_gather(output_weight)
    gate_up_full = fsdp_gather(spread(gate_up_for))
    down_full = fsdp_gather(down_weight)
    upstream = seq_gather(cotangent[0])

    count = positions.shape[1] // span
    where_at = positions[0].reshape(count, span)
    where_at = jnp.stack([lax.dynamic_index_in_dim(where_at, here ^ j, 0, False) for j in range(count)])
    rank = where_at[:, 0] // span
    order = jnp.argsort(rank).astype(jnp.int32)
    cosine, sine = rope_tables(where_at.reshape(-1))

    qkv = dot(qkv_full, normed_one, ((0,), (1,)))
    qrot, kv, attended, mix, lse = attend(order, rank, qkv, cosine, sine, heads, kvs, span)
    branch = seq_scatter(dot(attended, output_full, ((0,), (0,)), LOW))
    middle = token_rows + branch

    inv_two = lax.rsqrt(jnp.mean(middle * middle, -1, keepdims=True) + EPSILON)
    scaled_two = middle * inv_two
    normed_two = seq_gather(shuffled(scaled_two.astype(LOW)))
    gate_full, up_full = gate_up_full[:, :hidden_own], gate_up_full[:, hidden_own:]
    gate_rows = dot(normed_two, gate_full)
    up_rows = dot(normed_two, up_full)
    sigmoid = jax.nn.sigmoid(gate_rows)
    silu = gate_rows * sigmoid
    hidden = (silu * up_rows).astype(LOW)
    grad_hidden = dot(upstream, down_full, ((1,), (1,)))
    grad_gaterows = (grad_hidden * up_rows * sigmoid * (1.0 + gate_rows * (1.0 - sigmoid))).astype(LOW)
    grad_uprows = (grad_hidden * silu).astype(LOW)
    grad_down = fsdp_scatter(dot(hidden, upstream, ((0,), (0,)), LOW))
    grad_gate = fsdp_scatter(dot(normed_two, grad_gaterows, ((0,), (0,)), LOW))
    grad_up = fsdp_scatter(dot(normed_two, grad_uprows, ((0,), (0,)), LOW))
    grad_two = (dot(grad_gaterows, gate_full, ((1,), (1,))) + dot(grad_uprows, up_full, ((1,), (1,)))).astype(LOW)
    scaled_grad = unshuffled(seq_scatter(grad_two))
    block_out = (middle + seq_scatter(dot(hidden, down_full, out=LOW))).astype(LOW)
    grad_middle = cotangent[0].astype(FULL) + inv_two * (
        scaled_grad - scaled_two * jnp.mean(scaled_grad * scaled_two, -1, keepdims=True)
    )

    grad_branch = seq_gather(grad_middle.astype(LOW))
    grad_output = fsdp_scatter(dot(attended, grad_branch, out=LOW))
    grad_attended = dot(output_full, grad_branch, ((1,), (1,)), LOW)
    grad_qkv = attend_back(order, rank, qrot, kv, grad_attended, mix, lse, cosine, sine, heads, kvs, span)
    grad_qkv_weight = fsdp_scatter(dot(normed_one, grad_qkv, ((0,), (1,)), LOW))
    grad_one = dot(grad_qkv, qkv_full, ((0,), (1,)), LOW)
    scaled_grad = unshuffled(seq_scatter(grad_one))
    grad_tokens = grad_middle + inv_one * (
        scaled_grad - scaled_one * jnp.mean(scaled_grad * scaled_one, -1, keepdims=True)
    )

    def whole_rows(x):
        return x.swapaxes(0, 1).reshape(own_rows, -1)

    grad_gate, grad_up = (whole_rows(collect(g).astype(FULL)) for g in (grad_gate, grad_up))
    got = collect(grad_qkv_weight).astype(FULL)
    grad_query = whole_rows(got[:, :, :qw])

    def of_heads(x):
        return whole_rows(x.reshape(seq_size // shared, shared, own_rows, kw).sum(1))

    grad_key, grad_value = of_heads(got[:, :, qw:qw + kw]), of_heads(got[:, :, qw + kw:])
    grad_attn_gain = (
        jnp.sum(grad_query * query_weight.astype(FULL), 1)
        + jnp.sum(grad_key * key_weight.astype(FULL), 1)
        + jnp.sum(grad_value * value_weight.astype(FULL), 1)
    )
    grad_ffn_gain = jnp.sum(grad_gate * gate_weight.astype(FULL), 1) + jnp.sum(grad_up * up_weight.astype(FULL), 1)
    return (
        block_out[None],
        grad_tokens[None],
        grad_attn_gain,
        grad_query * gain_one,
        grad_key * gain_one,
        grad_value * gain_one,
        grad_output.astype(FULL),
        grad_ffn_gain,
        grad_gate * gain_two,
        grad_up * gain_two,
        grad_down.astype(FULL),
    )


def solution(mesh):
    rows, vector, matrix = P("fsdp", "seq", None), P(("seq", "fsdp")), P(("seq", "fsdp"), None)
    return jax.shard_map(
        functools.partial(layer, mesh.shape["seq"], mesh.shape["fsdp"]),
        mesh=mesh,
        in_specs=(
            rows, P("fsdp", None), vector, matrix, matrix, matrix, matrix, vector, matrix, matrix, matrix, rows,
        ),
        out_specs=(rows, rows, vector, matrix, matrix, matrix, matrix, vector, matrix, matrix, matrix),
        check_vma=False,
    )
```

```python
import functools
import math

import jax
import jax.numpy as jnp
from jax import lax
from jax.experimental import pallas as pl
from jax.experimental.pallas import tpu as pltpu
from jax.sharding import PartitionSpec as P

HEADS = 32
KV_HEADS = 4
HEAD_DIM = 64
HALF = HEAD_DIM // 2
GROUP = HEADS // KV_HEADS
EPSILON = 1e-05
SCALE = 1.0 / math.sqrt(HEAD_DIM)
LOW = jnp.bfloat16
FULL = jnp.float32
VMEM = pl.BlockSpec(memory_space=pltpu.VMEM)
ANY = pl.BlockSpec(memory_space=pltpu.HBM)
SMEM = pl.BlockSpec(memory_space=pltpu.SMEM)
PARAMS = pltpu.CompilerParams(vmem_limit_bytes=60 << 20)
NN, NT, TN = ((1,), (0,)), ((1,), (1,)), ((0,), (0,))


def dot(a, b, dims=NN):
    return lax.dot_general(a, b, (dims, ((), ())), preferred_element_type=FULL)


def like(shape, dtype=LOW):
    return jax.ShapeDtypeStruct(shape, dtype)


def rope_tables(where_at):
    frequency = 1.0 / 10000.0 ** (jnp.arange(HALF, dtype=FULL) * 2.0 / HEAD_DIM)
    angles = frequency[:, None] * where_at.astype(FULL)[None, :]
    return jnp.cos(angles), jnp.sin(angles)


def regroup(x, outer, inner, rows):
    return jnp.concatenate(
        [x[:, (o * inner + i) * rows:(o * inner + i + 1) * rows] for i in range(inner) for o in range(outer)], 1
    )


def join(pieces, whole_ref):
    at = 0
    for piece in pieces:
        whole_ref[at:at + piece.shape[0], :] = piece[...]
        at += piece.shape[0]


def fetch(pieces, whole_ref, sems):
    copies, at = [], 0
    for i, piece in enumerate(pieces):
        rows = piece.shape[0]
        copies.append(pltpu.make_async_copy(piece, whole_ref.at[pl.ds(at, rows)], sems.at[i]))
        at += rows
    for copy in copies:
        copy.start()
    for copy in copies:
        copy.wait()


def arrivals(count):
    return pltpu.SemaphoreType.DMA((count,))


def call_own(kernel, out_shape, *args):
    return pl.pallas_call(
        kernel, out_shape=out_shape, in_specs=[VMEM] * len(args),
        out_specs=jax.tree.map(lambda _: VMEM, out_shape), compiler_params=PARAMS, name=kernel.func.__name__,
    )(*args)


def added(refs):
    total = refs[0][...].astype(FULL)
    for ref in refs[1:]:
        total = total + ref[...].astype(FULL)
    return total


def regroup_kernel(grid, x_ref, *out_refs):
    x = regroup(x_ref[...].astype(FULL), *grid).astype(LOW)
    rows = out_refs[0].shape[0]
    for i, ref in enumerate(out_refs):
        ref[...] = x[i * rows:(i + 1) * rows]


def middle_kernel(grid, parts, *refs):
    tokens_ref, refs = refs[0], refs[1:]
    per = (len(refs) - 2 - parts) // parts
    middle_ref, inv_ref, *normed_refs = refs[per * parts:]
    rows = normed_refs[0].shape[0]
    for i in range(parts):
        at = slice(i * rows, (i + 1) * rows)
        middle = tokens_ref[at, :].astype(FULL) + added(refs[i * per:(i + 1) * per])
        inv = lax.rsqrt(jnp.mean(middle * middle, -1, keepdims=True) + EPSILON)
        middle_ref[at, :] = middle
        inv_ref[at, :] = inv
        normed_refs[i][...] = regroup(middle * inv, *grid).astype(LOW)


def grad_middle_kernel(grid, parts, *refs):
    upstream_ref, middle_ref, inv_ref, refs = refs[0], refs[1], refs[2], refs[3:]
    per = (len(refs) - 1 - parts) // parts
    out_ref, *low_refs = refs[per * parts:]
    rows = low_refs[0].shape[0]
    for i in range(parts):
        at = slice(i * rows, (i + 1) * rows)
        inv = inv_ref[at, :]
        normed = middle_ref[at, :] * inv
        grad = regroup(added(refs[i * per:(i + 1) * per]), *grid)
        grad = upstream_ref[at, :].astype(FULL) + inv * (grad - normed * jnp.mean(grad * normed, -1, keepdims=True))
        out_ref[at, :] = grad
        low_refs[i][...] = grad.astype(LOW)


def grad_tokens_kernel(grid, parts, *refs):
    tokens_ref, grad_ref, refs, out_ref = refs[0], refs[1], refs[2:-1], refs[-1]
    per = len(refs) // parts
    rows = out_ref.shape[0] // parts
    for i in range(parts):
        at = slice(i * rows, (i + 1) * rows)
        tokens = tokens_ref[at, :].astype(FULL)
        normed = tokens * lax.rsqrt(jnp.mean(tokens * tokens, -1, keepdims=True) + EPSILON)
        grad = regroup(added(refs[i * per:(i + 1) * per]), *grid)
        out_ref[at, :] = grad_ref[at, :] + grad - normed * jnp.mean(grad * normed, -1, keepdims=True)


def block_out_kernel(parts, *refs):
    middle_ref, refs, out_ref = refs[0], refs[1:-1], refs[-1]
    per = len(refs) // parts
    rows = out_ref.shape[0] // parts
    for i in range(parts):
        at = slice(i * rows, (i + 1) * rows)
        out_ref[at, :] = (middle_ref[at, :] + added(refs[i * per:(i + 1) * per])).astype(LOW)


def rows_of(pieces):
    return sum(p.shape[0] for p in pieces)


def whole(shape):
    return pl.BlockSpec(shape, lambda i: (0,) * len(shape))


def columns(rows, width):
    return pl.BlockSpec((rows, width), lambda i: (0, i))


def by_rows(height, width):
    return pl.BlockSpec((height, width), lambda i: (i, 0))


def hidden_kernel(count, chunk, *refs):
    pieces, (weight_ref, slope_ref, hidden_ref, normed_ref, sems) = refs[:count], refs[count:]

    @pl.when(pl.program_id(0) == 0)
    def _():
        fetch(pieces, normed_ref, sems)

    both = dot(normed_ref[...], weight_ref[...])
    gate, up = both[:, :chunk], both[:, chunk:]
    sigmoid = jax.nn.sigmoid(gate)
    silu = gate * sigmoid
    slope = up * sigmoid * (1.0 + gate * (1.0 - sigmoid))
    slope_ref[...] = jnp.concatenate([slope, silu], 1).astype(LOW)
    hidden_ref[...] = (silu * up).T.astype(LOW)


def hidden_of(pieces, weight, chunk):
    tokens, (width, both) = rows_of(pieces), weight.shape
    return pl.pallas_call(
        functools.partial(hidden_kernel, len(pieces), chunk),
        grid=(both // (2 * chunk),),
        in_specs=[ANY] * len(pieces) + [columns(width, 2 * chunk)],
        out_specs=(columns(tokens, 2 * chunk), by_rows(chunk, tokens)),
        out_shape=(like((tokens, both)), like((both // 2, tokens))),
        scratch_shapes=[pltpu.VMEM((tokens, width), LOW), arrivals(len(pieces))],
        compiler_params=PARAMS,
        name="hidden_of",
    )(*pieces, weight)


def grad_down_kernel(count, *refs):
    pieces, (hidden_ref, out_ref, block_ref) = refs[:count], refs[count:]
    join(pieces, block_ref)
    out_ref[...] = dot(hidden_ref[...], block_ref[...]).astype(LOW)


def grad_down_of(hidden, pieces, block=256):
    tokens, width = rows_of(pieces), pieces[0].shape[1]
    return pl.pallas_call(
        functools.partial(grad_down_kernel, len(pieces)),
        grid=(width // block,),
        in_specs=[columns(p.shape[0], block) for p in pieces] + [whole(hidden.shape)],
        out_specs=columns(hidden.shape[0], block),
        out_shape=like((hidden.shape[0], width)),
        scratch_shapes=[pltpu.VMEM((tokens, block), LOW)],
        compiler_params=PARAMS,
        name="grad_down_of",
    )(*pieces, hidden)


def grad_gate_up_kernel(count, chunk, places_ref, *refs):
    pieces, refs = refs[:count], refs[count:]
    *blocks, slope_ref, out_ref, down_ref, upstream_ref, sems, block_sems = refs
    step, steps = pl.program_id(0), pl.num_programs(0)

    @pl.when(step == 0)
    def _():
        copies = []
        for i, block in enumerate(blocks):
            rows = block.shape[0]
            there = pl.ds(pl.multiple_of(places_ref[i] * rows, math.gcd(rows, 16)), rows)
            copies.append(pltpu.make_async_copy(block, down_ref.at[there], block_sems.at[i]))
        for copy in copies:
            copy.start()
        fetch(pieces, upstream_ref, sems)
        for copy in copies:
            copy.wait()

    def work(chunks):
        rows = pl.ds(pl.multiple_of(step * 2 * chunk, 2 * chunk), chunks * chunk)
        grad = dot(upstream_ref[...], down_ref[rows, :], NT)
        each = [grad[:, c * chunk:(c + 1) * chunk] for c in range(chunks) for _ in range(2)]
        width = chunks * 2 * chunk
        out_ref[:, :width] = (jnp.concatenate(each, 1) * slope_ref[:, :width].astype(FULL)).astype(LOW)

    odd = down_ref.shape[0] // chunk % 2

    @pl.when(step < steps - odd)
    def _():
        work(2)

    if odd:

        @pl.when(step == steps - 1)
        def _():
            work(1)


def grad_gate_up_of(pieces, places, blocks, slope, chunk):
    tokens, width = rows_of(pieces), pieces[0].shape[1]
    depth = rows_of(blocks)
    return pl.pallas_call(
        functools.partial(grad_gate_up_kernel, len(pieces), chunk),
        grid=(pl.cdiv(depth, 2 * chunk),),
        in_specs=[SMEM] + [ANY] * (len(pieces) + len(blocks)) + [columns(tokens, 4 * chunk)],
        out_specs=(columns(tokens, 4 * chunk), whole((depth, width))),
        out_shape=(like(slope.shape), like((depth, width))),
        scratch_shapes=[pltpu.VMEM((tokens, width), LOW), arrivals(len(pieces)), arrivals(len(blocks))],
        compiler_params=PARAMS,
        name="grad_gate_up_of",
    )(places, *pieces, *blocks, slope)


def grad_rows_kernel(first, grad_ref, weight_ref, *out_refs):
    grad = dot(grad_ref[...], weight_ref[:, first:], NT).astype(LOW)
    rows = out_refs[0].shape[0]
    for i, ref in enumerate(out_refs):
        ref[...] = grad[i * rows:(i + 1) * rows]


def grad_rows_of(grad, weight, piece_rows, block=256):
    tokens, width = grad.shape[0], weight.shape[0]
    count = tokens // piece_rows
    return pl.pallas_call(
        functools.partial(grad_rows_kernel, weight.shape[1] - grad.shape[1]),
        grid=(width // block,),
        in_specs=[whole(grad.shape), by_rows(block, weight.shape[1])],
        out_specs=(columns(piece_rows, block),) * count,
        out_shape=(like((piece_rows, width)),) * count,
        compiler_params=PARAMS,
        name="grad_rows_of",
    )(grad, weight)


def grad_weight_kernel(count, *refs):
    pieces, (grad_ref, out_ref, block_ref) = refs[:count], refs[count:]
    join(pieces, block_ref)
    out_ref[...] = dot(block_ref[...], grad_ref[...], TN).astype(LOW)


def grad_weight_of(pieces, grad, block=256):
    tokens, width = rows_of(pieces), pieces[0].shape[1]
    return pl.pallas_call(
        functools.partial(grad_weight_kernel, len(pieces)),
        grid=(width // block,),
        in_specs=[columns(p.shape[0], block) for p in pieces] + [whole(grad.shape)],
        out_specs=by_rows(block, grad.shape[1]),
        out_shape=like((width, grad.shape[1])),
        scratch_shapes=[pltpu.VMEM((tokens, block), LOW)],
        compiler_params=PARAMS,
        name="grad_weight_of",
    )(*pieces, grad)


def rows_kernel(left_ref, weight_ref, *refs):
    *out_refs, turned_ref = refs

    @pl.when(pl.program_id(0) == 0)
    def _():
        turned_ref[...] = left_ref[...].T

    weight = weight_ref[...].reshape(turned_ref.shape[1], weight_ref.shape[-1])
    out = dot(turned_ref[...], weight).astype(LOW)
    rows = out_refs[0].shape[0]
    for i, ref in enumerate(out_refs):
        ref[...] = out[i * rows:(i + 1) * rows]


def rows_of_product(left, weight, piece_rows, inner=None, block=256):
    depth, tokens = left.shape
    count = tokens // piece_rows
    if inner is None:
        width, spec = weight.shape[1], columns(depth, block)
    else:
        seq_size, fsdp_size, own_rows = inner
        width = weight.shape[0]
        per = width // seq_size // block
        weight = weight.reshape(fsdp_size, seq_size, own_rows, -1)
        spec = pl.BlockSpec((fsdp_size, 1, own_rows, block), lambda i: (0, i // per, 0, i % per))
    return pl.pallas_call(
        rows_kernel,
        grid=(width // block,),
        in_specs=[whole(left.shape), spec],
        out_specs=(columns(piece_rows, block),) * count,
        out_shape=(like((piece_rows, width)),) * count,
        scratch_shapes=[pltpu.VMEM((tokens, depth), LOW)],
        compiler_params=PARAMS,
        name="rows_of_product",
    )(left, weight)


def attention_weights_kernel(count, inner, *refs):
    tokens, grads = refs[:count], refs[count:2 * count]
    grad_qkv_ref, attended_ref, out_ref, block_ref = refs[2 * count:]
    seq_size, fsdp_size, own_rows = inner
    step, block = pl.program_id(0), block_ref.shape[1]
    across = out_ref.shape[1] - grad_qkv_ref.shape[0]
    join(tokens, block_ref)
    there = pl.ds(pl.multiple_of(step * block, block), block)
    out_ref[there, across:] = dot(grad_qkv_ref[...], block_ref[...]).T.astype(LOW)
    join(grads, block_ref)
    got = dot(attended_ref[...], block_ref[...]).astype(LOW)
    part = step * block // across
    first = step * block % across
    for f in range(fsdp_size):
        rows = pl.ds(pl.multiple_of((f * seq_size + part) * own_rows, own_rows), own_rows)
        out_ref[rows, pl.ds(pl.multiple_of(first, 128), block)] = got[f * own_rows:(f + 1) * own_rows]


def attention_weights_of(tokens, grads, grad_qkv, attended, inner, block=256):
    count, width = len(tokens), tokens[0].shape[1]
    shape = (width, grad_qkv.shape[0] + width // inner[0])
    return pl.pallas_call(
        functools.partial(attention_weights_kernel, count, inner),
        grid=(width // block,),
        in_specs=[columns(p.shape[0], block) for p in (*tokens, *grads)]
        + [whole(grad_qkv.shape), whole(attended.shape)],
        out_specs=whole(shape),
        out_shape=like(shape),
        scratch_shapes=[pltpu.VMEM((rows_of(tokens), block), LOW)],
        compiler_params=PARAMS,
        name="attention_weights_of",
    )(*tokens, *grads, grad_qkv, attended)


def attend_kernel(heads, kvs, span, pieces, order_ref, rank_ref, *refs):
    token_refs, refs = refs[:pieces], refs[pieces:]
    weight_ref, cos_ref, sin_ref, qrot_ref, kv_ref, att_ref, mix_ref, lse_ref, inv_ref, *scratch = refs
    keys_ref, qkv_ref, tokens_ref, sems = scratch
    fetch(token_refs, tokens_ref, sems)
    count = cos_ref.shape[1] // span
    for at in range(0, tokens_ref.shape[0], span):
        there = slice(at, at + span)
        values = tokens_ref[there, :].astype(FULL)
        inv = lax.rsqrt(jnp.mean(values * values, -1, keepdims=True) + EPSILON)
        qkv_ref[:, there] = (dot(tokens_ref[there, :], weight_ref[:, -qkv_ref.shape[0]:]) * inv).T
        inv_ref[:, there] = jnp.broadcast_to(inv, (span, 128)).T[:1]
    qw, kw = heads * HEAD_DIM, kvs * HEAD_DIM
    cosine, sine = cos_ref[...], sin_ref[...]

    def rotated(row):
        one, two = qkv_ref[row:row + HALF, :], qkv_ref[row + HALF:row + HEAD_DIM, :]
        return jnp.concatenate([one * cosine - two * sine, two * cosine + one * sine], 0)

    for h in range(heads):
        qrot_ref[h * HEAD_DIM:(h + 1) * HEAD_DIM, :] = rotated(h * HEAD_DIM).astype(LOW)
    for k in range(kvs):
        turned = rotated(qw + k * HEAD_DIM).astype(LOW)
        kv_ref[k * HEAD_DIM:(k + 1) * HEAD_DIM, :] = turned
        keys_ref[k] = (turned.astype(FULL) * SCALE).T.astype(LOW)
    kv_ref[kw:, :] = qkv_ref[qw + kw:, :].astype(LOW)

    def one_block(qb, _):
        cols = pl.ds(pl.multiple_of(qb * span, span), span)
        rank = rank_ref[qb]

        def step(at, state, diagonal):
            rows = pl.ds(pl.multiple_of(order_ref[at] * span, span), span)
            out = []
            for h in range(heads):
                top, total, mixed = state[h]
                k = h * kvs // heads
                scores = dot(keys_ref[k, rows, :], qrot_ref[h * HEAD_DIM:(h + 1) * HEAD_DIM, cols])
                if diagonal:
                    key_at = lax.broadcasted_iota(jnp.int32, (span, span), 0)
                    query_at = lax.broadcasted_iota(jnp.int32, (span, span), 1)
                    scores = jnp.where(key_at <= query_at, scores, -1e30)
                new_top = jnp.maximum(top, jnp.max(scores, 0, keepdims=True))
                weights = jnp.exp(scores - new_top)
                fade = jnp.exp(top - new_top)
                total = total * fade + jnp.sum(weights, 0, keepdims=True)
                values = kv_ref[kw + k * HEAD_DIM:kw + (k + 1) * HEAD_DIM, rows]
                mixed = mixed * fade + dot(values, weights.astype(LOW))
                out.append((new_top, total, mixed))
            return out

        start = [(jnp.full((1, span), -1e30, FULL), jnp.zeros((1, span), FULL),
                  jnp.zeros((HEAD_DIM, span), FULL)) for _ in range(heads)]
        state = lax.fori_loop(0, rank, lambda at, st: step(at, st, False), start)
        state = step(rank, state, True)
        for h in range(heads):
            top, total, mixed = state[h]
            mixed = mixed / total
            mix_ref[h * HEAD_DIM:(h + 1) * HEAD_DIM, cols] = mixed
            att_ref[h * HEAD_DIM:(h + 1) * HEAD_DIM, cols] = mixed.astype(LOW)
            lse_ref[h:h + 1, cols] = top + jnp.log(total)
        return 0

    lax.fori_loop(0, count, one_block, 0)


def attend(order, rank, pieces, weight, cosine, sine, heads, kvs, span):
    tokens = cosine.shape[1]
    qw, kw = heads * HEAD_DIM, kvs * HEAD_DIM
    return pl.pallas_call(
        functools.partial(attend_kernel, heads, kvs, span, len(pieces)),
        out_shape=(
            like((qw, tokens)), like((2 * kw, tokens)), like((qw, tokens)), like((qw, tokens), FULL),
            like((heads, tokens), FULL), like((1, tokens), FULL),
        ),
        in_specs=[SMEM, SMEM] + [ANY] * len(pieces) + [VMEM] * 3,
        out_specs=(VMEM,) * 6,
        scratch_shapes=[
            pltpu.VMEM((kvs, tokens, HEAD_DIM), LOW),
            pltpu.VMEM((qw + 2 * kw, tokens), FULL),
            pltpu.VMEM((tokens, weight.shape[0]), LOW),
            arrivals(len(pieces)),
        ],
        compiler_params=PARAMS,
        name="attend",
    )(order, rank, *pieces, weight, cosine, sine)


def attend_back_kernel(heads, kvs, span, pieces, order_ref, rank_ref, *refs):
    branch_refs, refs = refs[:pieces], refs[pieces:]
    output_ref, qrot_ref, kv_ref, mix_ref, lse_ref, cos_ref, sin_ref, inv_ref, out_ref, turned_ref, *scratch = refs
    keys_ref, values_ref, delta_ref, dkv_ref, grad_ref, branch_ref, sems = scratch
    count = cos_ref.shape[1] // span
    qw, kw = heads * HEAD_DIM, kvs * HEAD_DIM
    fetch(branch_refs, branch_ref, sems)
    seq_size, across = output_ref.shape[1], branch_ref.shape[1] // output_ref.shape[1]
    for at in range(0, branch_ref.shape[0], span):
        total = 0.0
        for part in range(seq_size):
            weight = output_ref[:, part, :, :across].reshape(qw, across)
            total = total + dot(weight, branch_ref[at:at + span, part * across:(part + 1) * across], NT)
        grad_ref[:, at:at + span] = total.astype(LOW)
    qw, kw = heads * HEAD_DIM, kvs * HEAD_DIM
    for k in range(kvs):
        keys_ref[k] = (kv_ref[k * HEAD_DIM:(k + 1) * HEAD_DIM, :].astype(FULL) * SCALE).T.astype(LOW)
        values_ref[k] = kv_ref[kw + k * HEAD_DIM:kw + (k + 1) * HEAD_DIM, :].astype(FULL).T.astype(LOW)
    for h in range(heads):
        rows = slice(h * HEAD_DIM, (h + 1) * HEAD_DIM)
        delta_ref[h:h + 1, :] = jnp.sum(grad_ref[rows, :].astype(FULL) * mix_ref[rows, :], 0, keepdims=True)
    dkv_ref[...] = jnp.zeros_like(dkv_ref)

    def one_block(qb, _):
        cols = pl.ds(pl.multiple_of(qb * span, span), span)
        rank = rank_ref[qb]

        def step(at, state, diagonal):
            rows = pl.ds(pl.multiple_of(order_ref[at] * span, span), span)
            out = []
            dkeys = [None] * kvs
            dvalues = [None] * kvs
            for h in range(heads):
                k = h * kvs // heads
                mine = slice(h * HEAD_DIM, (h + 1) * HEAD_DIM)
                query = qrot_ref[mine, cols]
                grad = grad_ref[mine, cols]
                scores = dot(keys_ref[k, rows, :], query)
                weights = jnp.exp(scores - lse_ref[h:h + 1, cols])
                if diagonal:
                    key_at = lax.broadcasted_iota(jnp.int32, (span, span), 0)
                    query_at = lax.broadcasted_iota(jnp.int32, (span, span), 1)
                    weights = jnp.where(key_at <= query_at, weights, 0.0)
                grad_probs = dot(values_ref[k, rows, :], grad)
                grad_scores = (weights * (grad_probs - delta_ref[h:h + 1, cols])).astype(LOW)
                key_t = kv_ref[k * HEAD_DIM:(k + 1) * HEAD_DIM, rows]
                out.append(state[h] + dot(key_t, grad_scores))
                dk = dot(query, grad_scores, NT)
                dv = dot(grad, weights.astype(LOW), NT)
                dkeys[k] = dk if dkeys[k] is None else dkeys[k] + dk
                dvalues[k] = dv if dvalues[k] is None else dvalues[k] + dv
            for k in range(kvs):
                mine = slice(k * HEAD_DIM, (k + 1) * HEAD_DIM)
                dkv_ref[mine, rows] += dkeys[k]
                mine = slice(kw + k * HEAD_DIM, kw + (k + 1) * HEAD_DIM)
                dkv_ref[mine, rows] += dvalues[k]
            return out

        state = [jnp.zeros((HEAD_DIM, span), FULL) for _ in range(heads)]
        state = lax.fori_loop(0, rank, lambda at, st: step(at, st, False), state)
        state = step(rank, state, True)
        scale = inv_ref[:, cols] * SCALE
        cosine, sine = cos_ref[:, cols], sin_ref[:, cols]
        for h in range(heads):
            one, two = state[h][:HALF] * scale, state[h][HALF:] * scale
            out_ref[h * HEAD_DIM:h * HEAD_DIM + HALF, cols] = (one * cosine + two * sine).astype(LOW)
            out_ref[h * HEAD_DIM + HALF:(h + 1) * HEAD_DIM, cols] = (two * cosine - one * sine).astype(LOW)
        return 0

    lax.fori_loop(0, count, one_block, 0)
    cosine, sine = cos_ref[...], sin_ref[...]
    scale = inv_ref[...] * SCALE
    for k in range(kvs):
        top = k * HEAD_DIM
        one, two = dkv_ref[top:top + HALF, :] * scale, dkv_ref[top + HALF:top + HEAD_DIM, :] * scale
        out_ref[qw + top:qw + top + HALF, :] = (one * cosine + two * sine).astype(LOW)
        out_ref[qw + top + HALF:qw + top + HEAD_DIM, :] = (two * cosine - one * sine).astype(LOW)
    out_ref[qw + kw:, :] = (dkv_ref[kw:, :] * inv_ref[...]).astype(LOW)
    turned_ref[...] = out_ref[...].T


def attend_back(order, rank, pieces, output, qrot, kv, mix, lse, cosine, sine, inv, heads, kvs, span):
    tokens = cosine.shape[1]
    qw, kw = heads * HEAD_DIM, kvs * HEAD_DIM
    return pl.pallas_call(
        functools.partial(attend_back_kernel, heads, kvs, span, len(pieces)),
        out_shape=(like((qw + 2 * kw, tokens)), like((tokens, qw + 2 * kw))),
        in_specs=[SMEM, SMEM] + [ANY] * len(pieces) + [VMEM] * 8,
        out_specs=(VMEM, VMEM),
        scratch_shapes=[
            pltpu.VMEM((kvs, tokens, HEAD_DIM), LOW),
            pltpu.VMEM((kvs, tokens, HEAD_DIM), LOW),
            pltpu.VMEM((heads, tokens), FULL),
            pltpu.VMEM((2 * kw, tokens), FULL),
            pltpu.VMEM((qw, tokens), LOW),
            pltpu.VMEM((tokens, pieces[0].shape[1]), LOW),
            arrivals(len(pieces)),
        ],
        compiler_params=PARAMS,
        name="attend_back",
    )(order, rank, *pieces, output, qrot, kv, mix, lse, cosine, sine, inv)


def layer(seq_size, fsdp_size, tokens, positions, attn_gain, query_weight, key_weight, value_weight, output_weight,
          ffn_gain, gate_weight, up_weight, down_weight, cotangent):
    span, width = tokens.shape[1:]
    heads = HEADS // seq_size
    kvs = max(1, KV_HEADS // seq_size)
    shared = max(1, seq_size // KV_HEADS)
    qw, kw = heads * HEAD_DIM, kvs * HEAD_DIM
    own_rows = query_weight.shape[0]
    hidden_own = gate_weight.shape[1] // seq_size
    chunk = 128 if hidden_own % 128 == 0 else 64
    parts = 2 if seq_size == 4 else 1
    piece_rows = span // parts
    into, back = (seq_size, fsdp_size, own_rows), (fsdp_size, seq_size, own_rows)
    here = lax.axis_index("seq")

    def after(x, *others):
        return lax.optimization_barrier((x, *others))[0]

    def swap(x, j):
        return lax.ppermute(x, "seq", [(i, i ^ j) for i in range(seq_size)])

    def seq_gather(own):
        if parts == 1:
            return [own[0]] + [swap(own[0], j) for j in range(1, seq_size)]
        a, b = own
        ax, by = swap(a, 1), swap(b, 2)
        ay, bx = swap(a, 2), swap(b, 1)
        ad, bd = swap(ax, 2), swap(by, 1)
        return [a, b, ax, bx, ay, by, ad, bd]

    def seq_scatter(pieces):
        if parts == 1:
            return (), [pieces[0]] + [swap(pieces[j], j) for j in range(1, seq_size)]
        a, b = pieces[::2], pieces[1::2]
        da, db = swap(a[3], 2), swap(b[3], 1)
        ya, xb = swap(a[2], 2), swap(b[1], 1)
        xa = swap((a[1].astype(FULL) + da.astype(FULL)).astype(LOW), 1)
        yb = swap((b[2].astype(FULL) + db.astype(FULL)).astype(LOW), 2)
        return (da, db), [a[0], ya, xa, b[0], xb, yb]

    def direct_scatter(pieces):
        if parts == 1:
            return seq_scatter(pieces)[1]
        a, b = pieces[::2], pieces[1::2]
        return [a[0]] + [swap(a[j], j) for j in (1, 2, 3)] + [b[0]] + [swap(b[j], j) for j in (1, 2, 3)]

    def spread(pieces_for):
        got = [pieces_for(here)] + [swap(pieces_for(here ^ j), j) for j in range(1, seq_size)]
        stack = jnp.stack(got)
        return jnp.concatenate(
            [lax.dynamic_index_in_dim(stack, here ^ t, 0, False) for t in range(seq_size)], 0
        )

    def collect(x):
        blocks = x.reshape(seq_size, own_rows, x.shape[1])
        got = jnp.stack([lax.dynamic_index_in_dim(blocks, here, 0, False)] + [
            swap(lax.dynamic_index_in_dim(blocks, here ^ j, 0, False), j) for j in range(1, seq_size)
        ])
        return jnp.stack([lax.dynamic_index_in_dim(got, here ^ t, 0, False) for t in range(seq_size)])

    def fsdp_gather(x):
        return lax.all_gather(x, "fsdp", axis=0, tiled=True)

    def fsdp_scatter(x):
        return lax.psum_scatter(x, "fsdp", scatter_dimension=0, tiled=True)

    gain_one, gain_two = attn_gain.astype(FULL)[:, None], ffn_gain.astype(FULL)[:, None]

    def with_gain(weight, gain):
        return (weight.astype(FULL) * gain).astype(LOW)

    query_low, key_low, value_low = (with_gain(w, gain_one) for w in (query_weight, key_weight, value_weight))

    def qkv_for(t):
        first = (t * heads // GROUP) * HEAD_DIM
        return jnp.concatenate([
            lax.dynamic_slice_in_dim(query_low, t * qw, qw, 1),
            lax.dynamic_slice_in_dim(key_low, first, kw, 1),
            lax.dynamic_slice_in_dim(value_low, first, kw, 1),
        ], 1)

    own_tokens = tokens[0]
    own_pieces = call_own(
        functools.partial(regroup_kernel, into), (like((piece_rows, width)),) * parts, own_tokens
    )
    token_pieces = seq_gather(own_pieces)
    output_own = output_weight.reshape(own_rows, seq_size, -1).swapaxes(0, 1).reshape(seq_size * own_rows, -1)
    projections = fsdp_gather(jnp.concatenate([output_own, spread(qkv_for)], 1))
    gate_weight, up_weight = lax.optimization_barrier((gate_weight, up_weight, *own_pieces))[:2]
    gate_low, up_low = with_gain(gate_weight, gain_two), with_gain(up_weight, gain_two)

    def gate_up_for(t):
        gate = lax.dynamic_slice_in_dim(gate_low, t * hidden_own, hidden_own, 1)
        up = lax.dynamic_slice_in_dim(up_low, t * hidden_own, hidden_own, 1)
        return jnp.concatenate(
            [x[:, c:c + chunk] for c in range(0, hidden_own, chunk) for x in (gate, up)], 1
        )

    gate_up_own = spread(gate_up_for)
    gate_up_full = fsdp_gather(gate_up_own)
    down_full = fsdp_gather(down_weight)
    own_upstream = after(cotangent[0], gate_up_own, *token_pieces)
    upstream = [own_upstream] + [swap(own_upstream, j) for j in range(1, seq_size)]

    count = positions.shape[1] // span
    where_at = positions[0].reshape(count, span)
    where_at = jnp.stack([lax.dynamic_index_in_dim(where_at, here ^ j, 0, False) for j in range(count)])
    rank = where_at[:, 0] // span
    order = jnp.argsort(rank).astype(jnp.int32)
    cosine, sine = rope_tables(where_at.reshape(-1))

    qrot, kv, attended, mix, lse, inv_one = attend(
        order, rank, token_pieces, projections, cosine, sine, heads, kvs, span
    )
    attended, *upstream = lax.optimization_barrier((attended, *upstream))
    branch = seq_scatter(rows_of_product(attended, projections, piece_rows, into))[1]
    middle, inv_two, *own_pieces = call_own(
        functools.partial(middle_kernel, into, parts),
        (like((span, width), FULL), like((span, 1), FULL)) + (like((piece_rows, width)),) * parts,
        own_tokens, *branch,
    )

    normed_pieces = seq_gather(own_pieces)
    slope, hidden = hidden_of(normed_pieces, gate_up_full, chunk)
    part_down = grad_down_of(hidden, upstream)
    grad_down = fsdp_scatter(part_down)
    grad_gate_up, down_full = grad_gate_up_of(
        [after(upstream[0], part_down), *upstream[1:]], jnp.zeros((1,), jnp.int32), [down_full], slope, chunk
    )
    first, grad_pieces = seq_scatter(grad_rows_of(grad_gate_up, gate_up_full, piece_rows))
    part_gate_up = grad_weight_of([after(normed_pieces[0], *first), *normed_pieces[1:]], grad_gate_up)
    grad_gate_up_own = fsdp_scatter(after(part_gate_up, part_down))
    out_pieces = rows_of_product(after(hidden, part_gate_up), down_full, piece_rows)
    grad_pieces[0] = after(grad_pieces[0], out_pieces[0], grad_down)
    grad_middle, *own_pieces = call_own(
        functools.partial(grad_middle_kernel, back, parts),
        (like((span, width), FULL),) + (like((piece_rows, width)),) * parts,
        cotangent[0], middle, inv_two, *grad_pieces,
    )

    branch_pieces = seq_gather(own_pieces)
    out_pieces = direct_scatter(lax.optimization_barrier((*out_pieces, *branch_pieces))[:len(out_pieces)])
    grad_qkv, grad_qkv_turned = attend_back(
        order, rank, branch_pieces, projections.reshape(fsdp_size, seq_size, own_rows, -1), qrot, kv, mix, lse,
        cosine, sine, inv_one, heads, kvs, span,
    )
    grad_qkv, *out_pieces = lax.optimization_barrier((grad_qkv, *out_pieces))
    part_projections = attention_weights_of(token_pieces, branch_pieces, grad_qkv, attended, into)
    grad_pieces = grad_rows_of(after(grad_qkv_turned, part_projections), projections, piece_rows)
    grad_pieces = seq_scatter(grad_pieces)[1]
    grad_projections = fsdp_scatter(after(part_projections, grad_gate_up_own))
    grad_qkv_own = grad_projections[:, -qw - 2 * kw:]
    grad_output = grad_projections[:, :-qw - 2 * kw].reshape(seq_size, own_rows, -1).swapaxes(0, 1)
    grad_output = grad_output.reshape(own_rows, width)
    block_out = call_own(
        functools.partial(block_out_kernel, parts), like((span, width)), middle, *out_pieces
    )
    grad_tokens = call_own(
        functools.partial(grad_tokens_kernel, back, parts), like((span, width), FULL),
        own_tokens, grad_middle, *grad_pieces,
    )

    def whole_rows(x):
        return x.swapaxes(0, 1).reshape(own_rows, -1)

    got = collect(grad_gate_up_own).astype(FULL).reshape(seq_size, own_rows, -1, 2, chunk)
    grad_gate, grad_up = whole_rows(got[:, :, :, 0]), whole_rows(got[:, :, :, 1])
    got = collect(grad_qkv_own).astype(FULL)
    grad_query = whole_rows(got[:, :, :qw])

    def of_heads(x):
        return whole_rows(x.reshape(seq_size // shared, shared, own_rows, kw).sum(1))

    grad_key, grad_value = of_heads(got[:, :, qw:qw + kw]), of_heads(got[:, :, qw + kw:])
    grad_attn_gain = (
        jnp.sum(grad_query * query_weight.astype(FULL), 1)
        + jnp.sum(grad_key * key_weight.astype(FULL), 1)
        + jnp.sum(grad_value * value_weight.astype(FULL), 1)
    )
    grad_ffn_gain = jnp.sum(grad_gate * gate_weight.astype(FULL), 1) + jnp.sum(grad_up * up_weight.astype(FULL), 1)
    return (
        block_out[None],
        grad_tokens[None],
        grad_attn_gain,
        grad_query * gain_one,
        grad_key * gain_one,
        grad_value * gain_one,
        grad_output.astype(FULL),
        grad_ffn_gain,
        grad_gate * gain_two,
        grad_up * gain_two,
        grad_down.astype(FULL),
    )


def solution(mesh):
    rows, vector, matrix = P("fsdp", "seq", None), P(("seq", "fsdp")), P(("seq", "fsdp"), None)
    return jax.shard_map(
        functools.partial(layer, mesh.shape["seq"], mesh.shape["fsdp"]),
        mesh=mesh,
        in_specs=(
            rows, P("fsdp", None), vector, matrix, matrix, matrix, matrix, vector, matrix, matrix, matrix, rows,
        ),
        out_specs=(rows, rows, vector, matrix, matrix, matrix, matrix, vector, matrix, matrix, matrix),
        check_vma=False,
    )
```

```python
import functools
import math

import jax
import jax.numpy as jnp
from jax import lax
from jax.experimental import pallas as pl
from jax.experimental.pallas import tpu as pltpu
from jax.sharding import Mesh
from jax.sharding import PartitionSpec as P

HEADS = 32
KV_HEADS = 4
HEAD_DIM = 64
HALF = HEAD_DIM // 2
GROUP = HEADS // KV_HEADS
EPSILON = 1e-05
SCALE = 1.0 / math.sqrt(HEAD_DIM)
FSDP = ("chip", "core")
LOW = jnp.bfloat16
FULL = jnp.float32
VMEM = pl.BlockSpec(memory_space=pltpu.VMEM)
ANY = pl.BlockSpec(memory_space=pltpu.HBM)
SMEM = pl.BlockSpec(memory_space=pltpu.SMEM)
PARAMS = pltpu.CompilerParams(vmem_limit_bytes=60 << 20)
NN, NT, TN = ((1,), (0,)), ((1,), (1,)), ((0,), (0,))


def dot(a, b, dims=NN):
    return lax.dot_general(a, b, (dims, ((), ())), preferred_element_type=FULL)


def like(shape, dtype=LOW):
    return jax.ShapeDtypeStruct(shape, dtype)


def rope_tables(where_at):
    frequency = 1.0 / 10000.0 ** (jnp.arange(HALF, dtype=FULL) * 2.0 / HEAD_DIM)
    angles = frequency[:, None] * where_at.astype(FULL)[None, :]
    return jnp.cos(angles), jnp.sin(angles)


def regroup(x, outer, inner, rows):
    return jnp.concatenate(
        [x[:, (o * inner + i) * rows:(o * inner + i + 1) * rows] for i in range(inner) for o in range(outer)], 1
    )


def join(pieces, whole_ref):
    at = 0
    for piece in pieces:
        whole_ref[at:at + piece.shape[0], :] = piece[...]
        at += piece.shape[0]


def fetch(pieces, whole_ref, sems):
    copies, at = [], 0
    for i, piece in enumerate(pieces):
        rows = piece.shape[0]
        copies.append(pltpu.make_async_copy(piece, whole_ref.at[pl.ds(at, rows)], sems.at[i]))
        at += rows
    for copy in copies:
        copy.start()
    for copy in copies:
        copy.wait()


def arrivals(count):
    return pltpu.SemaphoreType.DMA((count,))


def call_own(kernel, out_shape, *args, scalars=()):
    return pl.pallas_call(
        kernel, out_shape=out_shape, in_specs=[SMEM] * len(scalars) + [VMEM] * len(args),
        out_specs=jax.tree.map(lambda _: VMEM, out_shape), compiler_params=PARAMS,
        name=getattr(kernel, "func", kernel).__name__,
    )(*scalars, *args)


def added(refs):
    total = refs[0][...].astype(FULL)
    for ref in refs[1:]:
        total = total + ref[...].astype(FULL)
    return total


def regroup_kernel(grid, x_ref, *out_refs):
    x = regroup(x_ref[...].astype(FULL), *grid).astype(LOW)
    rows = out_refs[0].shape[0]
    for i, ref in enumerate(out_refs):
        ref[...] = x[i * rows:(i + 1) * rows]


def middle_kernel(grid, parts, *refs):
    tokens_ref, refs = refs[0], refs[1:]
    per = (len(refs) - 2 - parts) // parts
    middle_ref, inv_ref, *normed_refs = refs[per * parts:]
    rows = normed_refs[0].shape[0]
    for i in range(parts):
        at = slice(i * rows, (i + 1) * rows)
        middle = tokens_ref[at, :].astype(FULL) + added(refs[i * per:(i + 1) * per])
        inv = lax.rsqrt(jnp.mean(middle * middle, -1, keepdims=True) + EPSILON)
        middle_ref[at, :] = middle
        inv_ref[at, :] = inv
        normed_refs[i][...] = regroup(middle * inv, *grid).astype(LOW)


def grad_middle_kernel(grid, parts, *refs):
    upstream_ref, middle_ref, inv_ref, refs = refs[0], refs[1], refs[2], refs[3:]
    out_ref, *low_refs = refs[-1 - parts:]
    per = (len(refs) - 1 - parts) // parts
    rows = low_refs[0].shape[0]
    for i in range(parts):
        at = slice(i * rows, (i + 1) * rows)
        inv = inv_ref[at, :]
        normed = middle_ref[at, :] * inv
        grad = regroup(added(refs[i * per:(i + 1) * per]), *grid)
        grad = upstream_ref[at, :].astype(FULL) + inv * (grad - normed * jnp.mean(grad * normed, -1, keepdims=True))
        out_ref[at, :] = grad
        low_refs[i][...] = grad.astype(LOW)


def grad_tokens_kernel(grid, parts, *refs):
    tokens_ref, grad_ref, refs, out_ref = refs[0], refs[1], refs[2:-1], refs[-1]
    per = len(refs) // parts
    rows = out_ref.shape[0] // parts
    for i in range(parts):
        at = slice(i * rows, (i + 1) * rows)
        tokens = tokens_ref[at, :].astype(FULL)
        normed = tokens * lax.rsqrt(jnp.mean(tokens * tokens, -1, keepdims=True) + EPSILON)
        grad = regroup(added(refs[i * per:(i + 1) * per]), *grid)
        out_ref[at, :] = grad_ref[at, :] + grad - normed * jnp.mean(grad * normed, -1, keepdims=True)


def block_out_kernel(middle_ref, *refs):
    refs[-1][...] = (middle_ref[...] + added(refs[:-1])).astype(LOW)


def as_row(column):
    return jnp.broadcast_to(column, (column.shape[0], 128)).T[:1]


def finish_gate_up_kernel(here_ref, *refs):
    *pieces, gate_ref, up_ref, gain_ref, grad_gate_ref, grad_up_ref, grad_gain_ref = refs
    gain, total = gain_ref[...], 0.0
    across, chunk = gate_ref.shape[1] // len(pieces), 128
    for j, piece in enumerate(pieces):
        first = (here_ref[0] ^ j) * across
        for c in range(across // chunk):
            there = pl.ds(pl.multiple_of(first + c * chunk, chunk), chunk)
            for i, (weight_ref, out_ref) in enumerate(((gate_ref, grad_gate_ref), (up_ref, grad_up_ref))):
                grad = piece[:, (2 * c + i) * chunk:(2 * c + i + 1) * chunk].astype(FULL)
                out_ref[:, there] = grad * gain
                total = total + grad * weight_ref[:, there].astype(FULL)
    grad_gain_ref[...] = as_row(jnp.sum(total, 1, keepdims=True))


def finish_projections_kernel(here_ref, *refs):
    *pieces, own_ref, query_ref, key_ref, value_ref, gain_ref = refs[:-5]
    grad_query_ref, grad_key_ref, grad_value_ref, grad_output_ref, grad_gain_ref = refs[-5:]
    gain, count = gain_ref[...], len(pieces)
    rows = gain.shape[0]
    qw, kw = query_ref.shape[1] // count, key_ref.shape[1] // count
    total = 0.0
    for j, piece in enumerate(pieces):
        there = pl.ds(pl.multiple_of((here_ref[0] ^ j) * qw, qw), qw)
        grad = piece[:, :qw].astype(FULL)
        grad_query_ref[:, there] = grad * gain
        total = total + jnp.sum(grad * query_ref[:, there].astype(FULL), 1, keepdims=True)
    for first, weight_ref, out_ref in ((qw, key_ref, grad_key_ref), (qw + kw, value_ref, grad_value_ref)):
        grad = [jnp.zeros((rows, kw), FULL)] * count
        for j, piece in enumerate(pieces):
            mine = piece[:, first:first + kw].astype(FULL)
            for t in range(count):
                grad[t] = jnp.where(here_ref[0] == t ^ j, mine, grad[t])
        grad = jnp.concatenate(grad, 1)
        out_ref[...] = grad * gain
        total = total + jnp.sum(grad * weight_ref[...].astype(FULL), 1, keepdims=True)
    across = grad_output_ref.shape[1] // count
    for part in range(count):
        grad_output_ref[:, part * across:(part + 1) * across] = own_ref[part * rows:(part + 1) * rows, :across].astype(FULL)
    grad_gain_ref[...] = as_row(total)


def rows_of(pieces):
    return sum(p.shape[0] for p in pieces)


def whole(shape):
    return pl.BlockSpec(shape, lambda i: (0,) * len(shape))


def columns(rows, width):
    return pl.BlockSpec((rows, width), lambda i: (0, i))


def by_rows(height, width):
    return pl.BlockSpec((height, width), lambda i: (i, 0))


def hidden_kernel(count, chunk, *refs):
    pieces, (weight_ref, slope_ref, hidden_ref, normed_ref, sems) = refs[:count], refs[count:]

    @pl.when(pl.program_id(0) == 0)
    def _():
        fetch(pieces, normed_ref, sems)

    both = dot(normed_ref[...], weight_ref[...])
    gate, up = both[:, :chunk], both[:, chunk:]
    sigmoid = jax.nn.sigmoid(gate)
    silu = gate * sigmoid
    slope = up * sigmoid * (1.0 + gate * (1.0 - sigmoid))
    slope_ref[...] = jnp.concatenate([slope, silu], 1).astype(LOW)
    hidden_ref[...] = (silu * up).T.astype(LOW)


def hidden_of(pieces, weight, chunk):
    tokens, (width, both) = rows_of(pieces), weight.shape
    return pl.pallas_call(
        functools.partial(hidden_kernel, len(pieces), chunk),
        grid=(both // (2 * chunk),),
        in_specs=[ANY] * len(pieces) + [columns(width, 2 * chunk)],
        out_specs=(columns(tokens, 2 * chunk), by_rows(chunk, tokens), whole((tokens, width))),
        out_shape=(like((tokens, both)), like((both // 2, tokens)), like((tokens, width))),
        scratch_shapes=[arrivals(len(pieces))],
        compiler_params=PARAMS,
        name="hidden_of",
    )(*pieces, weight)


def grad_down_kernel(count, *refs):
    pieces, (hidden_ref, out_ref, block_ref) = refs[:count], refs[count:]
    join(pieces, block_ref)
    out_ref[...] = dot(hidden_ref[...], block_ref[...]).astype(LOW)


def grad_down_of(hidden, pieces, block=256):
    tokens, width = rows_of(pieces), pieces[0].shape[1]
    return pl.pallas_call(
        functools.partial(grad_down_kernel, len(pieces)),
        grid=(width // block,),
        in_specs=[columns(p.shape[0], block) for p in pieces] + [whole(hidden.shape)],
        out_specs=columns(hidden.shape[0], block),
        out_shape=like((hidden.shape[0], width)),
        scratch_shapes=[pltpu.VMEM((tokens, block), LOW)],
        compiler_params=PARAMS,
        name="grad_down_of",
    )(*pieces, hidden)


def grad_gate_up_kernel(count, chunk, odd, *refs):
    pieces, (down_ref, slope_ref, out_ref, upstream_ref, sems) = refs[:count], refs[count:]
    step, steps = pl.program_id(0), pl.num_programs(0)

    @pl.when(step == 0)
    def _():
        fetch(pieces, upstream_ref, sems)

    def work(chunks):
        grad = dot(upstream_ref[...], down_ref[:chunks * chunk, :], NT)
        each = [grad[:, c * chunk:(c + 1) * chunk] for c in range(chunks) for _ in range(2)]
        width = chunks * 2 * chunk
        out_ref[:, :width] = (jnp.concatenate(each, 1) * slope_ref[:, :width].astype(FULL)).astype(LOW)

    @pl.when(step < steps - odd)
    def _():
        work(2)

    if odd:

        @pl.when(step == steps - 1)
        def _():
            work(1)


def grad_gate_up_of(pieces, down, slope, chunk):
    (tokens, width), depth = (rows_of(pieces), pieces[0].shape[1]), down.shape[0]
    return pl.pallas_call(
        functools.partial(grad_gate_up_kernel, len(pieces), chunk, depth // chunk % 2),
        grid=(pl.cdiv(depth, 2 * chunk),),
        in_specs=[ANY] * len(pieces) + [by_rows(2 * chunk, width), columns(tokens, 4 * chunk)],
        out_specs=columns(tokens, 4 * chunk),
        out_shape=like(slope.shape),
        scratch_shapes=[pltpu.VMEM((tokens, width), LOW), arrivals(len(pieces))],
        compiler_params=PARAMS,
        name="grad_gate_up_of",
    )(*pieces, down, slope)


def grad_rows_kernel(first, grad_ref, weight_ref, *out_refs):
    grad = dot(grad_ref[...], weight_ref[:, first:], NT).astype(LOW)
    rows = out_refs[0].shape[0]
    for i, ref in enumerate(out_refs):
        ref[...] = grad[i * rows:(i + 1) * rows]


def grad_rows_of(grad, weight, piece_rows, block=512):
    tokens, width = grad.shape[0], weight.shape[0]
    count = tokens // piece_rows
    return pl.pallas_call(
        functools.partial(grad_rows_kernel, weight.shape[1] - grad.shape[1]),
        grid=(width // block,),
        in_specs=[whole(grad.shape), by_rows(block, weight.shape[1])],
        out_specs=(columns(piece_rows, block),) * count,
        out_shape=(like((piece_rows, width)),) * count,
        compiler_params=PARAMS,
        name="grad_rows_of",
    )(grad, weight)


def grad_weight_kernel(core_ref, left_ref, other_left_ref, grad_ref, other_grad_ref, out_ref):
    got = dot(left_ref[...], grad_ref[...], TN) + dot(other_left_ref[...], other_grad_ref[...], TN)
    out_ref[...] = got.astype(LOW)


def grad_weight_of(left, other_left, grad, other_grad, core, chips):
    tokens, width = left.shape
    block = width // chips // 2
    mine = pl.BlockSpec((tokens, block), lambda i, core_ref: (0, i * 2 + core_ref[0]))
    every = pl.BlockSpec(grad.shape, lambda i, core_ref: (0, 0))
    return pl.pallas_call(
        grad_weight_kernel,
        grid_spec=pltpu.PrefetchScalarGridSpec(
            num_scalar_prefetch=1,
            grid=(chips,),
            in_specs=[mine, mine, every, every],
            out_specs=pl.BlockSpec((block, grad.shape[1]), lambda i, core_ref: (i, 0)),
        ),
        out_shape=like((width // 2, grad.shape[1])),
        compiler_params=PARAMS,
        name="grad_weight_of",
    )(core, left, other_left, grad, other_grad)


def rows_kernel(left_ref, weight_ref, *refs):
    *out_refs, turned_ref = refs

    @pl.when(pl.program_id(0) == 0)
    def _():
        turned_ref[...] = left_ref[...].T

    weight = weight_ref[...].reshape(turned_ref.shape[1], weight_ref.shape[-1])
    out = dot(turned_ref[...], weight).astype(LOW)
    rows = out_refs[0].shape[0]
    for i, ref in enumerate(out_refs):
        ref[...] = out[i * rows:(i + 1) * rows]


def rows_of_product(left, weight, piece_rows, inner=None, block=512):
    depth, tokens = left.shape
    count = tokens // piece_rows
    if inner is None:
        width, spec = weight.shape[1], columns(depth, block)
    else:
        seq_size, fsdp_size, own_rows = inner
        width = weight.shape[0]
        block = min(block, width // seq_size)
        per = width // seq_size // block
        weight = weight.reshape(fsdp_size, seq_size, own_rows, -1)
        spec = pl.BlockSpec((fsdp_size, 1, own_rows, block), lambda i: (0, i // per, 0, i % per))
    return pl.pallas_call(
        rows_kernel,
        grid=(width // block,),
        in_specs=[whole(left.shape), spec],
        out_specs=(columns(piece_rows, block),) * count,
        out_shape=(like((piece_rows, width)),) * count,
        scratch_shapes=[pltpu.VMEM((tokens, depth), LOW)],
        compiler_params=PARAMS,
        name="rows_of_product",
    )(left, weight)


def attention_weights_kernel(count, inner, *refs):
    tokens, grads = refs[:count], refs[count:2 * count]
    grad_qkv_ref, attended_ref, out_ref, block_ref = refs[2 * count:]
    seq_size, fsdp_size, own_rows = inner
    step, block = pl.program_id(0), block_ref.shape[1]
    across = out_ref.shape[1] - grad_qkv_ref.shape[0]
    join(tokens, block_ref)
    there = pl.ds(pl.multiple_of(step * block, block), block)
    out_ref[there, across:] = dot(grad_qkv_ref[...], block_ref[...]).T.astype(LOW)
    join(grads, block_ref)
    got = dot(attended_ref[...], block_ref[...]).astype(LOW)
    part = step * block // across
    first = step * block % across
    for f in range(fsdp_size):
        rows = pl.ds(pl.multiple_of((f * seq_size + part) * own_rows, own_rows), own_rows)
        out_ref[rows, pl.ds(pl.multiple_of(first, 128), block)] = got[f * own_rows:(f + 1) * own_rows]


def attention_weights_of(tokens, grads, grad_qkv, attended, inner, block=512):
    count, width = len(tokens), tokens[0].shape[1]
    block = min(block, width // inner[0])
    shape = (width, grad_qkv.shape[0] + width // inner[0])
    return pl.pallas_call(
        functools.partial(attention_weights_kernel, count, inner),
        grid=(width // block,),
        in_specs=[columns(p.shape[0], block) for p in (*tokens, *grads)]
        + [whole(grad_qkv.shape), whole(attended.shape)],
        out_specs=whole(shape),
        out_shape=like(shape),
        scratch_shapes=[pltpu.VMEM((rows_of(tokens), block), LOW)],
        compiler_params=PARAMS,
        name="attention_weights_of",
    )(*tokens, *grads, grad_qkv, attended)


def attend_kernel(heads, kvs, span, pieces, order_ref, rank_ref, *refs):
    token_refs, refs = refs[:pieces], refs[pieces:]
    weight_ref, cos_ref, sin_ref, qrot_ref, kv_ref, att_ref, mix_ref, lse_ref, inv_ref, *scratch = refs
    keys_ref, qkv_ref, tokens_ref, sems = scratch
    fetch(token_refs, tokens_ref, sems)
    count = cos_ref.shape[1] // span
    for at in range(0, tokens_ref.shape[0], span):
        there = slice(at, at + span)
        values = tokens_ref[there, :].astype(FULL)
        inv = lax.rsqrt(jnp.mean(values * values, -1, keepdims=True) + EPSILON)
        qkv_ref[:, there] = (dot(tokens_ref[there, :], weight_ref[:, -qkv_ref.shape[0]:]) * inv).T
        inv_ref[:, there] = jnp.broadcast_to(inv, (span, 128)).T[:1]
    qw, kw = heads * HEAD_DIM, kvs * HEAD_DIM
    cosine, sine = cos_ref[...], sin_ref[...]

    def rotated(row):
        one, two = qkv_ref[row:row + HALF, :], qkv_ref[row + HALF:row + HEAD_DIM, :]
        return jnp.concatenate([one * cosine - two * sine, two * cosine + one * sine], 0)

    for h in range(heads):
        qrot_ref[h * HEAD_DIM:(h + 1) * HEAD_DIM, :] = rotated(h * HEAD_DIM).astype(LOW)
    for k in range(kvs):
        turned = rotated(qw + k * HEAD_DIM).astype(LOW)
        kv_ref[k * HEAD_DIM:(k + 1) * HEAD_DIM, :] = turned
        keys_ref[k] = (turned.astype(FULL) * SCALE).T.astype(LOW)
    kv_ref[kw:, :] = qkv_ref[qw + kw:, :].astype(LOW)

    def one_block(qb, _):
        cols = pl.ds(pl.multiple_of(qb * span, span), span)
        rank = rank_ref[qb]

        def step(at, state, diagonal):
            rows = pl.ds(pl.multiple_of(order_ref[at] * span, span), span)
            out = []
            for h in range(heads):
                top, total, mixed = state[h]
                k = h * kvs // heads
                scores = dot(keys_ref[k, rows, :], qrot_ref[h * HEAD_DIM:(h + 1) * HEAD_DIM, cols])
                if diagonal:
                    key_at = lax.broadcasted_iota(jnp.int32, (span, span), 0)
                    query_at = lax.broadcasted_iota(jnp.int32, (span, span), 1)
                    scores = jnp.where(key_at <= query_at, scores, -1e30)
                new_top = jnp.maximum(top, jnp.max(scores, 0, keepdims=True))
                weights = jnp.exp(scores - new_top)
                fade = jnp.exp(top - new_top)
                total = total * fade + jnp.sum(weights, 0, keepdims=True)
                values = kv_ref[kw + k * HEAD_DIM:kw + (k + 1) * HEAD_DIM, rows]
                mixed = mixed * fade + dot(values, weights.astype(LOW))
                out.append((new_top, total, mixed))
            return out

        start = [(jnp.full((1, span), -1e30, FULL), jnp.zeros((1, span), FULL),
                  jnp.zeros((HEAD_DIM, span), FULL)) for _ in range(heads)]
        state = lax.fori_loop(0, rank, lambda at, st: step(at, st, False), start)
        state = step(rank, state, True)
        for h in range(heads):
            top, total, mixed = state[h]
            mixed = mixed / total
            mix_ref[h * HEAD_DIM:(h + 1) * HEAD_DIM, cols] = mixed
            att_ref[h * HEAD_DIM:(h + 1) * HEAD_DIM, cols] = mixed.astype(LOW)
            lse_ref[h:h + 1, cols] = top + jnp.log(total)
        return 0

    lax.fori_loop(0, count, one_block, 0)


def attend(order, rank, pieces, weight, cosine, sine, heads, kvs, span):
    tokens = cosine.shape[1]
    qw, kw = heads * HEAD_DIM, kvs * HEAD_DIM
    return pl.pallas_call(
        functools.partial(attend_kernel, heads, kvs, span, len(pieces)),
        out_shape=(
            like((qw, tokens)), like((2 * kw, tokens)), like((qw, tokens)), like((qw, tokens), FULL),
            like((heads, tokens), FULL), like((1, tokens), FULL),
        ),
        in_specs=[SMEM, SMEM] + [ANY] * len(pieces) + [VMEM] * 3,
        out_specs=(VMEM,) * 6,
        scratch_shapes=[
            pltpu.VMEM((kvs, tokens, HEAD_DIM), LOW),
            pltpu.VMEM((qw + 2 * kw, tokens), FULL),
            pltpu.VMEM((tokens, weight.shape[0]), LOW),
            arrivals(len(pieces)),
        ],
        compiler_params=PARAMS,
        name="attend",
    )(order, rank, *pieces, weight, cosine, sine)


def attend_back_kernel(heads, kvs, span, pieces, order_ref, rank_ref, *refs):
    branch_refs, refs = refs[:pieces], refs[pieces:]
    output_ref, qrot_ref, kv_ref, mix_ref, lse_ref, cos_ref, sin_ref, inv_ref, out_ref, turned_ref, *scratch = refs
    keys_ref, values_ref, delta_ref, dkv_ref, grad_ref, branch_ref, sems = scratch
    count = cos_ref.shape[1] // span
    qw, kw = heads * HEAD_DIM, kvs * HEAD_DIM
    fetch(branch_refs, branch_ref, sems)
    seq_size, across = output_ref.shape[1], branch_ref.shape[1] // output_ref.shape[1]
    for at in range(0, branch_ref.shape[0], span):
        total = 0.0
        for part in range(seq_size):
            weight = output_ref[:, part, :, :across].reshape(qw, across)
            total = total + dot(weight, branch_ref[at:at + span, part * across:(part + 1) * across], NT)
        grad_ref[:, at:at + span] = total.astype(LOW)
    qw, kw = heads * HEAD_DIM, kvs * HEAD_DIM
    for k in range(kvs):
        keys_ref[k] = (kv_ref[k * HEAD_DIM:(k + 1) * HEAD_DIM, :].astype(FULL) * SCALE).T.astype(LOW)
        values_ref[k] = kv_ref[kw + k * HEAD_DIM:kw + (k + 1) * HEAD_DIM, :].astype(FULL).T.astype(LOW)
    for h in range(heads):
        rows = slice(h * HEAD_DIM, (h + 1) * HEAD_DIM)
        delta_ref[h:h + 1, :] = jnp.sum(grad_ref[rows, :].astype(FULL) * mix_ref[rows, :], 0, keepdims=True)
    dkv_ref[...] = jnp.zeros_like(dkv_ref)

    def one_block(qb, _):
        cols = pl.ds(pl.multiple_of(qb * span, span), span)
        rank = rank_ref[qb]

        def step(at, state, diagonal):
            rows = pl.ds(pl.multiple_of(order_ref[at] * span, span), span)
            out = []
            dkeys = [None] * kvs
            dvalues = [None] * kvs
            for h in range(heads):
                k = h * kvs // heads
                mine = slice(h * HEAD_DIM, (h + 1) * HEAD_DIM)
                query = qrot_ref[mine, cols]
                grad = grad_ref[mine, cols]
                scores = dot(keys_ref[k, rows, :], query)
                weights = jnp.exp(scores - lse_ref[h:h + 1, cols])
                if diagonal:
                    key_at = lax.broadcasted_iota(jnp.int32, (span, span), 0)
                    query_at = lax.broadcasted_iota(jnp.int32, (span, span), 1)
                    weights = jnp.where(key_at <= query_at, weights, 0.0)
                grad_probs = dot(values_ref[k, rows, :], grad)
                grad_scores = (weights * (grad_probs - delta_ref[h:h + 1, cols])).astype(LOW)
                key_t = kv_ref[k * HEAD_DIM:(k + 1) * HEAD_DIM, rows]
                out.append(state[h] + dot(key_t, grad_scores))
                dk = dot(query, grad_scores, NT)
                dv = dot(grad, weights.astype(LOW), NT)
                dkeys[k] = dk if dkeys[k] is None else dkeys[k] + dk
                dvalues[k] = dv if dvalues[k] is None else dvalues[k] + dv
            for k in range(kvs):
                mine = slice(k * HEAD_DIM, (k + 1) * HEAD_DIM)
                dkv_ref[mine, rows] += dkeys[k]
                mine = slice(kw + k * HEAD_DIM, kw + (k + 1) * HEAD_DIM)
                dkv_ref[mine, rows] += dvalues[k]
            return out

        state = [jnp.zeros((HEAD_DIM, span), FULL) for _ in range(heads)]
        state = lax.fori_loop(0, rank, lambda at, st: step(at, st, False), state)
        state = step(rank, state, True)
        scale = inv_ref[:, cols] * SCALE
        cosine, sine = cos_ref[:, cols], sin_ref[:, cols]
        for h in range(heads):
            one, two = state[h][:HALF] * scale, state[h][HALF:] * scale
            out_ref[h * HEAD_DIM:h * HEAD_DIM + HALF, cols] = (one * cosine + two * sine).astype(LOW)
            out_ref[h * HEAD_DIM + HALF:(h + 1) * HEAD_DIM, cols] = (two * cosine - one * sine).astype(LOW)
        return 0

    lax.fori_loop(0, count, one_block, 0)
    cosine, sine = cos_ref[...], sin_ref[...]
    scale = inv_ref[...] * SCALE
    for k in range(kvs):
        top = k * HEAD_DIM
        one, two = dkv_ref[top:top + HALF, :] * scale, dkv_ref[top + HALF:top + HEAD_DIM, :] * scale
        out_ref[qw + top:qw + top + HALF, :] = (one * cosine + two * sine).astype(LOW)
        out_ref[qw + top + HALF:qw + top + HEAD_DIM, :] = (two * cosine - one * sine).astype(LOW)
    out_ref[qw + kw:, :] = (dkv_ref[kw:, :] * inv_ref[...]).astype(LOW)
    turned_ref[...] = out_ref[...].T


def attend_back(order, rank, pieces, output, qrot, kv, mix, lse, cosine, sine, inv, heads, kvs, span):
    tokens = cosine.shape[1]
    qw, kw = heads * HEAD_DIM, kvs * HEAD_DIM
    return pl.pallas_call(
        functools.partial(attend_back_kernel, heads, kvs, span, len(pieces)),
        out_shape=(like((qw + 2 * kw, tokens)), like((tokens, qw + 2 * kw))),
        in_specs=[SMEM, SMEM] + [ANY] * len(pieces) + [VMEM] * 8,
        out_specs=(VMEM, VMEM),
        scratch_shapes=[
            pltpu.VMEM((kvs, tokens, HEAD_DIM), LOW),
            pltpu.VMEM((kvs, tokens, HEAD_DIM), LOW),
            pltpu.VMEM((heads, tokens), FULL),
            pltpu.VMEM((2 * kw, tokens), FULL),
            pltpu.VMEM((qw, tokens), LOW),
            pltpu.VMEM((tokens, pieces[0].shape[1]), LOW),
            arrivals(len(pieces)),
        ],
        compiler_params=PARAMS,
        name="attend_back",
    )(order, rank, *pieces, output, qrot, kv, mix, lse, cosine, sine, inv)


def layer(seq_size, fsdp_size, tokens, positions, attn_gain, query_weight, key_weight, value_weight, output_weight,
          ffn_gain, gate_weight, up_weight, down_weight, cotangent):
    span, width = tokens.shape[1:]
    heads = HEADS // seq_size
    kvs = max(1, KV_HEADS // seq_size)
    shared = max(1, seq_size // KV_HEADS)
    qw, kw = heads * HEAD_DIM, kvs * HEAD_DIM
    own_rows = query_weight.shape[0]
    hidden_own = gate_weight.shape[1] // seq_size
    chunk = 128 if hidden_own % 128 == 0 else 64
    parts = 2 if seq_size == 4 else 1
    piece_rows = span // parts
    into, back = (seq_size, fsdp_size, own_rows), (fsdp_size, seq_size, own_rows)
    here = lax.axis_index("seq")

    def after(x, *others):
        return lax.optimization_barrier((x, *others))[0]

    def swap(x, j):
        return lax.ppermute(x, "seq", [(i, i ^ j) for i in range(seq_size)])

    def seq_gather(own):
        if parts == 1:
            return [own[0]] + [swap(own[0], j) for j in range(1, seq_size)]
        a, b = own
        ax, by = swap(a, 1), swap(b, 2)
        ay, bx = swap(a, 2), swap(b, 1)
        ad, bd = swap(ax, 2), swap(by, 1)
        return [a, b, ax, bx, ay, by, ad, bd]

    def seq_scatter(pieces):
        if parts == 1:
            return (), [pieces[0]] + [swap(pieces[j], j) for j in range(1, seq_size)]
        a, b = pieces[::2], pieces[1::2]
        da, db = swap(a[3], 2), swap(b[3], 1)
        ya, xb = swap(a[2], 2), swap(b[1], 1)
        da = (a[1].astype(FULL) + da.astype(FULL)).astype(LOW)
        db = (b[2].astype(FULL) + db.astype(FULL)).astype(LOW)
        xa, yb = swap(da, 1), swap(db, 2)
        return (da, db), [a[0], ya, xa, b[0], xb, yb]

    def direct_scatter(blocks):
        return [blocks[0]] + [swap(blocks[j], j) for j in range(1, seq_size)]

    def spread(pieces_for):
        got = [pieces_for(here)] + [swap(pieces_for(here ^ j), j) for j in range(1, seq_size)]
        stack = jnp.stack(got)
        return jnp.concatenate(
            [lax.dynamic_index_in_dim(stack, here ^ t, 0, False) for t in range(seq_size)], 0
        )

    def collect(x):
        blocks = x.reshape(seq_size, own_rows, x.shape[1])
        return [lax.dynamic_index_in_dim(blocks, here, 0, False)] + [
            swap(lax.dynamic_index_in_dim(blocks, here ^ j, 0, False), j) for j in range(1, seq_size)
        ]

    def in_order(got):
        got = jnp.stack(got)
        return jnp.stack([lax.dynamic_index_in_dim(got, here ^ t, 0, False) for t in range(seq_size)]).astype(FULL)

    def fsdp_gather(x):
        return lax.all_gather(x, FSDP, axis=0, tiled=True)

    def exchange(x):
        return lax.ppermute(x, "core", [(0, 1), (1, 0)])

    def chip_scatter(x):
        return lax.psum_scatter(x.reshape(-1, x.shape[-1]), "chip", scatter_dimension=0, tiled=True)

    def fsdp_scatter(x):
        return lax.psum_scatter(x, FSDP, scatter_dimension=0, tiled=True)

    gain_one, gain_two = attn_gain.astype(FULL)[:, None], ffn_gain.astype(FULL)[:, None]

    def with_gain(weight, gain):
        return (weight.astype(FULL) * gain).astype(LOW)

    query_low, key_low, value_low = (with_gain(w, gain_one) for w in (query_weight, key_weight, value_weight))

    def qkv_for(t):
        first = (t * heads // GROUP) * HEAD_DIM
        return jnp.concatenate([
            lax.dynamic_slice_in_dim(query_low, t * qw, qw, 1),
            lax.dynamic_slice_in_dim(key_low, first, kw, 1),
            lax.dynamic_slice_in_dim(value_low, first, kw, 1),
        ], 1)

    own_tokens = tokens[0]
    own_pieces = call_own(
        functools.partial(regroup_kernel, into), (like((piece_rows, width)),) * parts, own_tokens
    )
    token_pieces = seq_gather(own_pieces)
    output_own = output_weight.reshape(own_rows, seq_size, -1).swapaxes(0, 1).reshape(seq_size * own_rows, -1)
    projections = fsdp_gather(jnp.concatenate([output_own, spread(qkv_for)], 1))
    gate_weight, up_weight = lax.optimization_barrier((gate_weight, up_weight, *own_pieces))[:2]
    gate_low, up_low = with_gain(gate_weight, gain_two), with_gain(up_weight, gain_two)

    def gate_up_for(t):
        gate = lax.dynamic_slice_in_dim(gate_low, t * hidden_own, hidden_own, 1)
        up = lax.dynamic_slice_in_dim(up_low, t * hidden_own, hidden_own, 1)
        return jnp.concatenate(
            [x[:, c:c + chunk] for c in range(0, hidden_own, chunk) for x in (gate, up)], 1
        )

    gate_up_own = spread(gate_up_for)
    gate_up_full = fsdp_gather(gate_up_own)
    down_full = fsdp_gather(down_weight)
    own_upstream = after(cotangent[0], gate_up_own, *token_pieces)
    upstream = [own_upstream] + [swap(own_upstream, j) for j in range(1, seq_size)]

    count = positions.shape[1] // span
    where_at = positions[0].reshape(count, span)
    where_at = jnp.stack([lax.dynamic_index_in_dim(where_at, here ^ j, 0, False) for j in range(count)])
    rank = where_at[:, 0] // span
    order = jnp.argsort(rank).astype(jnp.int32)
    cosine, sine = rope_tables(where_at.reshape(-1))

    qrot, kv, attended, mix, lse, inv_one = attend(
        order, rank, token_pieces, projections, cosine, sine, heads, kvs, span
    )
    attended, *upstream = lax.optimization_barrier((attended, *upstream))
    branch = seq_scatter(rows_of_product(attended, projections, piece_rows, into))[1]
    middle, inv_two, *own_pieces = call_own(
        functools.partial(middle_kernel, into, parts),
        (like((span, width), FULL), like((span, 1), FULL)) + (like((piece_rows, width)),) * parts,
        own_tokens, *branch,
    )

    normed_pieces = seq_gather(own_pieces)
    slope, hidden, normed = hidden_of(normed_pieces, gate_up_full, chunk)
    part_down = grad_down_of(hidden, upstream)
    grad_down = fsdp_scatter(part_down)
    grad_gate_up = grad_gate_up_of([after(upstream[0], part_down), *upstream[1:]], down_full, slope, chunk)
    first, grad_pieces = seq_scatter(grad_rows_of(grad_gate_up, gate_up_full, piece_rows))
    place, core = (at.astype(jnp.int32).reshape(1) for at in (here, lax.axis_index("core")))
    part_gate_up = grad_weight_of(
        after(normed, *first), exchange(normed), grad_gate_up, exchange(grad_gate_up), core, fsdp_size // 2
    )
    part_gate_up, *grad_pieces = lax.optimization_barrier((part_gate_up, *grad_pieces))
    grad_gate_up_own = chip_scatter(part_gate_up)
    grad_pieces[0] = after(grad_pieces[0], grad_down)
    grad_middle, *own_pieces = call_own(
        functools.partial(grad_middle_kernel, back, parts),
        (like((span, width), FULL),) + (like((piece_rows, width)),) * parts,
        cotangent[0], middle, inv_two, *grad_pieces,
    )

    branch_pieces = seq_gather(own_pieces)
    out_pieces = rows_of_product(after(hidden, own_pieces[0]), down_full, span)
    out_pieces = lax.optimization_barrier((*out_pieces, *branch_pieces))[:seq_size]
    out_pieces = direct_scatter(out_pieces)
    grad_qkv, grad_qkv_turned = attend_back(
        order, rank, branch_pieces, projections.reshape(fsdp_size, seq_size, own_rows, -1), qrot, kv, mix, lse,
        cosine, sine, inv_one, heads, kvs, span,
    )
    grad_qkv, *out_pieces = lax.optimization_barrier((grad_qkv, *out_pieces))
    part_projections = attention_weights_of(token_pieces, branch_pieces, grad_qkv, attended, into)
    grad_pieces = grad_rows_of(after(grad_qkv_turned, part_projections), projections, piece_rows)
    grad_projections = fsdp_scatter(after(part_projections, grad_gate_up_own, grad_pieces[0]))
    grad_pieces = seq_scatter(grad_pieces)[1]
    got = collect(after(grad_gate_up_own, *grad_pieces))
    block_out = call_own(block_out_kernel, like((span, width)), middle, *out_pieces)


    def whole_rows(x):
        return x.swapaxes(0, 1).reshape(own_rows, -1)

    if chunk == 128:
        rows_like = like((own_rows, gate_weight.shape[1]), FULL)
        grad_gate, grad_up, grad_ffn_gain = call_own(
            finish_gate_up_kernel, (rows_like, rows_like, like((1, own_rows), FULL)),
            *got, gate_weight, up_weight, gain_two, scalars=(place,),
        )
    else:
        got = in_order(got).reshape(seq_size, own_rows, -1, 2, chunk)
        grad_gate, grad_up = whole_rows(got[:, :, :, 0]), whole_rows(got[:, :, :, 1])
        grad_ffn_gain = jnp.sum(grad_gate * gate_weight.astype(FULL) + grad_up * up_weight.astype(FULL), 1)
        grad_gate, grad_up = grad_gate * gain_two, grad_up * gain_two
    grad_tokens = call_own(
        functools.partial(grad_tokens_kernel, back, parts), like((span, width), FULL),
        own_tokens, grad_middle, *grad_pieces,
    )
    grad_projections = after(grad_projections, grad_tokens, block_out, grad_ffn_gain)
    got = collect(grad_projections[:, -qw - 2 * kw:])
    if shared == 1 and kvs == 1:
        grad_query, grad_key, grad_value, grad_output, grad_attn_gain = call_own(
            finish_projections_kernel,
            tuple(like(w.shape, FULL) for w in (query_weight, key_weight, value_weight, output_weight))
            + (like((1, own_rows), FULL),),
            *got, grad_projections, query_weight, key_weight, value_weight, gain_one, scalars=(place,),
        )
    else:
        grad_output = grad_projections[:, :-qw - 2 * kw].reshape(seq_size, own_rows, -1).swapaxes(0, 1)
        grad_output = grad_output.reshape(own_rows, width).astype(FULL)
        got = in_order(got)
        grad_query = whole_rows(got[:, :, :qw])

        def of_heads(x):
            return whole_rows(x.reshape(seq_size // shared, shared, own_rows, kw).sum(1))

        grad_key, grad_value = of_heads(got[:, :, qw:qw + kw]), of_heads(got[:, :, qw + kw:])
        grads = (grad_query, grad_key, grad_value)
        grad_attn_gain = sum(
            jnp.sum(g * w.astype(FULL), 1) for g, w in zip(grads, (query_weight, key_weight, value_weight))
        )
        grad_query, grad_key, grad_value = (g * gain_one for g in grads)
    return (
        block_out[None],
        grad_tokens[None],
        grad_attn_gain.reshape(-1),
        grad_query,
        grad_key,
        grad_value,
        grad_output,
        grad_ffn_gain.reshape(-1),
        grad_gate,
        grad_up,
        grad_down.astype(FULL),
    )


def solution(mesh):
    seq_size, fsdp_size = mesh.shape["seq"], mesh.shape["fsdp"]
    split = Mesh(mesh.devices.reshape(seq_size, fsdp_size // 2, 2), ("seq", "chip", "core"))
    rows, vector, matrix = P(FSDP, "seq", None), P(("seq", *FSDP)), P(("seq", *FSDP), None)
    return jax.shard_map(
        functools.partial(layer, seq_size, fsdp_size),
        mesh=split,
        in_specs=(
            rows, P(FSDP, None), vector, matrix, matrix, matrix, matrix, vector, matrix, matrix, matrix, rows,
        ),
        out_specs=(rows, rows, vector, matrix, matrix, matrix, matrix, vector, matrix, matrix, matrix),
        check_vma=False,
    )
```

```python
import functools
import math

import jax
import jax.numpy as jnp
from jax import lax
from jax.experimental import pallas as pl
from jax.experimental.pallas import tpu as pltpu
from jax.sharding import Mesh
from jax.sharding import PartitionSpec as P

HEADS = 32
KV_HEADS = 4
HEAD_DIM = 64
HALF = HEAD_DIM // 2
GROUP = HEADS // KV_HEADS
EPSILON = 1e-05
SCALE = 1.0 / math.sqrt(HEAD_DIM)
FSDP = ("chip", "core")
LOW = jnp.bfloat16
FULL = jnp.float32
VMEM = pl.BlockSpec(memory_space=pltpu.VMEM)
ANY = pl.BlockSpec(memory_space=pltpu.HBM)
SMEM = pl.BlockSpec(memory_space=pltpu.SMEM)
PARAMS = pltpu.CompilerParams(vmem_limit_bytes=60 << 20)
NN, NT, TN = ((1,), (0,)), ((1,), (1,)), ((0,), (0,))


def dot(a, b, dims=NN):
    return lax.dot_general(a, b, (dims, ((), ())), preferred_element_type=FULL)


def like(shape, dtype=LOW):
    return jax.ShapeDtypeStruct(shape, dtype)


def rope_tables(where_at):
    frequency = 1.0 / 10000.0 ** (jnp.arange(HALF, dtype=FULL) * 2.0 / HEAD_DIM)
    angles = frequency[:, None] * where_at.astype(FULL)[None, :]
    return jnp.cos(angles), jnp.sin(angles)


def regroup(x, outer, inner, rows):
    return jnp.concatenate(
        [x[:, (o * inner + i) * rows:(o * inner + i + 1) * rows] for i in range(inner) for o in range(outer)], 1
    )


def join(pieces, whole_ref):
    at = 0
    for piece in pieces:
        whole_ref[at:at + piece.shape[0], :] = piece[...]
        at += piece.shape[0]


def fetch(pieces, whole_ref, sems):
    copies, at = [], 0
    for i, piece in enumerate(pieces):
        rows = piece.shape[0]
        copies.append(pltpu.make_async_copy(piece, whole_ref.at[pl.ds(at, rows)], sems.at[i]))
        at += rows
    for copy in copies:
        copy.start()
    for copy in copies:
        copy.wait()


def arrivals(count):
    return pltpu.SemaphoreType.DMA((count,))


def call_own(kernel, out_shape, *args, scalars=()):
    return pl.pallas_call(
        kernel, out_shape=out_shape, in_specs=[SMEM] * len(scalars) + [VMEM] * len(args),
        out_specs=jax.tree.map(lambda _: VMEM, out_shape), compiler_params=PARAMS,
        name=getattr(kernel, "func", kernel).__name__,
    )(*scalars, *args)


def added(refs):
    total = refs[0][...].astype(FULL)
    for ref in refs[1:]:
        total = total + ref[...].astype(FULL)
    return total


def regroup_kernel(grid, x_ref, *out_refs):
    x = regroup(x_ref[...].astype(FULL), *grid).astype(LOW)
    rows = out_refs[0].shape[0]
    for i, ref in enumerate(out_refs):
        ref[...] = x[i * rows:(i + 1) * rows]


def middle_kernel(grid, parts, *refs):
    tokens_ref, refs = refs[0], refs[1:]
    per = (len(refs) - 2 - parts) // parts
    middle_ref, inv_ref, *normed_refs = refs[per * parts:]
    rows = normed_refs[0].shape[0]
    for i in range(parts):
        at = slice(i * rows, (i + 1) * rows)
        middle = tokens_ref[at, :].astype(FULL) + added(refs[i * per:(i + 1) * per])
        inv = lax.rsqrt(jnp.mean(middle * middle, -1, keepdims=True) + EPSILON)
        middle_ref[at, :] = middle
        inv_ref[at, :] = inv
        normed_refs[i][...] = regroup(middle * inv, *grid).astype(LOW)


def grad_middle_kernel(grid, parts, *refs):
    upstream_ref, middle_ref, inv_ref, refs = refs[0], refs[1], refs[2], refs[3:]
    out_ref, *low_refs = refs[-1 - parts:]
    per = (len(refs) - 1 - parts) // parts
    rows = low_refs[0].shape[0]
    for i in range(parts):
        at = slice(i * rows, (i + 1) * rows)
        inv = inv_ref[at, :]
        normed = middle_ref[at, :] * inv
        grad = regroup(added(refs[i * per:(i + 1) * per]), *grid)
        grad = upstream_ref[at, :].astype(FULL) + inv * (grad - normed * jnp.mean(grad * normed, -1, keepdims=True))
        out_ref[at, :] = grad
        low_refs[i][...] = grad.astype(LOW)


def grad_tokens_kernel(grid, parts, *refs):
    tokens_ref, grad_ref, refs, out_ref = refs[0], refs[1], refs[2:-1], refs[-1]
    per = len(refs) // parts
    rows = out_ref.shape[0] // parts
    for i in range(parts):
        at = slice(i * rows, (i + 1) * rows)
        tokens = tokens_ref[at, :].astype(FULL)
        normed = tokens * lax.rsqrt(jnp.mean(tokens * tokens, -1, keepdims=True) + EPSILON)
        grad = regroup(added(refs[i * per:(i + 1) * per]), *grid)
        out_ref[at, :] = grad_ref[at, :] + grad - normed * jnp.mean(grad * normed, -1, keepdims=True)


def block_out_kernel(parts, *refs):
    middle_ref, refs, out_ref = refs[0], refs[1:-1], refs[-1]
    per, rows = len(refs) // parts, out_ref.shape[0] // parts
    for i in range(parts):
        at = slice(i * rows, (i + 1) * rows)
        out_ref[at, :] = (middle_ref[at, :] + added(refs[i * per:(i + 1) * per])).astype(LOW)


def as_row(column):
    return jnp.broadcast_to(column, (column.shape[0], 128)).T[:1]


def finish_gate_up_kernel(here_ref, *refs):
    *pieces, gate_ref, up_ref, gain_ref, grad_gate_ref, grad_up_ref, grad_gain_ref = refs
    gain, total = gain_ref[...], 0.0
    across, chunk = gate_ref.shape[1] // len(pieces), 128
    for j, piece in enumerate(pieces):
        first = (here_ref[0] ^ j) * across
        for c in range(across // chunk):
            there = pl.ds(pl.multiple_of(first + c * chunk, chunk), chunk)
            for i, (weight_ref, out_ref) in enumerate(((gate_ref, grad_gate_ref), (up_ref, grad_up_ref))):
                grad = piece[:, (2 * c + i) * chunk:(2 * c + i + 1) * chunk].astype(FULL)
                out_ref[:, there] = grad * gain
                total = total + grad * weight_ref[:, there].astype(FULL)
    grad_gain_ref[...] = as_row(jnp.sum(total, 1, keepdims=True))


def finish_projections_kernel(here_ref, *refs):
    *pieces, own_ref, query_ref, key_ref, value_ref, gain_ref = refs[:-5]
    grad_query_ref, grad_key_ref, grad_value_ref, grad_output_ref, grad_gain_ref = refs[-5:]
    gain, count = gain_ref[...], len(pieces)
    rows = gain.shape[0]
    qw, kw = query_ref.shape[1] // count, key_ref.shape[1] // count
    total = 0.0
    for j, piece in enumerate(pieces):
        there = pl.ds(pl.multiple_of((here_ref[0] ^ j) * qw, qw), qw)
        grad = piece[:, :qw].astype(FULL)
        grad_query_ref[:, there] = grad * gain
        total = total + jnp.sum(grad * query_ref[:, there].astype(FULL), 1, keepdims=True)
    for first, weight_ref, out_ref in ((qw, key_ref, grad_key_ref), (qw + kw, value_ref, grad_value_ref)):
        grad = [jnp.zeros((rows, kw), FULL)] * count
        for j, piece in enumerate(pieces):
            mine = piece[:, first:first + kw].astype(FULL)
            for t in range(count):
                grad[t] = jnp.where(here_ref[0] == t ^ j, mine, grad[t])
        grad = jnp.concatenate(grad, 1)
        out_ref[...] = grad * gain
        total = total + jnp.sum(grad * weight_ref[...].astype(FULL), 1, keepdims=True)
    across = grad_output_ref.shape[1] // count
    for part in range(count):
        grad_output_ref[:, part * across:(part + 1) * across] = own_ref[part * rows:(part + 1) * rows, :across].astype(FULL)
    grad_gain_ref[...] = as_row(total)


def rows_of(pieces):
    return sum(p.shape[0] for p in pieces)


def whole(shape):
    return pl.BlockSpec(shape, lambda i: (0,) * len(shape))


def columns(rows, width):
    return pl.BlockSpec((rows, width), lambda i: (0, i))


def by_rows(height, width):
    return pl.BlockSpec((height, width), lambda i: (i, 0))


def hidden_kernel(count, chunk, *refs):
    pieces, refs = refs[:count], refs[count:]
    weight_ref, slope_ref, hidden_ref, out_ref, normed_ref, sems, out_sem = refs
    step = pl.program_id(0)
    out_copy = pltpu.make_async_copy(normed_ref, out_ref, out_sem)

    @pl.when(step == 0)
    def _():
        fetch(pieces, normed_ref, sems)
        out_copy.start()

    both = dot(normed_ref[...], weight_ref[...])
    gate, up = both[:, :chunk], both[:, chunk:]
    sigmoid = jax.nn.sigmoid(gate)
    silu = gate * sigmoid
    slope = up * sigmoid * (1.0 + gate * (1.0 - sigmoid))
    slope_ref[...] = jnp.concatenate([slope, silu], 1).astype(LOW)
    hidden_ref[...] = (silu * up).T.astype(LOW)

    @pl.when(step == pl.num_programs(0) - 1)
    def _():
        out_copy.wait()


def hidden_of(pieces, weight, chunk):
    tokens, (width, both) = rows_of(pieces), weight.shape
    return pl.pallas_call(
        functools.partial(hidden_kernel, len(pieces), chunk),
        grid=(both // (2 * chunk),),
        in_specs=[ANY] * len(pieces) + [columns(width, 2 * chunk)],
        out_specs=(columns(tokens, 2 * chunk), by_rows(chunk, tokens), ANY),
        out_shape=(like((tokens, both)), like((both // 2, tokens)), like((tokens, width))),
        scratch_shapes=[pltpu.VMEM((tokens, width), LOW), arrivals(len(pieces)), pltpu.SemaphoreType.DMA],
        compiler_params=PARAMS,
        name="hidden_of",
    )(*pieces, weight)


def grad_down_kernel(count, *refs):
    pieces, (hidden_ref, out_ref, block_ref) = refs[:count], refs[count:]
    join(pieces, block_ref)
    out_ref[...] = dot(hidden_ref[...], block_ref[...]).astype(LOW)


def grad_down_of(hidden, pieces, block=256):
    tokens, width = rows_of(pieces), pieces[0].shape[1]
    return pl.pallas_call(
        functools.partial(grad_down_kernel, len(pieces)),
        grid=(width // block,),
        in_specs=[columns(p.shape[0], block) for p in pieces] + [whole(hidden.shape)],
        out_specs=columns(hidden.shape[0], block),
        out_shape=like((hidden.shape[0], width)),
        scratch_shapes=[pltpu.VMEM((tokens, block), LOW)],
        compiler_params=PARAMS,
        name="grad_down_of",
    )(*pieces, hidden)


def grad_gate_up_kernel(count, chunk, odd, *refs):
    pieces, (down_ref, slope_ref, out_ref, upstream_ref, sems) = refs[:count], refs[count:]
    step, steps = pl.program_id(0), pl.num_programs(0)

    @pl.when(step == 0)
    def _():
        fetch(pieces, upstream_ref, sems)

    def work(chunks):
        grad = dot(upstream_ref[...], down_ref[:chunks * chunk, :], NT)
        each = [grad[:, c * chunk:(c + 1) * chunk] for c in range(chunks) for _ in range(2)]
        width = chunks * 2 * chunk
        out_ref[:, :width] = (jnp.concatenate(each, 1) * slope_ref[:, :width].astype(FULL)).astype(LOW)

    @pl.when(step < steps - odd)
    def _():
        work(2)

    if odd:

        @pl.when(step == steps - 1)
        def _():
            work(1)


def grad_gate_up_of(pieces, down, slope, chunk):
    (tokens, width), depth = (rows_of(pieces), pieces[0].shape[1]), down.shape[0]
    return pl.pallas_call(
        functools.partial(grad_gate_up_kernel, len(pieces), chunk, depth // chunk % 2),
        grid=(pl.cdiv(depth, 2 * chunk),),
        in_specs=[ANY] * len(pieces) + [by_rows(2 * chunk, width), columns(tokens, 4 * chunk)],
        out_specs=columns(tokens, 4 * chunk),
        out_shape=like(slope.shape),
        scratch_shapes=[pltpu.VMEM((tokens, width), LOW), arrivals(len(pieces))],
        compiler_params=PARAMS,
        name="grad_gate_up_of",
    )(*pieces, down, slope)


def grad_rows_kernel(first, grad_ref, weight_ref, *out_refs):
    grad = dot(grad_ref[...], weight_ref[:, first:], NT).astype(LOW)
    rows = out_refs[0].shape[0]
    for i, ref in enumerate(out_refs):
        ref[...] = grad[i * rows:(i + 1) * rows]


def grad_rows_of(grad, weight, piece_rows, block=512):
    tokens, width = grad.shape[0], weight.shape[0]
    count = tokens // piece_rows
    return pl.pallas_call(
        functools.partial(grad_rows_kernel, weight.shape[1] - grad.shape[1]),
        grid=(width // block,),
        in_specs=[whole(grad.shape), by_rows(block, weight.shape[1])],
        out_specs=(columns(piece_rows, block),) * count,
        out_shape=(like((piece_rows, width)),) * count,
        compiler_params=PARAMS,
        name="grad_rows_of",
    )(grad, weight)


def grad_weight_kernel(core_ref, left_ref, other_left_ref, grad_ref, other_grad_ref, out_ref):
    got = dot(left_ref[...], grad_ref[...], TN) + dot(other_left_ref[...], other_grad_ref[...], TN)
    out_ref[...] = got.astype(LOW)


def grad_weight_of(left, other_left, grad, other_grad, core, chips):
    tokens, width = left.shape
    block = width // chips // 2
    mine = pl.BlockSpec((tokens, block), lambda i, core_ref: (0, i * 2 + core_ref[0]))
    every = pl.BlockSpec(grad.shape, lambda i, core_ref: (0, 0))
    return pl.pallas_call(
        grad_weight_kernel,
        grid_spec=pltpu.PrefetchScalarGridSpec(
            num_scalar_prefetch=1,
            grid=(chips,),
            in_specs=[mine, mine, every, every],
            out_specs=pl.BlockSpec((block, grad.shape[1]), lambda i, core_ref: (i, 0)),
        ),
        out_shape=like((width // 2, grad.shape[1])),
        compiler_params=PARAMS,
        name="grad_weight_of",
    )(core, left, other_left, grad, other_grad)


def rows_kernel(left_ref, weight_ref, *refs):
    *out_refs, turned_ref = refs

    @pl.when(pl.program_id(0) == 0)
    def _():
        turned_ref[...] = left_ref[...].T

    weight = weight_ref[...].reshape(turned_ref.shape[1], weight_ref.shape[-1])
    out = dot(turned_ref[...], weight).astype(LOW)
    rows = out_refs[0].shape[0]
    for i, ref in enumerate(out_refs):
        ref[...] = out[i * rows:(i + 1) * rows]


def rows_of_product(left, weight, piece_rows, inner=None, block=512):
    depth, tokens = left.shape
    count = tokens // piece_rows
    if inner is None:
        width, spec = weight.shape[1], columns(depth, block)
    else:
        seq_size, fsdp_size, own_rows = inner
        width = weight.shape[0]
        block = min(block, width // seq_size)
        per = width // seq_size // block
        weight = weight.reshape(fsdp_size, seq_size, own_rows, -1)
        spec = pl.BlockSpec((fsdp_size, 1, own_rows, block), lambda i: (0, i // per, 0, i % per))
    return pl.pallas_call(
        rows_kernel,
        grid=(width // block,),
        in_specs=[whole(left.shape), spec],
        out_specs=(columns(piece_rows, block),) * count,
        out_shape=(like((piece_rows, width)),) * count,
        scratch_shapes=[pltpu.VMEM((tokens, depth), LOW)],
        compiler_params=PARAMS,
        name="rows_of_product",
    )(left, weight)


def attention_weights_kernel(count, inner, *refs):
    tokens, grads = refs[:count], refs[count:2 * count]
    grad_qkv_ref, attended_ref, out_ref, block_ref = refs[2 * count:]
    seq_size, fsdp_size, own_rows = inner
    step, block = pl.program_id(0), block_ref.shape[1]
    across = out_ref.shape[1] - grad_qkv_ref.shape[0]
    join(tokens, block_ref)
    there = pl.ds(pl.multiple_of(step * block, block), block)
    out_ref[there, across:] = dot(grad_qkv_ref[...], block_ref[...]).T.astype(LOW)
    join(grads, block_ref)
    got = dot(attended_ref[...], block_ref[...]).astype(LOW)
    part = step * block // across
    first = step * block % across
    for f in range(fsdp_size):
        rows = pl.ds(pl.multiple_of((f * seq_size + part) * own_rows, own_rows), own_rows)
        out_ref[rows, pl.ds(pl.multiple_of(first, 128), block)] = got[f * own_rows:(f + 1) * own_rows]


def attention_weights_of(tokens, grads, grad_qkv, attended, inner, block=512):
    count, width = len(tokens), tokens[0].shape[1]
    block = min(block, width // inner[0])
    shape = (width, grad_qkv.shape[0] + width // inner[0])
    return pl.pallas_call(
        functools.partial(attention_weights_kernel, count, inner),
        grid=(width // block,),
        in_specs=[columns(p.shape[0], block) for p in (*tokens, *grads)]
        + [whole(grad_qkv.shape), whole(attended.shape)],
        out_specs=whole(shape),
        out_shape=like(shape),
        scratch_shapes=[pltpu.VMEM((rows_of(tokens), block), LOW)],
        compiler_params=PARAMS,
        name="attention_weights_of",
    )(*tokens, *grads, grad_qkv, attended)


def attend_kernel(heads, kvs, span, pieces, order_ref, rank_ref, *refs):
    token_refs, refs = refs[:pieces], refs[pieces:]
    weight_ref, cos_ref, sin_ref, qrot_ref, kv_ref, att_ref, mix_ref, lse_ref, inv_ref, *scratch = refs
    keys_ref, qkv_ref, tokens_ref, sems = scratch
    fetch(token_refs, tokens_ref, sems)
    count = cos_ref.shape[1] // span
    for at in range(0, tokens_ref.shape[0], span):
        there = slice(at, at + span)
        values = tokens_ref[there, :].astype(FULL)
        inv = lax.rsqrt(jnp.mean(values * values, -1, keepdims=True) + EPSILON)
        qkv_ref[:, there] = (dot(tokens_ref[there, :], weight_ref[:, -qkv_ref.shape[0]:]) * inv).T
        inv_ref[:, there] = jnp.broadcast_to(inv, (span, 128)).T[:1]
    qw, kw = heads * HEAD_DIM, kvs * HEAD_DIM
    cosine, sine = cos_ref[...], sin_ref[...]

    def rotated(row):
        one, two = qkv_ref[row:row + HALF, :], qkv_ref[row + HALF:row + HEAD_DIM, :]
        return jnp.concatenate([one * cosine - two * sine, two * cosine + one * sine], 0)

    for h in range(heads):
        qrot_ref[h * HEAD_DIM:(h + 1) * HEAD_DIM, :] = rotated(h * HEAD_DIM).astype(LOW)
    for k in range(kvs):
        turned = rotated(qw + k * HEAD_DIM).astype(LOW)
        kv_ref[k * HEAD_DIM:(k + 1) * HEAD_DIM, :] = turned
        keys_ref[k] = (turned.astype(FULL) * SCALE).T.astype(LOW)
    kv_ref[kw:, :] = qkv_ref[qw + kw:, :].astype(LOW)

    def one_block(qb, _):
        cols = pl.ds(pl.multiple_of(qb * span, span), span)
        rank = rank_ref[qb]

        def step(at, state, diagonal):
            rows = pl.ds(pl.multiple_of(order_ref[at] * span, span), span)
            out = []
            for h in range(heads):
                top, total, mixed = state[h]
                k = h * kvs // heads
                scores = dot(keys_ref[k, rows, :], qrot_ref[h * HEAD_DIM:(h + 1) * HEAD_DIM, cols])
                if diagonal:
                    key_at = lax.broadcasted_iota(jnp.int32, (span, span), 0)
                    query_at = lax.broadcasted_iota(jnp.int32, (span, span), 1)
                    scores = jnp.where(key_at <= query_at, scores, -1e30)
                new_top = jnp.maximum(top, jnp.max(scores, 0, keepdims=True))
                weights = jnp.exp(scores - new_top)
                fade = jnp.exp(top - new_top)
                total = total * fade + jnp.sum(weights, 0, keepdims=True)
                values = kv_ref[kw + k * HEAD_DIM:kw + (k + 1) * HEAD_DIM, rows]
                mixed = mixed * fade + dot(values, weights.astype(LOW))
                out.append((new_top, total, mixed))
            return out

        start = [(jnp.full((1, span), -1e30, FULL), jnp.zeros((1, span), FULL),
                  jnp.zeros((HEAD_DIM, span), FULL)) for _ in range(heads)]
        state = lax.fori_loop(0, rank, lambda at, st: step(at, st, False), start)
        state = step(rank, state, True)
        for h in range(heads):
            top, total, mixed = state[h]
            mixed = mixed / total
            mix_ref[h * HEAD_DIM:(h + 1) * HEAD_DIM, cols] = mixed
            att_ref[h * HEAD_DIM:(h + 1) * HEAD_DIM, cols] = mixed.astype(LOW)
            lse_ref[h:h + 1, cols] = top + jnp.log(total)
        return 0

    lax.fori_loop(0, count, one_block, 0)


def attend(order, rank, pieces, weight, cosine, sine, heads, kvs, span):
    tokens = cosine.shape[1]
    qw, kw = heads * HEAD_DIM, kvs * HEAD_DIM
    return pl.pallas_call(
        functools.partial(attend_kernel, heads, kvs, span, len(pieces)),
        out_shape=(
            like((qw, tokens)), like((2 * kw, tokens)), like((qw, tokens)), like((qw, tokens), FULL),
            like((heads, tokens), FULL), like((1, tokens), FULL),
        ),
        in_specs=[SMEM, SMEM] + [ANY] * len(pieces) + [VMEM] * 3,
        out_specs=(VMEM,) * 6,
        scratch_shapes=[
            pltpu.VMEM((kvs, tokens, HEAD_DIM), LOW),
            pltpu.VMEM((qw + 2 * kw, tokens), FULL),
            pltpu.VMEM((tokens, weight.shape[0]), LOW),
            arrivals(len(pieces)),
        ],
        compiler_params=PARAMS,
        name="attend",
    )(order, rank, *pieces, weight, cosine, sine)


def attend_back_kernel(heads, kvs, span, pieces, order_ref, rank_ref, *refs):
    branch_refs, refs = refs[:pieces], refs[pieces:]
    output_ref, qrot_ref, kv_ref, mix_ref, lse_ref, cos_ref, sin_ref, inv_ref, out_ref, turned_ref, *scratch = refs
    keys_ref, values_ref, delta_ref, dkv_ref, grad_ref, branch_ref, sems = scratch
    count = cos_ref.shape[1] // span
    qw, kw = heads * HEAD_DIM, kvs * HEAD_DIM
    fetch(branch_refs, branch_ref, sems)
    seq_size, across = output_ref.shape[1], branch_ref.shape[1] // output_ref.shape[1]
    for at in range(0, branch_ref.shape[0], span):
        total = 0.0
        for part in range(seq_size):
            weight = output_ref[:, part, :, :across].reshape(qw, across)
            total = total + dot(weight, branch_ref[at:at + span, part * across:(part + 1) * across], NT)
        grad_ref[:, at:at + span] = total.astype(LOW)
    qw, kw = heads * HEAD_DIM, kvs * HEAD_DIM
    for k in range(kvs):
        keys_ref[k] = (kv_ref[k * HEAD_DIM:(k + 1) * HEAD_DIM, :].astype(FULL) * SCALE).T.astype(LOW)
        values_ref[k] = kv_ref[kw + k * HEAD_DIM:kw + (k + 1) * HEAD_DIM, :].astype(FULL).T.astype(LOW)
    for h in range(heads):
        rows = slice(h * HEAD_DIM, (h + 1) * HEAD_DIM)
        delta_ref[h:h + 1, :] = jnp.sum(grad_ref[rows, :].astype(FULL) * mix_ref[rows, :], 0, keepdims=True)
    dkv_ref[...] = jnp.zeros_like(dkv_ref)

    def one_block(qb, _):
        cols = pl.ds(pl.multiple_of(qb * span, span), span)
        rank = rank_ref[qb]

        def step(at, state, diagonal):
            rows = pl.ds(pl.multiple_of(order_ref[at] * span, span), span)
            out = []
            dkeys = [None] * kvs
            dvalues = [None] * kvs
            for h in range(heads):
                k = h * kvs // heads
                mine = slice(h * HEAD_DIM, (h + 1) * HEAD_DIM)
                query = qrot_ref[mine, cols]
                grad = grad_ref[mine, cols]
                scores = dot(keys_ref[k, rows, :], query)
                weights = jnp.exp(scores - lse_ref[h:h + 1, cols])
                if diagonal:
                    key_at = lax.broadcasted_iota(jnp.int32, (span, span), 0)
                    query_at = lax.broadcasted_iota(jnp.int32, (span, span), 1)
                    weights = jnp.where(key_at <= query_at, weights, 0.0)
                grad_probs = dot(values_ref[k, rows, :], grad)
                grad_scores = (weights * (grad_probs - delta_ref[h:h + 1, cols])).astype(LOW)
                key_t = kv_ref[k * HEAD_DIM:(k + 1) * HEAD_DIM, rows]
                out.append(state[h] + dot(key_t, grad_scores))
                dk = dot(query, grad_scores, NT)
                dv = dot(grad, weights.astype(LOW), NT)
                dkeys[k] = dk if dkeys[k] is None else dkeys[k] + dk
                dvalues[k] = dv if dvalues[k] is None else dvalues[k] + dv
            for k in range(kvs):
                mine = slice(k * HEAD_DIM, (k + 1) * HEAD_DIM)
                dkv_ref[mine, rows] += dkeys[k]
                mine = slice(kw + k * HEAD_DIM, kw + (k + 1) * HEAD_DIM)
                dkv_ref[mine, rows] += dvalues[k]
            return out

        state = [jnp.zeros((HEAD_DIM, span), FULL) for _ in range(heads)]
        state = lax.fori_loop(0, rank, lambda at, st: step(at, st, False), state)
        state = step(rank, state, True)
        scale = inv_ref[:, cols] * SCALE
        cosine, sine = cos_ref[:, cols], sin_ref[:, cols]
        for h in range(heads):
            one, two = state[h][:HALF] * scale, state[h][HALF:] * scale
            out_ref[h * HEAD_DIM:h * HEAD_DIM + HALF, cols] = (one * cosine + two * sine).astype(LOW)
            out_ref[h * HEAD_DIM + HALF:(h + 1) * HEAD_DIM, cols] = (two * cosine - one * sine).astype(LOW)
        return 0

    lax.fori_loop(0, count, one_block, 0)
    cosine, sine = cos_ref[...], sin_ref[...]
    scale = inv_ref[...] * SCALE
    for k in range(kvs):
        top = k * HEAD_DIM
        one, two = dkv_ref[top:top + HALF, :] * scale, dkv_ref[top + HALF:top + HEAD_DIM, :] * scale
        out_ref[qw + top:qw + top + HALF, :] = (one * cosine + two * sine).astype(LOW)
        out_ref[qw + top + HALF:qw + top + HEAD_DIM, :] = (two * cosine - one * sine).astype(LOW)
    out_ref[qw + kw:, :] = (dkv_ref[kw:, :] * inv_ref[...]).astype(LOW)
    turned_ref[...] = out_ref[...].T


def attend_back(order, rank, pieces, output, qrot, kv, mix, lse, cosine, sine, inv, heads, kvs, span):
    tokens = cosine.shape[1]
    qw, kw = heads * HEAD_DIM, kvs * HEAD_DIM
    return pl.pallas_call(
        functools.partial(attend_back_kernel, heads, kvs, span, len(pieces)),
        out_shape=(like((qw + 2 * kw, tokens)), like((tokens, qw + 2 * kw))),
        in_specs=[SMEM, SMEM] + [ANY] * len(pieces) + [VMEM] * 8,
        out_specs=(VMEM, VMEM),
        scratch_shapes=[
            pltpu.VMEM((kvs, tokens, HEAD_DIM), LOW),
            pltpu.VMEM((kvs, tokens, HEAD_DIM), LOW),
            pltpu.VMEM((heads, tokens), FULL),
            pltpu.VMEM((2 * kw, tokens), FULL),
            pltpu.VMEM((qw, tokens), LOW),
            pltpu.VMEM((tokens, pieces[0].shape[1]), LOW),
            arrivals(len(pieces)),
        ],
        compiler_params=PARAMS,
        name="attend_back",
    )(order, rank, *pieces, output, qrot, kv, mix, lse, cosine, sine, inv)


def layer(seq_size, fsdp_size, tokens, positions, attn_gain, query_weight, key_weight, value_weight, output_weight,
          ffn_gain, gate_weight, up_weight, down_weight, cotangent):
    span, width = tokens.shape[1:]
    heads = HEADS // seq_size
    kvs = max(1, KV_HEADS // seq_size)
    shared = max(1, seq_size // KV_HEADS)
    qw, kw = heads * HEAD_DIM, kvs * HEAD_DIM
    own_rows = query_weight.shape[0]
    hidden_own = gate_weight.shape[1] // seq_size
    chunk = 128 if hidden_own % 128 == 0 else 64
    parts = 2 if seq_size == 4 else 1
    piece_rows = span // parts
    into, back = (seq_size, fsdp_size, own_rows), (fsdp_size, seq_size, own_rows)
    here = lax.axis_index("seq")

    def after(x, *others):
        return lax.optimization_barrier((x, *others))[0]

    def swap(x, j):
        return lax.ppermute(x, "seq", [(i, i ^ j) for i in range(seq_size)])

    def seq_gather(own):
        if parts == 1:
            return [own[0]] + [swap(own[0], j) for j in range(1, seq_size)]
        a, b = own
        ax, by = swap(a, 1), swap(b, 2)
        ay, bx = swap(a, 2), swap(b, 1)
        ad, bd = swap(ax, 2), swap(by, 1)
        return [a, b, ax, bx, ay, by, ad, bd]

    def scatter_start(pieces):
        if parts == 1:
            return [swap(pieces[j], j) for j in range(1, seq_size)]
        a, b = pieces[::2], pieces[1::2]
        return [swap(a[3], 2), swap(b[3], 1), swap(a[2], 2), swap(b[1], 1)]

    def scatter_end(pieces, came):
        if parts == 1:
            return (), [pieces[0], *came]
        a, b, (da, db, ya, xb) = pieces[::2], pieces[1::2], came
        da = (a[1].astype(FULL) + da.astype(FULL)).astype(LOW)
        db = (b[2].astype(FULL) + db.astype(FULL)).astype(LOW)
        return (da, db), [a[0], ya, swap(da, 1), b[0], xb, swap(db, 2)]

    def seq_scatter(pieces):
        return scatter_end(pieces, scatter_start(pieces))

    def spread(pieces_for):
        got = [pieces_for(here)] + [swap(pieces_for(here ^ j), j) for j in range(1, seq_size)]
        stack = jnp.stack(got)
        return jnp.concatenate(
            [lax.dynamic_index_in_dim(stack, here ^ t, 0, False) for t in range(seq_size)], 0
        )

    def collect(x):
        blocks = x.reshape(seq_size, own_rows, x.shape[1])
        return [lax.dynamic_index_in_dim(blocks, here, 0, False)] + [
            swap(lax.dynamic_index_in_dim(blocks, here ^ j, 0, False), j) for j in range(1, seq_size)
        ]

    def in_order(got):
        got = jnp.stack(got)
        return jnp.stack([lax.dynamic_index_in_dim(got, here ^ t, 0, False) for t in range(seq_size)]).astype(FULL)

    def fsdp_gather(x):
        return lax.all_gather(x, FSDP, axis=0, tiled=True)

    def exchange(x):
        return lax.ppermute(x, "core", [(0, 1), (1, 0)])

    def chip_scatter(x):
        return lax.psum_scatter(x.reshape(-1, x.shape[-1]), "chip", scatter_dimension=0, tiled=True)

    def fsdp_scatter(x):
        return lax.psum_scatter(x, FSDP, scatter_dimension=0, tiled=True)

    gain_one, gain_two = attn_gain.astype(FULL)[:, None], ffn_gain.astype(FULL)[:, None]

    def with_gain(weight, gain):
        return (weight.astype(FULL) * gain).astype(LOW)

    query_low, key_low, value_low = (with_gain(w, gain_one) for w in (query_weight, key_weight, value_weight))

    def qkv_for(t):
        first = (t * heads // GROUP) * HEAD_DIM
        return jnp.concatenate([
            lax.dynamic_slice_in_dim(query_low, t * qw, qw, 1),
            lax.dynamic_slice_in_dim(key_low, first, kw, 1),
            lax.dynamic_slice_in_dim(value_low, first, kw, 1),
        ], 1)

    own_tokens = tokens[0]
    own_pieces = call_own(
        functools.partial(regroup_kernel, into), (like((piece_rows, width)),) * parts, own_tokens
    )
    token_pieces = seq_gather(own_pieces)
    output_own = output_weight.reshape(own_rows, seq_size, -1).swapaxes(0, 1).reshape(seq_size * own_rows, -1)
    projections = fsdp_gather(jnp.concatenate([output_own, spread(qkv_for)], 1))
    gate_weight, up_weight = lax.optimization_barrier((gate_weight, up_weight, *own_pieces))[:2]
    gate_low, up_low = with_gain(gate_weight, gain_two), with_gain(up_weight, gain_two)

    def gate_up_for(t):
        gate = lax.dynamic_slice_in_dim(gate_low, t * hidden_own, hidden_own, 1)
        up = lax.dynamic_slice_in_dim(up_low, t * hidden_own, hidden_own, 1)
        return jnp.concatenate(
            [x[:, c:c + chunk] for c in range(0, hidden_own, chunk) for x in (gate, up)], 1
        )

    gate_up_own = spread(gate_up_for)
    gate_up_full = fsdp_gather(gate_up_own)
    down_full = fsdp_gather(down_weight)
    own_upstream = after(cotangent[0], gate_up_own, *token_pieces)
    upstream = [own_upstream] + [swap(own_upstream, j) for j in range(1, seq_size)]

    count = positions.shape[1] // span
    where_at = positions[0].reshape(count, span)
    where_at = jnp.stack([lax.dynamic_index_in_dim(where_at, here ^ j, 0, False) for j in range(count)])
    rank = where_at[:, 0] // span
    order = jnp.argsort(rank).astype(jnp.int32)
    cosine, sine = rope_tables(where_at.reshape(-1))

    qrot, kv, attended, mix, lse, inv_one = attend(
        order, rank, token_pieces, projections, cosine, sine, heads, kvs, span
    )
    attended, *upstream = lax.optimization_barrier((attended, *upstream))
    branch = seq_scatter(rows_of_product(attended, projections, piece_rows, into))[1]
    middle, inv_two, *own_pieces = call_own(
        functools.partial(middle_kernel, into, parts),
        (like((span, width), FULL), like((span, 1), FULL)) + (like((piece_rows, width)),) * parts,
        own_tokens, *branch,
    )

    normed_pieces = seq_gather(own_pieces)
    slope, hidden, normed = hidden_of(normed_pieces, gate_up_full, chunk)
    part_down = grad_down_of(hidden, upstream)
    grad_down = fsdp_scatter(part_down)
    grad_gate_up = grad_gate_up_of([after(upstream[0], part_down), *upstream[1:]], down_full, slope, chunk)
    first, grad_pieces = seq_scatter(grad_rows_of(grad_gate_up, gate_up_full, piece_rows))
    place, core = (at.astype(jnp.int32).reshape(1) for at in (here, lax.axis_index("core")))
    part_gate_up = grad_weight_of(
        after(normed, *first), exchange(normed), grad_gate_up, exchange(grad_gate_up), core, fsdp_size // 2
    )
    part_gate_up, *grad_pieces = lax.optimization_barrier((part_gate_up, *grad_pieces))
    grad_gate_up_own = chip_scatter(part_gate_up)
    grad_pieces[0] = after(grad_pieces[0], grad_down)
    grad_middle, *own_pieces = call_own(
        functools.partial(grad_middle_kernel, back, parts),
        (like((span, width), FULL),) + (like((piece_rows, width)),) * parts,
        cotangent[0], middle, inv_two, *grad_pieces,
    )

    branch_pieces = seq_gather(own_pieces)
    out_pieces = rows_of_product(after(hidden, own_pieces[0]), down_full, piece_rows)
    out_pieces = lax.optimization_barrier((*out_pieces, *branch_pieces))[:len(out_pieces)]
    out_came = scatter_start(out_pieces)
    grad_qkv, grad_qkv_turned = attend_back(
        order, rank, branch_pieces, projections.reshape(fsdp_size, seq_size, own_rows, -1), qrot, kv, mix, lse,
        cosine, sine, inv_one, heads, kvs, span,
    )
    grad_qkv, grad_qkv_turned, *out_came = lax.optimization_barrier((grad_qkv, grad_qkv_turned, *out_came))
    part_projections = attention_weights_of(token_pieces, branch_pieces, grad_qkv, attended, into)
    grad_pieces = grad_rows_of(grad_qkv_turned, projections, piece_rows)
    first, grad_pieces = seq_scatter(grad_pieces)
    grad_projections = fsdp_scatter(after(part_projections, grad_gate_up_own, *first))
    got = collect(after(grad_gate_up_own, *grad_pieces))
    out_pieces = scatter_end(out_pieces, out_came)[1]
    block_out = call_own(functools.partial(block_out_kernel, parts), like((span, width)), middle, *out_pieces)


    def whole_rows(x):
        return x.swapaxes(0, 1).reshape(own_rows, -1)

    if chunk == 128:
        rows_like = like((own_rows, gate_weight.shape[1]), FULL)
        grad_gate, grad_up, grad_ffn_gain = call_own(
            finish_gate_up_kernel, (rows_like, rows_like, like((1, own_rows), FULL)),
            *got, gate_weight, up_weight, gain_two, scalars=(place,),
        )
    else:
        got = in_order(got).reshape(seq_size, own_rows, -1, 2, chunk)
        grad_gate, grad_up = whole_rows(got[:, :, :, 0]), whole_rows(got[:, :, :, 1])
        grad_ffn_gain = jnp.sum(grad_gate * gate_weight.astype(FULL) + grad_up * up_weight.astype(FULL), 1)
        grad_gate, grad_up = grad_gate * gain_two, grad_up * gain_two
    grad_tokens = call_own(
        functools.partial(grad_tokens_kernel, back, parts), like((span, width), FULL),
        own_tokens, grad_middle, *grad_pieces,
    )
    grad_projections = after(grad_projections, grad_tokens, block_out, grad_ffn_gain)
    got = collect(grad_projections[:, -qw - 2 * kw:])
    if shared == 1 and kvs == 1:
        grad_query, grad_key, grad_value, grad_output, grad_attn_gain = call_own(
            finish_projections_kernel,
            tuple(like(w.shape, FULL) for w in (query_weight, key_weight, value_weight, output_weight))
            + (like((1, own_rows), FULL),),
            *got, grad_projections, query_weight, key_weight, value_weight, gain_one, scalars=(place,),
        )
    else:
        grad_output = grad_projections[:, :-qw - 2 * kw].reshape(seq_size, own_rows, -1).swapaxes(0, 1)
        grad_output = grad_output.reshape(own_rows, width).astype(FULL)
        got = in_order(got)
        grad_query = whole_rows(got[:, :, :qw])

        def of_heads(x):
            return whole_rows(x.reshape(seq_size // shared, shared, own_rows, kw).sum(1))

        grad_key, grad_value = of_heads(got[:, :, qw:qw + kw]), of_heads(got[:, :, qw + kw:])
        grads = (grad_query, grad_key, grad_value)
        grad_attn_gain = sum(
            jnp.sum(g * w.astype(FULL), 1) for g, w in zip(grads, (query_weight, key_weight, value_weight))
        )
        grad_query, grad_key, grad_value = (g * gain_one for g in grads)
    return (
        block_out[None],
        grad_tokens[None],
        grad_attn_gain.reshape(-1),
        grad_query,
        grad_key,
        grad_value,
        grad_output,
        grad_ffn_gain.reshape(-1),
        grad_gate,
        grad_up,
        grad_down.astype(FULL),
    )


def solution(mesh):
    seq_size, fsdp_size = mesh.shape["seq"], mesh.shape["fsdp"]
    split = Mesh(mesh.devices.reshape(seq_size, fsdp_size // 2, 2), ("seq", "chip", "core"))
    rows, vector, matrix = P(FSDP, "seq", None), P(("seq", *FSDP)), P(("seq", *FSDP), None)
    return jax.shard_map(
        functools.partial(layer, seq_size, fsdp_size),
        mesh=split,
        in_specs=(
            rows, P(FSDP, None), vector, matrix, matrix, matrix, matrix, vector, matrix, matrix, matrix, rows,
        ),
        out_specs=(rows, rows, vector, matrix, matrix, matrix, matrix, vector, matrix, matrix, matrix),
        check_vma=False,
    )
```

```python
import functools
import math

import jax
import jax.numpy as jnp
from jax import lax
from jax.experimental import pallas as pl
from jax.experimental.pallas import tpu as pltpu
from jax.sharding import Mesh
from jax.sharding import PartitionSpec as P

HEADS = 32
KV_HEADS = 4
HEAD_DIM = 64
HALF = HEAD_DIM // 2
GROUP = HEADS // KV_HEADS
EPSILON = 1e-05
SCALE = 1.0 / math.sqrt(HEAD_DIM)
FSDP = ("chip", "core")
LOW = jnp.bfloat16
FULL = jnp.float32
VMEM = pl.BlockSpec(memory_space=pltpu.VMEM)
ANY = pl.BlockSpec(memory_space=pltpu.HBM)
SMEM = pl.BlockSpec(memory_space=pltpu.SMEM)
PARAMS = pltpu.CompilerParams(vmem_limit_bytes=60 << 20)
NN, NT, TN = ((1,), (0,)), ((1,), (1,)), ((0,), (0,))


def dot(a, b, dims=NN):
    return lax.dot_general(a, b, (dims, ((), ())), preferred_element_type=FULL)


def like(shape, dtype=LOW):
    return jax.ShapeDtypeStruct(shape, dtype)


def rope_tables(where_at):
    frequency = 1.0 / 10000.0 ** (jnp.arange(HALF, dtype=FULL) * 2.0 / HEAD_DIM)
    angles = frequency[:, None] * where_at.astype(FULL)[None, :]
    return jnp.cos(angles), jnp.sin(angles)


def regroup(x, outer, inner, rows):
    return jnp.concatenate(
        [x[:, (o * inner + i) * rows:(o * inner + i + 1) * rows] for i in range(inner) for o in range(outer)], 1
    )


def join(pieces, whole_ref):
    at = 0
    for piece in pieces:
        whole_ref[at:at + piece.shape[0], :] = piece[...]
        at += piece.shape[0]


def fetch(pieces, whole_ref, sems):
    copies, at = [], 0
    for i, piece in enumerate(pieces):
        rows = piece.shape[0]
        copies.append(pltpu.make_async_copy(piece, whole_ref.at[pl.ds(at, rows)], sems.at[i]))
        at += rows
    for copy in copies:
        copy.start()
    for copy in copies:
        copy.wait()


def arrivals(count):
    return pltpu.SemaphoreType.DMA((count,))


def call_own(kernel, out_shape, *args, scalars=()):
    return pl.pallas_call(
        kernel, out_shape=out_shape, in_specs=[SMEM] * len(scalars) + [VMEM] * len(args),
        out_specs=jax.tree.map(lambda _: VMEM, out_shape), compiler_params=PARAMS,
        name=getattr(kernel, "func", kernel).__name__,
    )(*scalars, *args)


def added(refs):
    total = refs[0][...].astype(FULL)
    for ref in refs[1:]:
        total = total + ref[...].astype(FULL)
    return total


def regroup_kernel(grid, x_ref, *out_refs):
    x = regroup(x_ref[...].astype(FULL), *grid).astype(LOW)
    rows = out_refs[0].shape[0]
    for i, ref in enumerate(out_refs):
        ref[...] = x[i * rows:(i + 1) * rows]


def middle_kernel(grid, parts, *refs):
    tokens_ref, refs = refs[0], refs[1:]
    per = (len(refs) - 2 - parts) // parts
    middle_ref, inv_ref, *normed_refs = refs[per * parts:]
    rows = normed_refs[0].shape[0]
    for i in range(parts):
        at = slice(i * rows, (i + 1) * rows)
        middle = tokens_ref[at, :].astype(FULL) + added(refs[i * per:(i + 1) * per])
        inv = lax.rsqrt(jnp.mean(middle * middle, -1, keepdims=True) + EPSILON)
        middle_ref[at, :] = middle
        inv_ref[at, :] = inv
        normed_refs[i][...] = regroup(middle * inv, *grid).astype(LOW)


def grad_middle_kernel(grid, parts, *refs):
    upstream_ref, middle_ref, inv_ref, refs = refs[0], refs[1], refs[2], refs[3:]
    out_ref, *low_refs = refs[-1 - parts:]
    per = (len(refs) - 1 - parts) // parts
    rows = low_refs[0].shape[0]
    for i in range(parts):
        at = slice(i * rows, (i + 1) * rows)
        inv = inv_ref[at, :]
        normed = middle_ref[at, :] * inv
        grad = regroup(added(refs[i * per:(i + 1) * per]), *grid)
        grad = upstream_ref[at, :].astype(FULL) + inv * (grad - normed * jnp.mean(grad * normed, -1, keepdims=True))
        out_ref[at, :] = grad
        low_refs[i][...] = grad.astype(LOW)


def grad_tokens_kernel(grid, parts, *refs):
    tokens_ref, grad_ref, refs, out_ref = refs[0], refs[1], refs[2:-1], refs[-1]
    per = len(refs) // parts
    rows = out_ref.shape[0] // parts
    for i in range(parts):
        at = slice(i * rows, (i + 1) * rows)
        tokens = tokens_ref[at, :].astype(FULL)
        normed = tokens * lax.rsqrt(jnp.mean(tokens * tokens, -1, keepdims=True) + EPSILON)
        grad = regroup(added(refs[i * per:(i + 1) * per]), *grid)
        out_ref[at, :] = grad_ref[at, :] + grad - normed * jnp.mean(grad * normed, -1, keepdims=True)


def block_out_kernel(parts, *refs):
    middle_ref, refs, out_ref = refs[0], refs[1:-1], refs[-1]
    per, rows = len(refs) // parts, out_ref.shape[0] // parts
    for i in range(parts):
        at = slice(i * rows, (i + 1) * rows)
        out_ref[at, :] = (middle_ref[at, :] + added(refs[i * per:(i + 1) * per])).astype(LOW)


def as_row(column):
    return jnp.broadcast_to(column, (column.shape[0], 128)).T[:1]


def finish_gate_up_kernel(here_ref, *refs):
    *pieces, gate_ref, up_ref, gain_ref, grad_gate_ref, grad_up_ref, grad_gain_ref = refs
    gain, total = gain_ref[...], 0.0
    across, chunk = gate_ref.shape[1] // len(pieces), 128
    for j, piece in enumerate(pieces):
        first = (here_ref[0] ^ j) * across
        for c in range(across // chunk):
            there = pl.ds(pl.multiple_of(first + c * chunk, chunk), chunk)
            for i, (weight_ref, out_ref) in enumerate(((gate_ref, grad_gate_ref), (up_ref, grad_up_ref))):
                grad = piece[:, (2 * c + i) * chunk:(2 * c + i + 1) * chunk].astype(FULL)
                out_ref[:, there] = grad * gain
                total = total + grad * weight_ref[:, there].astype(FULL)
    grad_gain_ref[...] = as_row(jnp.sum(total, 1, keepdims=True))


def finish_projections_kernel(here_ref, *refs):
    *pieces, own_ref, query_ref, key_ref, value_ref, gain_ref = refs[:-5]
    grad_query_ref, grad_key_ref, grad_value_ref, grad_output_ref, grad_gain_ref = refs[-5:]
    gain, count = gain_ref[...], len(pieces)
    rows = gain.shape[0]
    qw, kw = query_ref.shape[1] // count, key_ref.shape[1] // count
    total = 0.0
    for j, piece in enumerate(pieces):
        there = pl.ds(pl.multiple_of((here_ref[0] ^ j) * qw, qw), qw)
        grad = piece[:, :qw].astype(FULL)
        grad_query_ref[:, there] = grad * gain
        total = total + jnp.sum(grad * query_ref[:, there].astype(FULL), 1, keepdims=True)
    for first, weight_ref, out_ref in ((qw, key_ref, grad_key_ref), (qw + kw, value_ref, grad_value_ref)):
        grad = [jnp.zeros((rows, kw), FULL)] * count
        for j, piece in enumerate(pieces):
            mine = piece[:, first:first + kw].astype(FULL)
            for t in range(count):
                grad[t] = jnp.where(here_ref[0] == t ^ j, mine, grad[t])
        grad = jnp.concatenate(grad, 1)
        out_ref[...] = grad * gain
        total = total + jnp.sum(grad * weight_ref[...].astype(FULL), 1, keepdims=True)
    across = grad_output_ref.shape[1] // count
    for part in range(count):
        grad_output_ref[:, part * across:(part + 1) * across] = own_ref[part * rows:(part + 1) * rows, :across].astype(FULL)
    grad_gain_ref[...] = as_row(total)


def rows_of(pieces):
    return sum(p.shape[0] for p in pieces)


def whole(shape):
    return pl.BlockSpec(shape, lambda i: (0,) * len(shape))


def columns(rows, width):
    return pl.BlockSpec((rows, width), lambda i: (0, i))


def by_rows(height, width):
    return pl.BlockSpec((height, width), lambda i: (i, 0))


def hidden_kernel(count, chunk, *refs):
    pieces, refs = refs[:count], refs[count:]
    weight_ref, slope_ref, hidden_ref, out_ref, normed_ref, sems, out_sem = refs
    step = pl.program_id(0)
    out_copy = pltpu.make_async_copy(normed_ref, out_ref, out_sem)

    @pl.when(step == 0)
    def _():
        fetch(pieces, normed_ref, sems)
        out_copy.start()

    both = dot(normed_ref[...], weight_ref[...])
    gate, up = both[:, :chunk], both[:, chunk:]
    sigmoid = jax.nn.sigmoid(gate)
    silu = gate * sigmoid
    slope = up * sigmoid * (1.0 + gate * (1.0 - sigmoid))
    slope_ref[...] = jnp.concatenate([slope, silu], 1).astype(LOW)
    hidden_ref[...] = (silu * up).T.astype(LOW)

    @pl.when(step == pl.num_programs(0) - 1)
    def _():
        out_copy.wait()


def hidden_of(pieces, weight, chunk):
    tokens, (width, both) = rows_of(pieces), weight.shape
    return pl.pallas_call(
        functools.partial(hidden_kernel, len(pieces), chunk),
        grid=(both // (2 * chunk),),
        in_specs=[ANY] * len(pieces) + [columns(width, 2 * chunk)],
        out_specs=(columns(tokens, 2 * chunk), by_rows(chunk, tokens), ANY),
        out_shape=(like((tokens, both)), like((both // 2, tokens)), like((tokens, width))),
        scratch_shapes=[pltpu.VMEM((tokens, width), LOW), arrivals(len(pieces)), pltpu.SemaphoreType.DMA],
        compiler_params=PARAMS,
        name="hidden_of",
    )(*pieces, weight)


def grad_down_kernel(count, *refs):
    pieces, (hidden_ref, out_ref, block_ref) = refs[:count], refs[count:]
    join(pieces, block_ref)
    out_ref[...] = dot(hidden_ref[...], block_ref[...]).astype(LOW)


def grad_down_of(hidden, pieces, block=256):
    tokens, width = rows_of(pieces), pieces[0].shape[1]
    return pl.pallas_call(
        functools.partial(grad_down_kernel, len(pieces)),
        grid=(width // block,),
        in_specs=[columns(p.shape[0], block) for p in pieces] + [whole(hidden.shape)],
        out_specs=columns(hidden.shape[0], block),
        out_shape=like((hidden.shape[0], width)),
        scratch_shapes=[pltpu.VMEM((tokens, block), LOW)],
        compiler_params=PARAMS,
        name="grad_down_of",
    )(*pieces, hidden)


def grad_gate_up_kernel(count, chunk, odd, *refs):
    pieces, (down_ref, slope_ref, out_ref, upstream_ref, sems) = refs[:count], refs[count:]
    step, steps = pl.program_id(0), pl.num_programs(0)

    @pl.when(step == 0)
    def _():
        fetch(pieces, upstream_ref, sems)

    def work(chunks):
        grad = dot(upstream_ref[...], down_ref[:chunks * chunk, :], NT)
        each = [grad[:, c * chunk:(c + 1) * chunk] for c in range(chunks) for _ in range(2)]
        width = chunks * 2 * chunk
        out_ref[:, :width] = (jnp.concatenate(each, 1) * slope_ref[:, :width].astype(FULL)).astype(LOW)

    @pl.when(step < steps - odd)
    def _():
        work(2)

    if odd:

        @pl.when(step == steps - 1)
        def _():
            work(1)


def grad_gate_up_of(pieces, down, slope, chunk):
    (tokens, width), depth = (rows_of(pieces), pieces[0].shape[1]), down.shape[0]
    return pl.pallas_call(
        functools.partial(grad_gate_up_kernel, len(pieces), chunk, depth // chunk % 2),
        grid=(pl.cdiv(depth, 2 * chunk),),
        in_specs=[ANY] * len(pieces) + [by_rows(2 * chunk, width), columns(tokens, 4 * chunk)],
        out_specs=columns(tokens, 4 * chunk),
        out_shape=like(slope.shape),
        scratch_shapes=[pltpu.VMEM((tokens, width), LOW), arrivals(len(pieces))],
        compiler_params=PARAMS,
        name="grad_gate_up_of",
    )(*pieces, down, slope)


def grad_rows_kernel(first, grad_ref, weight_ref, *out_refs):
    grad = dot(grad_ref[...], weight_ref[:, first:], NT).astype(LOW)
    rows = out_refs[0].shape[0]
    for i, ref in enumerate(out_refs):
        ref[...] = grad[i * rows:(i + 1) * rows]


def grad_rows_of(grad, weight, piece_rows, block=512):
    tokens, width = grad.shape[0], weight.shape[0]
    count = tokens // piece_rows
    return pl.pallas_call(
        functools.partial(grad_rows_kernel, weight.shape[1] - grad.shape[1]),
        grid=(width // block,),
        in_specs=[whole(grad.shape), by_rows(block, weight.shape[1])],
        out_specs=(columns(piece_rows, block),) * count,
        out_shape=(like((piece_rows, width)),) * count,
        compiler_params=PARAMS,
        name="grad_rows_of",
    )(grad, weight)


def grad_weight_kernel(core_ref, left_ref, other_left_ref, grad_ref, other_grad_ref, out_ref):
    got = dot(left_ref[...], grad_ref[...], TN) + dot(other_left_ref[...], other_grad_ref[...], TN)
    out_ref[...] = got.astype(LOW)


def grad_weight_of(left, other_left, grad, other_grad, core, chips):
    tokens, width = left.shape
    block = width // chips // 2
    mine = pl.BlockSpec((tokens, block), lambda i, core_ref: (0, i * 2 + core_ref[0]))
    every = pl.BlockSpec(grad.shape, lambda i, core_ref: (0, 0))
    return pl.pallas_call(
        grad_weight_kernel,
        grid_spec=pltpu.PrefetchScalarGridSpec(
            num_scalar_prefetch=1,
            grid=(chips,),
            in_specs=[mine, mine, every, every],
            out_specs=pl.BlockSpec((block, grad.shape[1]), lambda i, core_ref: (i, 0)),
        ),
        out_shape=like((width // 2, grad.shape[1])),
        compiler_params=PARAMS,
        name="grad_weight_of",
    )(core, left, other_left, grad, other_grad)


def rows_kernel(left_ref, weight_ref, *refs):
    *out_refs, turned_ref = refs

    @pl.when(pl.program_id(0) == 0)
    def _():
        turned_ref[...] = left_ref[...].T

    weight = weight_ref[...].reshape(turned_ref.shape[1], weight_ref.shape[-1])
    out = dot(turned_ref[...], weight).astype(LOW)
    rows = out_refs[0].shape[0]
    for i, ref in enumerate(out_refs):
        ref[...] = out[i * rows:(i + 1) * rows]


def rows_of_product(left, weight, piece_rows, inner=None, block=512):
    depth, tokens = left.shape
    count = tokens // piece_rows
    if inner is None:
        width, spec = weight.shape[1], columns(depth, block)
    else:
        seq_size, fsdp_size, own_rows = inner
        width = weight.shape[0]
        block = min(block, width // seq_size)
        per = width // seq_size // block
        weight = weight.reshape(fsdp_size, seq_size, own_rows, -1)
        spec = pl.BlockSpec((fsdp_size, 1, own_rows, block), lambda i: (0, i // per, 0, i % per))
    return pl.pallas_call(
        rows_kernel,
        grid=(width // block,),
        in_specs=[whole(left.shape), spec],
        out_specs=(columns(piece_rows, block),) * count,
        out_shape=(like((piece_rows, width)),) * count,
        scratch_shapes=[pltpu.VMEM((tokens, depth), LOW)],
        compiler_params=PARAMS,
        name="rows_of_product",
    )(left, weight)


def attention_weights_kernel(count, inner, *refs):
    tokens, grads = refs[:count], refs[count:2 * count]
    grad_qkv_ref, attended_ref, out_ref, block_ref = refs[2 * count:]
    seq_size, fsdp_size, own_rows = inner
    step, block = pl.program_id(0), block_ref.shape[1]
    across = out_ref.shape[1] - grad_qkv_ref.shape[0]
    join(tokens, block_ref)
    there = pl.ds(pl.multiple_of(step * block, block), block)
    out_ref[there, across:] = dot(grad_qkv_ref[...], block_ref[...]).T.astype(LOW)
    join(grads, block_ref)
    got = dot(attended_ref[...], block_ref[...]).astype(LOW)
    part = step * block // across
    first = step * block % across
    for f in range(fsdp_size):
        rows = pl.ds(pl.multiple_of((f * seq_size + part) * own_rows, own_rows), own_rows)
        out_ref[rows, pl.ds(pl.multiple_of(first, 128), block)] = got[f * own_rows:(f + 1) * own_rows]


def attention_weights_of(tokens, grads, grad_qkv, attended, inner, block=512):
    count, width = len(tokens), tokens[0].shape[1]
    block = min(block, width // inner[0])
    shape = (width, grad_qkv.shape[0] + width // inner[0])
    return pl.pallas_call(
        functools.partial(attention_weights_kernel, count, inner),
        grid=(width // block,),
        in_specs=[columns(p.shape[0], block) for p in (*tokens, *grads)]
        + [whole(grad_qkv.shape), whole(attended.shape)],
        out_specs=whole(shape),
        out_shape=like(shape),
        scratch_shapes=[pltpu.VMEM((rows_of(tokens), block), LOW)],
        compiler_params=PARAMS,
        name="attention_weights_of",
    )(*tokens, *grads, grad_qkv, attended)


def attend_kernel(heads, kvs, span, pieces, order_ref, rank_ref, *refs):
    token_refs, refs = refs[:pieces], refs[pieces:]
    weight_ref, cos_ref, sin_ref, qrot_ref, kv_ref, att_ref, mix_ref, lse_ref, inv_ref, *scratch = refs
    keys_ref, qkv_ref, tokens_ref, sems = scratch
    fetch(token_refs, tokens_ref, sems)
    count = cos_ref.shape[1] // span
    for at in range(0, tokens_ref.shape[0], span):
        there = slice(at, at + span)
        values = tokens_ref[there, :].astype(FULL)
        inv = lax.rsqrt(jnp.mean(values * values, -1, keepdims=True) + EPSILON)
        qkv_ref[:, there] = (dot(tokens_ref[there, :], weight_ref[:, -qkv_ref.shape[0]:]) * inv).T
        inv_ref[:, there] = jnp.broadcast_to(inv, (span, 128)).T[:1]
    qw, kw = heads * HEAD_DIM, kvs * HEAD_DIM
    cosine, sine = cos_ref[...], sin_ref[...]

    def rotated(row):
        one, two = qkv_ref[row:row + HALF, :], qkv_ref[row + HALF:row + HEAD_DIM, :]
        return jnp.concatenate([one * cosine - two * sine, two * cosine + one * sine], 0)

    for h in range(heads):
        qrot_ref[h * HEAD_DIM:(h + 1) * HEAD_DIM, :] = rotated(h * HEAD_DIM).astype(LOW)
    for k in range(kvs):
        turned = rotated(qw + k * HEAD_DIM).astype(LOW)
        kv_ref[k * HEAD_DIM:(k + 1) * HEAD_DIM, :] = turned
        keys_ref[k] = (turned.astype(FULL) * SCALE).T.astype(LOW)
    kv_ref[kw:, :] = qkv_ref[qw + kw:, :].astype(LOW)

    def one_block(qb, _):
        cols = pl.ds(pl.multiple_of(qb * span, span), span)
        rank = rank_ref[qb]

        def step(at, state, diagonal):
            rows = pl.ds(pl.multiple_of(order_ref[at] * span, span), span)
            out = []
            for h in range(heads):
                top, total, mixed = state[h]
                k = h * kvs // heads
                scores = dot(keys_ref[k, rows, :], qrot_ref[h * HEAD_DIM:(h + 1) * HEAD_DIM, cols])
                if diagonal:
                    key_at = lax.broadcasted_iota(jnp.int32, (span, span), 0)
                    query_at = lax.broadcasted_iota(jnp.int32, (span, span), 1)
                    scores = jnp.where(key_at <= query_at, scores, -1e30)
                new_top = jnp.maximum(top, jnp.max(scores, 0, keepdims=True))
                weights = jnp.exp(scores - new_top)
                fade = jnp.exp(top - new_top)
                total = total * fade + jnp.sum(weights, 0, keepdims=True)
                values = kv_ref[kw + k * HEAD_DIM:kw + (k + 1) * HEAD_DIM, rows]
                mixed = mixed * fade + dot(values, weights.astype(LOW))
                out.append((new_top, total, mixed))
            return out

        start = [(jnp.full((1, span), -1e30, FULL), jnp.zeros((1, span), FULL),
                  jnp.zeros((HEAD_DIM, span), FULL)) for _ in range(heads)]
        state = lax.fori_loop(0, rank, lambda at, st: step(at, st, False), start)
        state = step(rank, state, True)
        for h in range(heads):
            top, total, mixed = state[h]
            mixed = mixed / total
            mix_ref[h * HEAD_DIM:(h + 1) * HEAD_DIM, cols] = mixed
            att_ref[h * HEAD_DIM:(h + 1) * HEAD_DIM, cols] = mixed.astype(LOW)
            lse_ref[h:h + 1, cols] = top + jnp.log(total)
        return 0

    lax.fori_loop(0, count, one_block, 0)


def attend(order, rank, pieces, weight, cosine, sine, heads, kvs, span):
    tokens = cosine.shape[1]
    qw, kw = heads * HEAD_DIM, kvs * HEAD_DIM
    return pl.pallas_call(
        functools.partial(attend_kernel, heads, kvs, span, len(pieces)),
        out_shape=(
            like((qw, tokens)), like((2 * kw, tokens)), like((qw, tokens)), like((qw, tokens), FULL),
            like((heads, tokens), FULL), like((1, tokens), FULL),
        ),
        in_specs=[SMEM, SMEM] + [ANY] * len(pieces) + [VMEM] * 3,
        out_specs=(VMEM,) * 6,
        scratch_shapes=[
            pltpu.VMEM((kvs, tokens, HEAD_DIM), LOW),
            pltpu.VMEM((qw + 2 * kw, tokens), FULL),
            pltpu.VMEM((tokens, weight.shape[0]), LOW),
            arrivals(len(pieces)),
        ],
        compiler_params=PARAMS,
        name="attend",
    )(order, rank, *pieces, weight, cosine, sine)


def attend_back_kernel(heads, kvs, span, pieces, order_ref, rank_ref, *refs):
    branch_refs, refs = refs[:pieces], refs[pieces:]
    output_ref, qrot_ref, kv_ref, mix_ref, lse_ref, cos_ref, sin_ref, inv_ref, out_ref, turned_ref, *scratch = refs
    keys_ref, values_ref, delta_ref, dkv_ref, grad_ref, branch_ref, sems = scratch
    count = cos_ref.shape[1] // span
    qw, kw = heads * HEAD_DIM, kvs * HEAD_DIM
    fetch(branch_refs, branch_ref, sems)
    seq_size, across = output_ref.shape[1], branch_ref.shape[1] // output_ref.shape[1]
    for at in range(0, branch_ref.shape[0], span):
        total = 0.0
        for part in range(seq_size):
            weight = output_ref[:, part, :, :across].reshape(qw, across)
            total = total + dot(weight, branch_ref[at:at + span, part * across:(part + 1) * across], NT)
        grad_ref[:, at:at + span] = total.astype(LOW)
    qw, kw = heads * HEAD_DIM, kvs * HEAD_DIM
    for k in range(kvs):
        keys_ref[k] = (kv_ref[k * HEAD_DIM:(k + 1) * HEAD_DIM, :].astype(FULL) * SCALE).T.astype(LOW)
        values_ref[k] = kv_ref[kw + k * HEAD_DIM:kw + (k + 1) * HEAD_DIM, :].astype(FULL).T.astype(LOW)
    for h in range(heads):
        rows = slice(h * HEAD_DIM, (h + 1) * HEAD_DIM)
        delta_ref[h:h + 1, :] = jnp.sum(grad_ref[rows, :].astype(FULL) * mix_ref[rows, :], 0, keepdims=True)
    dkv_ref[...] = jnp.zeros_like(dkv_ref)

    def one_block(qb, _):
        cols = pl.ds(pl.multiple_of(qb * span, span), span)
        rank = rank_ref[qb]

        def step(at, state, diagonal):
            rows = pl.ds(pl.multiple_of(order_ref[at] * span, span), span)
            out = []
            dkeys = [None] * kvs
            dvalues = [None] * kvs
            for h in range(heads):
                k = h * kvs // heads
                mine = slice(h * HEAD_DIM, (h + 1) * HEAD_DIM)
                query = qrot_ref[mine, cols]
                grad = grad_ref[mine, cols]
                scores = dot(keys_ref[k, rows, :], query)
                weights = jnp.exp(scores - lse_ref[h:h + 1, cols])
                if diagonal:
                    key_at = lax.broadcasted_iota(jnp.int32, (span, span), 0)
                    query_at = lax.broadcasted_iota(jnp.int32, (span, span), 1)
                    weights = jnp.where(key_at <= query_at, weights, 0.0)
                grad_probs = dot(values_ref[k, rows, :], grad)
                grad_scores = (weights * (grad_probs - delta_ref[h:h + 1, cols])).astype(LOW)
                key_t = kv_ref[k * HEAD_DIM:(k + 1) * HEAD_DIM, rows]
                out.append(state[h] + dot(key_t, grad_scores))
                dk = dot(query, grad_scores, NT)
                dv = dot(grad, weights.astype(LOW), NT)
                dkeys[k] = dk if dkeys[k] is None else dkeys[k] + dk
                dvalues[k] = dv if dvalues[k] is None else dvalues[k] + dv
            for k in range(kvs):
                mine = slice(k * HEAD_DIM, (k + 1) * HEAD_DIM)
                dkv_ref[mine, rows] += dkeys[k]
                mine = slice(kw + k * HEAD_DIM, kw + (k + 1) * HEAD_DIM)
                dkv_ref[mine, rows] += dvalues[k]
            return out

        state = [jnp.zeros((HEAD_DIM, span), FULL) for _ in range(heads)]
        state = lax.fori_loop(0, rank, lambda at, st: step(at, st, False), state)
        state = step(rank, state, True)
        scale = inv_ref[:, cols] * SCALE
        cosine, sine = cos_ref[:, cols], sin_ref[:, cols]
        for h in range(heads):
            one, two = state[h][:HALF] * scale, state[h][HALF:] * scale
            out_ref[h * HEAD_DIM:h * HEAD_DIM + HALF, cols] = (one * cosine + two * sine).astype(LOW)
            out_ref[h * HEAD_DIM + HALF:(h + 1) * HEAD_DIM, cols] = (two * cosine - one * sine).astype(LOW)
        return 0

    lax.fori_loop(0, count, one_block, 0)
    cosine, sine = cos_ref[...], sin_ref[...]
    scale = inv_ref[...] * SCALE
    for k in range(kvs):
        top = k * HEAD_DIM
        one, two = dkv_ref[top:top + HALF, :] * scale, dkv_ref[top + HALF:top + HEAD_DIM, :] * scale
        out_ref[qw + top:qw + top + HALF, :] = (one * cosine + two * sine).astype(LOW)
        out_ref[qw + top + HALF:qw + top + HEAD_DIM, :] = (two * cosine - one * sine).astype(LOW)
    out_ref[qw + kw:, :] = (dkv_ref[kw:, :] * inv_ref[...]).astype(LOW)
    turned_ref[...] = out_ref[...].T


def attend_back(order, rank, pieces, output, qrot, kv, mix, lse, cosine, sine, inv, heads, kvs, span):
    tokens = cosine.shape[1]
    qw, kw = heads * HEAD_DIM, kvs * HEAD_DIM
    return pl.pallas_call(
        functools.partial(attend_back_kernel, heads, kvs, span, len(pieces)),
        out_shape=(like((qw + 2 * kw, tokens)), like((tokens, qw + 2 * kw))),
        in_specs=[SMEM, SMEM] + [ANY] * len(pieces) + [VMEM] * 8,
        out_specs=(VMEM, VMEM),
        scratch_shapes=[
            pltpu.VMEM((kvs, tokens, HEAD_DIM), LOW),
            pltpu.VMEM((kvs, tokens, HEAD_DIM), LOW),
            pltpu.VMEM((heads, tokens), FULL),
            pltpu.VMEM((2 * kw, tokens), FULL),
            pltpu.VMEM((qw, tokens), LOW),
            pltpu.VMEM((tokens, pieces[0].shape[1]), LOW),
            arrivals(len(pieces)),
        ],
        compiler_params=PARAMS,
        name="attend_back",
    )(order, rank, *pieces, output, qrot, kv, mix, lse, cosine, sine, inv)


def layer(seq_size, fsdp_size, tokens, positions, attn_gain, query_weight, key_weight, value_weight, output_weight,
          ffn_gain, gate_weight, up_weight, down_weight, cotangent):
    span, width = tokens.shape[1:]
    heads = HEADS // seq_size
    kvs = max(1, KV_HEADS // seq_size)
    shared = max(1, seq_size // KV_HEADS)
    qw, kw = heads * HEAD_DIM, kvs * HEAD_DIM
    own_rows = query_weight.shape[0]
    hidden_own = gate_weight.shape[1] // seq_size
    chunk = 128 if hidden_own % 128 == 0 else 64
    parts = 2 if seq_size == 4 else 1
    piece_rows = span // parts
    into, back = (seq_size, fsdp_size, own_rows), (fsdp_size, seq_size, own_rows)
    here = lax.axis_index("seq")

    def after(x, *others):
        return lax.optimization_barrier((x, *others))[0]

    def swap(x, j):
        return lax.ppermute(x, "seq", [(i, i ^ j) for i in range(seq_size)])

    def seq_gather(own):
        if parts == 1:
            return [own[0]] + [swap(own[0], j) for j in range(1, seq_size)]
        a, b = own
        ax, by = swap(a, 1), swap(b, 2)
        ay, bx = swap(a, 2), swap(b, 1)
        ad, bd = swap(ax, 2), swap(by, 1)
        return [a, b, ax, bx, ay, by, ad, bd]

    def scatter_start(pieces):
        if parts == 1:
            return [swap(pieces[j], j) for j in range(1, seq_size)]
        a, b = pieces[::2], pieces[1::2]
        return [swap(a[3], 2), swap(b[3], 1), swap(a[2], 2), swap(b[1], 1)]

    def scatter_end(pieces, came):
        if parts == 1:
            return (), [pieces[0], *came]
        a, b, (da, db, ya, xb) = pieces[::2], pieces[1::2], came
        da = (a[1].astype(FULL) + da.astype(FULL)).astype(LOW)
        db = (b[2].astype(FULL) + db.astype(FULL)).astype(LOW)
        return (da, db), [a[0], ya, swap(da, 1), b[0], xb, swap(db, 2)]

    def seq_scatter(pieces):
        return scatter_end(pieces, scatter_start(pieces))

    def spread(pieces_for):
        got = [pieces_for(here)] + [swap(pieces_for(here ^ j), j) for j in range(1, seq_size)]
        stack = jnp.stack(got)
        return jnp.concatenate(
            [lax.dynamic_index_in_dim(stack, here ^ t, 0, False) for t in range(seq_size)], 0
        )

    def collect(x):
        blocks = x.reshape(seq_size, own_rows, x.shape[1])
        return [lax.dynamic_index_in_dim(blocks, here, 0, False)] + [
            swap(lax.dynamic_index_in_dim(blocks, here ^ j, 0, False), j) for j in range(1, seq_size)
        ]

    def in_order(got):
        got = jnp.stack(got)
        return jnp.stack([lax.dynamic_index_in_dim(got, here ^ t, 0, False) for t in range(seq_size)]).astype(FULL)

    def fsdp_gather(x):
        return lax.all_gather(x, FSDP, axis=0, tiled=True)

    def exchange(x):
        return lax.ppermute(x, "core", [(0, 1), (1, 0)])

    def chip_scatter(x):
        return lax.psum_scatter(x.reshape(-1, x.shape[-1]), "chip", scatter_dimension=0, tiled=True)

    def fsdp_scatter(x):
        return lax.psum_scatter(x, FSDP, scatter_dimension=0, tiled=True)

    gain_one, gain_two = attn_gain.astype(FULL)[:, None], ffn_gain.astype(FULL)[:, None]

    def with_gain(weight, gain):
        return (weight.astype(FULL) * gain).astype(LOW)

    query_low, key_low, value_low = (with_gain(w, gain_one) for w in (query_weight, key_weight, value_weight))

    def qkv_for(t):
        first = (t * heads // GROUP) * HEAD_DIM
        return jnp.concatenate([
            lax.dynamic_slice_in_dim(query_low, t * qw, qw, 1),
            lax.dynamic_slice_in_dim(key_low, first, kw, 1),
            lax.dynamic_slice_in_dim(value_low, first, kw, 1),
        ], 1)

    count = positions.shape[1] // span
    where_at = positions[0].reshape(count, span)
    where_at = jnp.stack([lax.dynamic_index_in_dim(where_at, here ^ j, 0, False) for j in range(count)])
    rank = where_at[:, 0] // span
    order = jnp.argsort(rank).astype(jnp.int32)
    cosine, sine = rope_tables(where_at.reshape(-1))

    own_tokens = tokens[0]
    own_pieces = call_own(
        functools.partial(regroup_kernel, into), (like((piece_rows, width)),) * parts, own_tokens
    )
    token_pieces = seq_gather(own_pieces)
    output_own = output_weight.reshape(own_rows, seq_size, -1).swapaxes(0, 1).reshape(seq_size * own_rows, -1)
    projections = fsdp_gather(jnp.concatenate([output_own, spread(qkv_for)], 1))
    gate_weight, up_weight = lax.optimization_barrier((gate_weight, up_weight, *own_pieces, order, cosine, sine))[:2]
    gate_low, up_low = with_gain(gate_weight, gain_two), with_gain(up_weight, gain_two)

    def gate_up_for(t):
        gate = lax.dynamic_slice_in_dim(gate_low, t * hidden_own, hidden_own, 1)
        up = lax.dynamic_slice_in_dim(up_low, t * hidden_own, hidden_own, 1)
        return jnp.concatenate(
            [x[:, c:c + chunk] for c in range(0, hidden_own, chunk) for x in (gate, up)], 1
        )

    gate_up_own = spread(gate_up_for)
    gate_up_full = fsdp_gather(gate_up_own)
    down_full = fsdp_gather(down_weight)
    own_upstream = after(cotangent[0], gate_up_own, *token_pieces)
    upstream = [own_upstream] + [swap(own_upstream, j) for j in range(1, seq_size)]

    qrot, kv, attended, mix, lse, inv_one = attend(
        order, rank, token_pieces, projections, cosine, sine, heads, kvs, span
    )
    branch = rows_of_product(attended, projections, piece_rows, into)
    branch, upstream = lax.optimization_barrier((branch, upstream))
    branch = seq_scatter(branch)[1]
    middle, inv_two, *own_pieces = call_own(
        functools.partial(middle_kernel, into, parts),
        (like((span, width), FULL), like((span, 1), FULL)) + (like((piece_rows, width)),) * parts,
        own_tokens, *branch,
    )

    normed_pieces = seq_gather(own_pieces)
    slope, hidden, normed = hidden_of(normed_pieces, gate_up_full, chunk)
    part_down = grad_down_of(hidden, upstream)
    grad_down = fsdp_scatter(part_down)
    grad_gate_up = grad_gate_up_of([after(upstream[0], part_down), *upstream[1:]], down_full, slope, chunk)
    first, grad_pieces = seq_scatter(grad_rows_of(grad_gate_up, gate_up_full, piece_rows))
    place, core = (at.astype(jnp.int32).reshape(1) for at in (here, lax.axis_index("core")))
    part_gate_up = grad_weight_of(
        after(normed, *first), exchange(normed), grad_gate_up, exchange(grad_gate_up), core, fsdp_size // 2
    )
    part_gate_up, *grad_pieces = lax.optimization_barrier((part_gate_up, *grad_pieces))
    grad_gate_up_own = chip_scatter(part_gate_up)
    grad_pieces[0] = after(grad_pieces[0], grad_down)
    grad_middle, *own_pieces = call_own(
        functools.partial(grad_middle_kernel, back, parts),
        (like((span, width), FULL),) + (like((piece_rows, width)),) * parts,
        cotangent[0], middle, inv_two, *grad_pieces,
    )

    branch_pieces = seq_gather(own_pieces)
    out_pieces = rows_of_product(after(hidden, own_pieces[0]), down_full, piece_rows)
    out_pieces = lax.optimization_barrier((*out_pieces, *branch_pieces))[:len(out_pieces)]
    out_came = scatter_start(out_pieces)
    grad_qkv, grad_qkv_turned = attend_back(
        order, rank, branch_pieces, projections.reshape(fsdp_size, seq_size, own_rows, -1), qrot, kv, mix, lse,
        cosine, sine, inv_one, heads, kvs, span,
    )
    grad_qkv, grad_qkv_turned, *out_came = lax.optimization_barrier((grad_qkv, grad_qkv_turned, *out_came))
    part_projections = attention_weights_of(token_pieces, branch_pieces, grad_qkv, attended, into)
    grad_pieces = grad_rows_of(grad_qkv_turned, projections, piece_rows)
    first, grad_pieces = seq_scatter(grad_pieces)
    grad_projections = fsdp_scatter(after(part_projections, grad_gate_up_own, *first))
    got = collect(after(grad_gate_up_own, *grad_pieces))
    out_pieces = scatter_end(out_pieces, out_came)[1]
    block_out = call_own(functools.partial(block_out_kernel, parts), like((span, width)), middle, *out_pieces)


    def whole_rows(x):
        return x.swapaxes(0, 1).reshape(own_rows, -1)

    if chunk == 128:
        rows_like = like((own_rows, gate_weight.shape[1]), FULL)
        grad_gate, grad_up, grad_ffn_gain = call_own(
            finish_gate_up_kernel, (rows_like, rows_like, like((1, own_rows), FULL)),
            *got, gate_weight, up_weight, gain_two, scalars=(place,),
        )
    else:
        got = in_order(got).reshape(seq_size, own_rows, -1, 2, chunk)
        grad_gate, grad_up = whole_rows(got[:, :, :, 0]), whole_rows(got[:, :, :, 1])
        grad_ffn_gain = jnp.sum(grad_gate * gate_weight.astype(FULL) + grad_up * up_weight.astype(FULL), 1)
        grad_gate, grad_up = grad_gate * gain_two, grad_up * gain_two
    grad_tokens = call_own(
        functools.partial(grad_tokens_kernel, back, parts), like((span, width), FULL),
        own_tokens, grad_middle, *grad_pieces,
    )
    grad_projections = after(grad_projections, grad_tokens, block_out, grad_ffn_gain)
    got = collect(grad_projections[:, -qw - 2 * kw:])
    if shared == 1 and kvs == 1:
        grad_query, grad_key, grad_value, grad_output, grad_attn_gain = call_own(
            finish_projections_kernel,
            tuple(like(w.shape, FULL) for w in (query_weight, key_weight, value_weight, output_weight))
            + (like((1, own_rows), FULL),),
            *got, grad_projections, query_weight, key_weight, value_weight, gain_one, scalars=(place,),
        )
    else:
        grad_output = grad_projections[:, :-qw - 2 * kw].reshape(seq_size, own_rows, -1).swapaxes(0, 1)
        grad_output = grad_output.reshape(own_rows, width).astype(FULL)
        got = in_order(got)
        grad_query = whole_rows(got[:, :, :qw])

        def of_heads(x):
            return whole_rows(x.reshape(seq_size // shared, shared, own_rows, kw).sum(1))

        grad_key, grad_value = of_heads(got[:, :, qw:qw + kw]), of_heads(got[:, :, qw + kw:])
        grads = (grad_query, grad_key, grad_value)
        grad_attn_gain = sum(
            jnp.sum(g * w.astype(FULL), 1) for g, w in zip(grads, (query_weight, key_weight, value_weight))
        )
        grad_query, grad_key, grad_value = (g * gain_one for g in grads)
    return (
        block_out[None],
        grad_tokens[None],
        grad_attn_gain.reshape(-1),
        grad_query,
        grad_key,
        grad_value,
        grad_output,
        grad_ffn_gain.reshape(-1),
        grad_gate,
        grad_up,
        grad_down.astype(FULL),
    )


def solution(mesh):
    seq_size, fsdp_size = mesh.shape["seq"], mesh.shape["fsdp"]
    split = Mesh(mesh.devices.reshape(seq_size, fsdp_size // 2, 2), ("seq", "chip", "core"))
    rows, vector, matrix = P(FSDP, "seq", None), P(("seq", *FSDP)), P(("seq", *FSDP), None)
    return jax.shard_map(
        functools.partial(layer, seq_size, fsdp_size),
        mesh=split,
        in_specs=(
            rows, P(FSDP, None), vector, matrix, matrix, matrix, matrix, vector, matrix, matrix, matrix, rows,
        ),
        out_specs=(rows, rows, vector, matrix, matrix, matrix, matrix, vector, matrix, matrix, matrix),
        check_vma=False,
    )
```

```python
import functools
import math

import jax
import jax.numpy as jnp
from jax import lax
from jax.experimental import pallas as pl
from jax.experimental.pallas import tpu as pltpu
from jax.sharding import Mesh
from jax.sharding import PartitionSpec as P

HEADS = 32
KV_HEADS = 4
HEAD_DIM = 64
HALF = HEAD_DIM // 2
GROUP = HEADS // KV_HEADS
EPSILON = 1e-05
SCALE = 1.0 / math.sqrt(HEAD_DIM)
FSDP = ("chip", "core")
LOW = jnp.bfloat16
FULL = jnp.float32
VMEM = pl.BlockSpec(memory_space=pltpu.VMEM)
ANY = pl.BlockSpec(memory_space=pltpu.HBM)
SMEM = pl.BlockSpec(memory_space=pltpu.SMEM)
PARAMS = pltpu.CompilerParams(vmem_limit_bytes=60 << 20)
SMALL = pltpu.CompilerParams(vmem_limit_bytes=20 << 20)
NN, NT, TN = ((1,), (0,)), ((1,), (1,)), ((0,), (0,))


def dot(a, b, dims=NN):
    return lax.dot_general(a, b, (dims, ((), ())), preferred_element_type=FULL)


def like(shape, dtype=LOW):
    return jax.ShapeDtypeStruct(shape, dtype)


def rope_tables(where_at):
    frequency = 1.0 / 10000.0 ** (jnp.arange(HALF, dtype=FULL) * 2.0 / HEAD_DIM)
    angles = frequency[:, None] * where_at.astype(FULL)[None, :]
    return jnp.cos(angles), jnp.sin(angles)


def regroup(x, outer, inner, rows):
    return jnp.concatenate(
        [x[:, (o * inner + i) * rows:(o * inner + i + 1) * rows] for i in range(inner) for o in range(outer)], 1
    )


def join(pieces, whole_ref):
    at = 0
    for piece in pieces:
        whole_ref[at:at + piece.shape[0], :] = piece[...]
        at += piece.shape[0]


def fetch(pieces, whole_ref, sems):
    copies, at = [], 0
    for i, piece in enumerate(pieces):
        rows = piece.shape[0]
        copies.append(pltpu.make_async_copy(piece, whole_ref.at[pl.ds(at, rows)], sems.at[i]))
        at += rows
    for copy in copies:
        copy.start()
    for copy in copies:
        copy.wait()


def arrivals(count):
    return pltpu.SemaphoreType.DMA((count,))


def call_own(kernel, out_shape, *args, scalars=(), params=PARAMS):
    return pl.pallas_call(
        kernel, out_shape=out_shape, in_specs=[SMEM] * len(scalars) + [VMEM] * len(args),
        out_specs=jax.tree.map(lambda _: VMEM, out_shape), compiler_params=params,
        name=getattr(kernel, "func", kernel).__name__,
    )(*scalars, *args)


def added(refs):
    total = refs[0][...].astype(FULL)
    for ref in refs[1:]:
        total = total + ref[...].astype(FULL)
    return total


def regroup_kernel(grid, x_ref, *out_refs):
    x = regroup(x_ref[...].astype(FULL), *grid).astype(LOW)
    rows = out_refs[0].shape[0]
    for i, ref in enumerate(out_refs):
        ref[...] = x[i * rows:(i + 1) * rows]


def middle_kernel(grid, parts, *refs):
    tokens_ref, refs = refs[0], refs[1:]
    per = (len(refs) - 2 - parts) // parts
    middle_ref, inv_ref, *normed_refs = refs[per * parts:]
    rows = normed_refs[0].shape[0]
    for i in range(parts):
        at = slice(i * rows, (i + 1) * rows)
        middle = tokens_ref[at, :].astype(FULL) + added(refs[i * per:(i + 1) * per])
        inv = lax.rsqrt(jnp.mean(middle * middle, -1, keepdims=True) + EPSILON)
        middle_ref[at, :] = middle
        inv_ref[at, :] = inv
        normed_refs[i][...] = regroup(middle * inv, *grid).astype(LOW)


def grad_middle_kernel(grid, parts, *refs):
    upstream_ref, middle_ref, inv_ref, refs = refs[0], refs[1], refs[2], refs[3:]
    out_ref, *low_refs = refs[-1 - parts:]
    per = (len(refs) - 1 - parts) // parts
    rows = low_refs[0].shape[0]
    for i in range(parts):
        at = slice(i * rows, (i + 1) * rows)
        inv = inv_ref[at, :]
        normed = middle_ref[at, :] * inv
        grad = regroup(added(refs[i * per:(i + 1) * per]), *grid)
        grad = upstream_ref[at, :].astype(FULL) + inv * (grad - normed * jnp.mean(grad * normed, -1, keepdims=True))
        out_ref[at, :] = grad
        low_refs[i][...] = grad.astype(LOW)


def grad_tokens_kernel(grid, parts, *refs):
    tokens_ref, grad_ref, refs, out_ref = refs[0], refs[1], refs[2:-1], refs[-1]
    per = len(refs) // parts
    rows = out_ref.shape[0] // parts
    for i in range(parts):
        at = slice(i * rows, (i + 1) * rows)
        tokens = tokens_ref[at, :].astype(FULL)
        normed = tokens * lax.rsqrt(jnp.mean(tokens * tokens, -1, keepdims=True) + EPSILON)
        grad = regroup(added(refs[i * per:(i + 1) * per]), *grid)
        out_ref[at, :] = grad_ref[at, :] + grad - normed * jnp.mean(grad * normed, -1, keepdims=True)


def block_out_kernel(parts, *refs):
    middle_ref, refs, out_ref = refs[0], refs[1:-1], refs[-1]
    per, rows = len(refs) // parts, out_ref.shape[0] // parts
    for i in range(parts):
        at = slice(i * rows, (i + 1) * rows)
        out_ref[at, :] = (middle_ref[at, :] + added(refs[i * per:(i + 1) * per])).astype(LOW)


def as_row(column):
    return jnp.broadcast_to(column, (column.shape[0], 128)).T[:1]


def finish_gate_up_kernel(here_ref, *refs):
    *pieces, gate_ref, up_ref, gain_ref, grad_gate_ref, grad_up_ref, grad_gain_ref = refs
    gain, total = gain_ref[...], 0.0
    across, chunk = gate_ref.shape[1] // len(pieces), 128
    for j, piece in enumerate(pieces):
        first = (here_ref[0] ^ j) * across
        for c in range(across // chunk):
            there = pl.ds(pl.multiple_of(first + c * chunk, chunk), chunk)
            for i, (weight_ref, out_ref) in enumerate(((gate_ref, grad_gate_ref), (up_ref, grad_up_ref))):
                grad = piece[:, (2 * c + i) * chunk:(2 * c + i + 1) * chunk].astype(FULL)
                out_ref[:, there] = grad * gain
                total = total + grad * weight_ref[:, there].astype(FULL)
    grad_gain_ref[...] = as_row(jnp.sum(total, 1, keepdims=True))


def finish_projections_kernel(here_ref, *refs):
    *pieces, own_ref, query_ref, key_ref, value_ref, gain_ref = refs[:-5]
    grad_query_ref, grad_key_ref, grad_value_ref, grad_output_ref, grad_gain_ref = refs[-5:]
    gain, count = gain_ref[...], len(pieces)
    rows = gain.shape[0]
    qw, kw = query_ref.shape[1] // count, key_ref.shape[1] // count
    total = 0.0
    for j, piece in enumerate(pieces):
        there = pl.ds(pl.multiple_of((here_ref[0] ^ j) * qw, qw), qw)
        grad = piece[:, :qw].astype(FULL)
        grad_query_ref[:, there] = grad * gain
        total = total + jnp.sum(grad * query_ref[:, there].astype(FULL), 1, keepdims=True)
    for first, weight_ref, out_ref in ((qw, key_ref, grad_key_ref), (qw + kw, value_ref, grad_value_ref)):
        grad = [jnp.zeros((rows, kw), FULL)] * count
        for j, piece in enumerate(pieces):
            mine = piece[:, first:first + kw].astype(FULL)
            for t in range(count):
                grad[t] = jnp.where(here_ref[0] == t ^ j, mine, grad[t])
        grad = jnp.concatenate(grad, 1)
        out_ref[...] = grad * gain
        total = total + jnp.sum(grad * weight_ref[...].astype(FULL), 1, keepdims=True)
    across = grad_output_ref.shape[1] // count
    for part in range(count):
        grad_output_ref[:, part * across:(part + 1) * across] = own_ref[part * rows:(part + 1) * rows, :across].astype(FULL)
    grad_gain_ref[...] = as_row(total)


def rows_of(pieces):
    return sum(p.shape[0] for p in pieces)


def whole(shape):
    return pl.BlockSpec(shape, lambda i: (0,) * len(shape))


def columns(rows, width):
    return pl.BlockSpec((rows, width), lambda i: (0, i))


def by_rows(height, width):
    return pl.BlockSpec((height, width), lambda i: (i, 0))


def hidden_kernel(count, chunk, *refs):
    pieces, refs = refs[:count], refs[count:]
    weight_ref, slope_ref, hidden_ref, out_ref, normed_ref, sems, out_sem = refs
    step = pl.program_id(0)
    out_copy = pltpu.make_async_copy(normed_ref, out_ref, out_sem)

    @pl.when(step == 0)
    def _():
        fetch(pieces, normed_ref, sems)
        out_copy.start()

    both = dot(normed_ref[...], weight_ref[...])
    gate, up = both[:, :chunk], both[:, chunk:]
    sigmoid = jax.nn.sigmoid(gate)
    silu = gate * sigmoid
    slope = up * sigmoid * (1.0 + gate * (1.0 - sigmoid))
    slope_ref[...] = jnp.concatenate([slope, silu], 1).astype(LOW)
    hidden_ref[...] = (silu * up).T.astype(LOW)

    @pl.when(step == pl.num_programs(0) - 1)
    def _():
        out_copy.wait()


def hidden_of(pieces, weight, chunk):
    tokens, (width, both) = rows_of(pieces), weight.shape
    return pl.pallas_call(
        functools.partial(hidden_kernel, len(pieces), chunk),
        grid=(both // (2 * chunk),),
        in_specs=[ANY] * len(pieces) + [columns(width, 2 * chunk)],
        out_specs=(columns(tokens, 2 * chunk), by_rows(chunk, tokens), ANY),
        out_shape=(like((tokens, both)), like((both // 2, tokens)), like((tokens, width))),
        scratch_shapes=[pltpu.VMEM((tokens, width), LOW), arrivals(len(pieces)), pltpu.SemaphoreType.DMA],
        compiler_params=PARAMS,
        name="hidden_of",
    )(*pieces, weight)


def grad_down_kernel(count, *refs):
    pieces, (hidden_ref, out_ref, block_ref) = refs[:count], refs[count:]
    join(pieces, block_ref)
    out_ref[...] = dot(hidden_ref[...], block_ref[...]).astype(LOW)


def grad_down_of(hidden, pieces, block=256):
    tokens, width = rows_of(pieces), pieces[0].shape[1]
    return pl.pallas_call(
        functools.partial(grad_down_kernel, len(pieces)),
        grid=(width // block,),
        in_specs=[columns(p.shape[0], block) for p in pieces] + [whole(hidden.shape)],
        out_specs=columns(hidden.shape[0], block),
        out_shape=like((hidden.shape[0], width)),
        scratch_shapes=[pltpu.VMEM((tokens, block), LOW)],
        compiler_params=PARAMS,
        name="grad_down_of",
    )(*pieces, hidden)


def grad_gate_up_kernel(count, chunk, odd, *refs):
    pieces, (down_ref, slope_ref, out_ref, upstream_ref, sems) = refs[:count], refs[count:]
    step, steps = pl.program_id(0), pl.num_programs(0)

    @pl.when(step == 0)
    def _():
        fetch(pieces, upstream_ref, sems)

    def work(chunks):
        grad = dot(upstream_ref[...], down_ref[:chunks * chunk, :], NT)
        each = [grad[:, c * chunk:(c + 1) * chunk] for c in range(chunks) for _ in range(2)]
        width = chunks * 2 * chunk
        out_ref[:, :width] = (jnp.concatenate(each, 1) * slope_ref[:, :width].astype(FULL)).astype(LOW)

    @pl.when(step < steps - odd)
    def _():
        work(2)

    if odd:

        @pl.when(step == steps - 1)
        def _():
            work(1)


def grad_gate_up_of(pieces, down, slope, chunk):
    (tokens, width), depth = (rows_of(pieces), pieces[0].shape[1]), down.shape[0]
    return pl.pallas_call(
        functools.partial(grad_gate_up_kernel, len(pieces), chunk, depth // chunk % 2),
        grid=(pl.cdiv(depth, 2 * chunk),),
        in_specs=[ANY] * len(pieces) + [by_rows(2 * chunk, width), columns(tokens, 4 * chunk)],
        out_specs=columns(tokens, 4 * chunk),
        out_shape=like(slope.shape),
        scratch_shapes=[pltpu.VMEM((tokens, width), LOW), arrivals(len(pieces))],
        compiler_params=PARAMS,
        name="grad_gate_up_of",
    )(*pieces, down, slope)


def grad_rows_kernel(first, grad_ref, weight_ref, *out_refs):
    grad = dot(grad_ref[...], weight_ref[:, first:], NT).astype(LOW)
    rows = out_refs[0].shape[0]
    for i, ref in enumerate(out_refs):
        ref[...] = grad[i * rows:(i + 1) * rows]


def grad_rows_of(grad, weight, piece_rows, block=512):
    tokens, width = grad.shape[0], weight.shape[0]
    count = tokens // piece_rows
    return pl.pallas_call(
        functools.partial(grad_rows_kernel, weight.shape[1] - grad.shape[1]),
        grid=(width // block,),
        in_specs=[whole(grad.shape), by_rows(block, weight.shape[1])],
        out_specs=(columns(piece_rows, block),) * count,
        out_shape=(like((piece_rows, width)),) * count,
        compiler_params=PARAMS,
        name="grad_rows_of",
    )(grad, weight)


def grad_weight_kernel(core_ref, left_ref, other_left_ref, grad_ref, other_grad_ref, out_ref):
    got = dot(left_ref[...], grad_ref[...], TN) + dot(other_left_ref[...], other_grad_ref[...], TN)
    out_ref[...] = got.astype(LOW)


def grad_weight_of(left, other_left, grad, other_grad, core, chips):
    tokens, width = left.shape
    block = width // chips // 2
    mine = pl.BlockSpec((tokens, block), lambda i, core_ref: (0, i * 2 + core_ref[0]))
    every = pl.BlockSpec(grad.shape, lambda i, core_ref: (0, 0))
    return pl.pallas_call(
        grad_weight_kernel,
        grid_spec=pltpu.PrefetchScalarGridSpec(
            num_scalar_prefetch=1,
            grid=(chips,),
            in_specs=[mine, mine, every, every],
            out_specs=pl.BlockSpec((block, grad.shape[1]), lambda i, core_ref: (i, 0)),
        ),
        out_shape=like((width // 2, grad.shape[1])),
        compiler_params=PARAMS,
        name="grad_weight_of",
    )(core, left, other_left, grad, other_grad)


def rows_kernel(left_ref, weight_ref, *refs):
    *out_refs, turned_ref = refs

    @pl.when(pl.program_id(0) == 0)
    def _():
        turned_ref[...] = left_ref[...].T

    weight = weight_ref[...].reshape(turned_ref.shape[1], weight_ref.shape[-1])
    out = dot(turned_ref[...], weight).astype(LOW)
    rows = out_refs[0].shape[0]
    for i, ref in enumerate(out_refs):
        ref[...] = out[i * rows:(i + 1) * rows]


def rows_of_product(left, weight, piece_rows, inner=None, block=512):
    depth, tokens = left.shape
    count = tokens // piece_rows
    if inner is None:
        width, spec = weight.shape[1], columns(depth, block)
    else:
        seq_size, fsdp_size, own_rows = inner
        width = weight.shape[0]
        block = min(block, width // seq_size)
        per = width // seq_size // block
        weight = weight.reshape(fsdp_size, seq_size, own_rows, -1)
        spec = pl.BlockSpec((fsdp_size, 1, own_rows, block), lambda i: (0, i // per, 0, i % per))
    return pl.pallas_call(
        rows_kernel,
        grid=(width // block,),
        in_specs=[whole(left.shape), spec],
        out_specs=(columns(piece_rows, block),) * count,
        out_shape=(like((piece_rows, width)),) * count,
        scratch_shapes=[pltpu.VMEM((tokens, depth), LOW)],
        compiler_params=PARAMS,
        name="rows_of_product",
    )(left, weight)


def attention_weights_kernel(count, inner, *refs):
    tokens, grads = refs[:count], refs[count:2 * count]
    grad_qkv_ref, attended_ref, out_ref, block_ref = refs[2 * count:]
    seq_size, fsdp_size, own_rows = inner
    step, block = pl.program_id(0), block_ref.shape[1]
    across = out_ref.shape[1] - grad_qkv_ref.shape[0]
    join(tokens, block_ref)
    there = pl.ds(pl.multiple_of(step * block, block), block)
    out_ref[there, across:] = dot(grad_qkv_ref[...], block_ref[...]).T.astype(LOW)
    join(grads, block_ref)
    got = dot(attended_ref[...], block_ref[...]).astype(LOW)
    part = step * block // across
    first = step * block % across
    for f in range(fsdp_size):
        rows = pl.ds(pl.multiple_of((f * seq_size + part) * own_rows, own_rows), own_rows)
        out_ref[rows, pl.ds(pl.multiple_of(first, 128), block)] = got[f * own_rows:(f + 1) * own_rows]


def attention_weights_of(tokens, grads, grad_qkv, attended, inner, block=512):
    count, width = len(tokens), tokens[0].shape[1]
    block = min(block, width // inner[0])
    shape = (width, grad_qkv.shape[0] + width // inner[0])
    return pl.pallas_call(
        functools.partial(attention_weights_kernel, count, inner),
        grid=(width // block,),
        in_specs=[columns(p.shape[0], block) for p in (*tokens, *grads)]
        + [whole(grad_qkv.shape), whole(attended.shape)],
        out_specs=whole(shape),
        out_shape=like(shape),
        scratch_shapes=[pltpu.VMEM((rows_of(tokens), block), LOW)],
        compiler_params=PARAMS,
        name="attention_weights_of",
    )(*tokens, *grads, grad_qkv, attended)


def attend_kernel(heads, kvs, span, pieces, order_ref, rank_ref, *refs):
    token_refs, refs = refs[:pieces], refs[pieces:]
    weight_ref, cos_ref, sin_ref, qrot_ref, kv_ref, att_ref, mix_ref, lse_ref, inv_ref, *scratch = refs
    keys_ref, qkv_ref, tokens_ref, sems = scratch
    fetch(token_refs, tokens_ref, sems)
    count = cos_ref.shape[1] // span
    for at in range(0, tokens_ref.shape[0], span):
        there = slice(at, at + span)
        values = tokens_ref[there, :].astype(FULL)
        inv = lax.rsqrt(jnp.mean(values * values, -1, keepdims=True) + EPSILON)
        qkv_ref[:, there] = (dot(tokens_ref[there, :], weight_ref[:, -qkv_ref.shape[0]:]) * inv).T
        inv_ref[:, there] = jnp.broadcast_to(inv, (span, 128)).T[:1]
    qw, kw = heads * HEAD_DIM, kvs * HEAD_DIM
    cosine, sine = cos_ref[...], sin_ref[...]

    def rotated(row):
        one, two = qkv_ref[row:row + HALF, :], qkv_ref[row + HALF:row + HEAD_DIM, :]
        return jnp.concatenate([one * cosine - two * sine, two * cosine + one * sine], 0)

    for h in range(heads):
        qrot_ref[h * HEAD_DIM:(h + 1) * HEAD_DIM, :] = rotated(h * HEAD_DIM).astype(LOW)
    for k in range(kvs):
        turned = rotated(qw + k * HEAD_DIM).astype(LOW)
        kv_ref[k * HEAD_DIM:(k + 1) * HEAD_DIM, :] = turned
        keys_ref[k] = (turned.astype(FULL) * SCALE).T.astype(LOW)
    kv_ref[kw:, :] = qkv_ref[qw + kw:, :].astype(LOW)

    def one_block(qb, _):
        cols = pl.ds(pl.multiple_of(qb * span, span), span)
        rank = rank_ref[qb]

        def step(at, state, diagonal):
            rows = pl.ds(pl.multiple_of(order_ref[at] * span, span), span)
            out = []
            for h in range(heads):
                top, total, mixed = state[h]
                k = h * kvs // heads
                scores = dot(keys_ref[k, rows, :], qrot_ref[h * HEAD_DIM:(h + 1) * HEAD_DIM, cols])
                if diagonal:
                    key_at = lax.broadcasted_iota(jnp.int32, (span, span), 0)
                    query_at = lax.broadcasted_iota(jnp.int32, (span, span), 1)
                    scores = jnp.where(key_at <= query_at, scores, -1e30)
                new_top = jnp.maximum(top, jnp.max(scores, 0, keepdims=True))
                weights = jnp.exp(scores - new_top)
                fade = jnp.exp(top - new_top)
                total = total * fade + jnp.sum(weights, 0, keepdims=True)
                values = kv_ref[kw + k * HEAD_DIM:kw + (k + 1) * HEAD_DIM, rows]
                mixed = mixed * fade + dot(values, weights.astype(LOW))
                out.append((new_top, total, mixed))
            return out

        start = [(jnp.full((1, span), -1e30, FULL), jnp.zeros((1, span), FULL),
                  jnp.zeros((HEAD_DIM, span), FULL)) for _ in range(heads)]
        state = lax.fori_loop(0, rank, lambda at, st: step(at, st, False), start)
        state = step(rank, state, True)
        for h in range(heads):
            top, total, mixed = state[h]
            mixed = mixed / total
            mix_ref[h * HEAD_DIM:(h + 1) * HEAD_DIM, cols] = mixed
            att_ref[h * HEAD_DIM:(h + 1) * HEAD_DIM, cols] = mixed.astype(LOW)
            lse_ref[h:h + 1, cols] = top + jnp.log(total)
        return 0

    lax.fori_loop(0, count, one_block, 0)


def attend(order, rank, pieces, weight, cosine, sine, heads, kvs, span):
    tokens = cosine.shape[1]
    qw, kw = heads * HEAD_DIM, kvs * HEAD_DIM
    return pl.pallas_call(
        functools.partial(attend_kernel, heads, kvs, span, len(pieces)),
        out_shape=(
            like((qw, tokens)), like((2 * kw, tokens)), like((qw, tokens)), like((qw, tokens), FULL),
            like((heads, tokens), FULL), like((1, tokens), FULL),
        ),
        in_specs=[SMEM, SMEM] + [ANY] * len(pieces) + [VMEM] * 3,
        out_specs=(VMEM,) * 6,
        scratch_shapes=[
            pltpu.VMEM((kvs, tokens, HEAD_DIM), LOW),
            pltpu.VMEM((qw + 2 * kw, tokens), FULL),
            pltpu.VMEM((tokens, weight.shape[0]), LOW),
            arrivals(len(pieces)),
        ],
        compiler_params=PARAMS,
        name="attend",
    )(order, rank, *pieces, weight, cosine, sine)


def attend_back_kernel(heads, kvs, span, pieces, order_ref, rank_ref, *refs):
    branch_refs, refs = refs[:pieces], refs[pieces:]
    output_ref, qrot_ref, kv_ref, mix_ref, lse_ref, cos_ref, sin_ref, inv_ref, out_ref, turned_ref, *scratch = refs
    keys_ref, values_ref, delta_ref, dkv_ref, grad_ref, branch_ref, sems = scratch
    count = cos_ref.shape[1] // span
    qw, kw = heads * HEAD_DIM, kvs * HEAD_DIM
    fetch(branch_refs, branch_ref, sems)
    seq_size, across = output_ref.shape[1], branch_ref.shape[1] // output_ref.shape[1]
    for at in range(0, branch_ref.shape[0], span):
        total = 0.0
        for part in range(seq_size):
            weight = output_ref[:, part, :, :across].reshape(qw, across)
            total = total + dot(weight, branch_ref[at:at + span, part * across:(part + 1) * across], NT)
        grad_ref[:, at:at + span] = total.astype(LOW)
    qw, kw = heads * HEAD_DIM, kvs * HEAD_DIM
    for k in range(kvs):
        keys_ref[k] = (kv_ref[k * HEAD_DIM:(k + 1) * HEAD_DIM, :].astype(FULL) * SCALE).T.astype(LOW)
        values_ref[k] = kv_ref[kw + k * HEAD_DIM:kw + (k + 1) * HEAD_DIM, :].astype(FULL).T.astype(LOW)
    for h in range(heads):
        rows = slice(h * HEAD_DIM, (h + 1) * HEAD_DIM)
        delta_ref[h:h + 1, :] = jnp.sum(grad_ref[rows, :].astype(FULL) * mix_ref[rows, :], 0, keepdims=True)
    dkv_ref[...] = jnp.zeros_like(dkv_ref)

    def one_block(qb, _):
        cols = pl.ds(pl.multiple_of(qb * span, span), span)
        rank = rank_ref[qb]

        def step(at, state, diagonal):
            rows = pl.ds(pl.multiple_of(order_ref[at] * span, span), span)
            out = []
            dkeys = [None] * kvs
            dvalues = [None] * kvs
            for h in range(heads):
                k = h * kvs // heads
                mine = slice(h * HEAD_DIM, (h + 1) * HEAD_DIM)
                query = qrot_ref[mine, cols]
                grad = grad_ref[mine, cols]
                scores = dot(keys_ref[k, rows, :], query)
                weights = jnp.exp(scores - lse_ref[h:h + 1, cols])
                if diagonal:
                    key_at = lax.broadcasted_iota(jnp.int32, (span, span), 0)
                    query_at = lax.broadcasted_iota(jnp.int32, (span, span), 1)
                    weights = jnp.where(key_at <= query_at, weights, 0.0)
                grad_probs = dot(values_ref[k, rows, :], grad)
                grad_scores = (weights * (grad_probs - delta_ref[h:h + 1, cols])).astype(LOW)
                key_t = kv_ref[k * HEAD_DIM:(k + 1) * HEAD_DIM, rows]
                out.append(state[h] + dot(key_t, grad_scores))
                dk = dot(query, grad_scores, NT)
                dv = dot(grad, weights.astype(LOW), NT)
                dkeys[k] = dk if dkeys[k] is None else dkeys[k] + dk
                dvalues[k] = dv if dvalues[k] is None else dvalues[k] + dv
            for k in range(kvs):
                mine = slice(k * HEAD_DIM, (k + 1) * HEAD_DIM)
                dkv_ref[mine, rows] += dkeys[k]
                mine = slice(kw + k * HEAD_DIM, kw + (k + 1) * HEAD_DIM)
                dkv_ref[mine, rows] += dvalues[k]
            return out

        state = [jnp.zeros((HEAD_DIM, span), FULL) for _ in range(heads)]
        state = lax.fori_loop(0, rank, lambda at, st: step(at, st, False), state)
        state = step(rank, state, True)
        scale = inv_ref[:, cols] * SCALE
        cosine, sine = cos_ref[:, cols], sin_ref[:, cols]
        for h in range(heads):
            one, two = state[h][:HALF] * scale, state[h][HALF:] * scale
            out_ref[h * HEAD_DIM:h * HEAD_DIM + HALF, cols] = (one * cosine + two * sine).astype(LOW)
            out_ref[h * HEAD_DIM + HALF:(h + 1) * HEAD_DIM, cols] = (two * cosine - one * sine).astype(LOW)
        return 0

    lax.fori_loop(0, count, one_block, 0)
    cosine, sine = cos_ref[...], sin_ref[...]
    scale = inv_ref[...] * SCALE
    for k in range(kvs):
        top = k * HEAD_DIM
        one, two = dkv_ref[top:top + HALF, :] * scale, dkv_ref[top + HALF:top + HEAD_DIM, :] * scale
        out_ref[qw + top:qw + top + HALF, :] = (one * cosine + two * sine).astype(LOW)
        out_ref[qw + top + HALF:qw + top + HEAD_DIM, :] = (two * cosine - one * sine).astype(LOW)
    out_ref[qw + kw:, :] = (dkv_ref[kw:, :] * inv_ref[...]).astype(LOW)
    turned_ref[...] = out_ref[...].T


def attend_back(order, rank, pieces, output, qrot, kv, mix, lse, cosine, sine, inv, heads, kvs, span):
    tokens = cosine.shape[1]
    qw, kw = heads * HEAD_DIM, kvs * HEAD_DIM
    return pl.pallas_call(
        functools.partial(attend_back_kernel, heads, kvs, span, len(pieces)),
        out_shape=(like((qw + 2 * kw, tokens)), like((tokens, qw + 2 * kw))),
        in_specs=[SMEM, SMEM] + [ANY] * len(pieces) + [VMEM] * 8,
        out_specs=(VMEM, VMEM),
        scratch_shapes=[
            pltpu.VMEM((kvs, tokens, HEAD_DIM), LOW),
            pltpu.VMEM((kvs, tokens, HEAD_DIM), LOW),
            pltpu.VMEM((heads, tokens), FULL),
            pltpu.VMEM((2 * kw, tokens), FULL),
            pltpu.VMEM((qw, tokens), LOW),
            pltpu.VMEM((tokens, pieces[0].shape[1]), LOW),
            arrivals(len(pieces)),
        ],
        compiler_params=PARAMS,
        name="attend_back",
    )(order, rank, *pieces, output, qrot, kv, mix, lse, cosine, sine, inv)


def layer(seq_size, fsdp_size, tokens, positions, attn_gain, query_weight, key_weight, value_weight, output_weight,
          ffn_gain, gate_weight, up_weight, down_weight, cotangent):
    span, width = tokens.shape[1:]
    heads = HEADS // seq_size
    kvs = max(1, KV_HEADS // seq_size)
    shared = max(1, seq_size // KV_HEADS)
    qw, kw = heads * HEAD_DIM, kvs * HEAD_DIM
    own_rows = query_weight.shape[0]
    hidden_own = gate_weight.shape[1] // seq_size
    chunk = 128 if hidden_own % 128 == 0 else 64
    parts = 2 if seq_size == 4 else 1
    piece_rows = span // parts
    into, back = (seq_size, fsdp_size, own_rows), (fsdp_size, seq_size, own_rows)
    here = lax.axis_index("seq")

    def after(x, *others):
        return lax.optimization_barrier((x, *others))[0]

    def swap(x, j):
        return lax.ppermute(x, "seq", [(i, i ^ j) for i in range(seq_size)])

    def seq_gather(own):
        if parts == 1:
            return [own[0]] + [swap(own[0], j) for j in range(1, seq_size)]
        a, b = own
        ax, by = swap(a, 1), swap(b, 2)
        ay, bx = swap(a, 2), swap(b, 1)
        ad, bd = swap(ax, 2), swap(by, 1)
        return [a, b, ax, bx, ay, by, ad, bd]

    def scatter_start(pieces):
        if parts == 1:
            return [swap(pieces[j], j) for j in range(1, seq_size)]
        a, b = pieces[::2], pieces[1::2]
        return [swap(a[3], 2), swap(b[3], 1), swap(a[2], 2), swap(b[1], 1)]

    def scatter_end(pieces, came):
        if parts == 1:
            return (), [pieces[0], *came]
        a, b, (da, db, ya, xb) = pieces[::2], pieces[1::2], came
        da = (a[1].astype(FULL) + da.astype(FULL)).astype(LOW)
        db = (b[2].astype(FULL) + db.astype(FULL)).astype(LOW)
        return (da, db), [a[0], ya, swap(da, 1), b[0], xb, swap(db, 2)]

    def seq_scatter(pieces):
        return scatter_end(pieces, scatter_start(pieces))

    def spread(pieces_for):
        got = [pieces_for(here)] + [swap(pieces_for(here ^ j), j) for j in range(1, seq_size)]
        stack = jnp.stack(got)
        return jnp.concatenate(
            [lax.dynamic_index_in_dim(stack, here ^ t, 0, False) for t in range(seq_size)], 0
        )

    def collect(x):
        blocks = x.reshape(seq_size, own_rows, x.shape[1])
        return [lax.dynamic_index_in_dim(blocks, here, 0, False)] + [
            swap(lax.dynamic_index_in_dim(blocks, here ^ j, 0, False), j) for j in range(1, seq_size)
        ]

    def in_order(got):
        got = jnp.stack(got)
        return jnp.stack([lax.dynamic_index_in_dim(got, here ^ t, 0, False) for t in range(seq_size)]).astype(FULL)

    def fsdp_gather(x):
        return lax.all_gather(x, FSDP, axis=0, tiled=True)

    def exchange(x):
        return lax.ppermute(x, "core", [(0, 1), (1, 0)])

    def chip_scatter(x):
        return lax.psum_scatter(x.reshape(-1, x.shape[-1]), "chip", scatter_dimension=0, tiled=True)

    def fsdp_scatter(x):
        return lax.psum_scatter(x, FSDP, scatter_dimension=0, tiled=True)

    gain_one, gain_two = attn_gain.astype(FULL)[:, None], ffn_gain.astype(FULL)[:, None]

    def with_gain(weight, gain):
        return (weight.astype(FULL) * gain).astype(LOW)

    query_low, key_low, value_low = (with_gain(w, gain_one) for w in (query_weight, key_weight, value_weight))

    def qkv_for(t):
        first = (t * heads // GROUP) * HEAD_DIM
        return jnp.concatenate([
            lax.dynamic_slice_in_dim(query_low, t * qw, qw, 1),
            lax.dynamic_slice_in_dim(key_low, first, kw, 1),
            lax.dynamic_slice_in_dim(value_low, first, kw, 1),
        ], 1)

    count = positions.shape[1] // span
    where_at = positions[0].reshape(count, span)
    where_at = jnp.stack([lax.dynamic_index_in_dim(where_at, here ^ j, 0, False) for j in range(count)])
    rank = where_at[:, 0] // span
    order = jnp.argsort(rank).astype(jnp.int32)
    cosine, sine = rope_tables(where_at.reshape(-1))

    own_tokens = tokens[0]
    own_pieces = call_own(
        functools.partial(regroup_kernel, into), (like((piece_rows, width)),) * parts, own_tokens
    )
    token_pieces = seq_gather(own_pieces)
    output_own = output_weight.reshape(own_rows, seq_size, -1).swapaxes(0, 1).reshape(seq_size * own_rows, -1)
    projections = fsdp_gather(jnp.concatenate([output_own, spread(qkv_for)], 1))
    gate_weight, up_weight = lax.optimization_barrier((gate_weight, up_weight, *own_pieces, order, cosine, sine))[:2]
    gate_low, up_low = with_gain(gate_weight, gain_two), with_gain(up_weight, gain_two)

    def gate_up_for(t):
        gate = lax.dynamic_slice_in_dim(gate_low, t * hidden_own, hidden_own, 1)
        up = lax.dynamic_slice_in_dim(up_low, t * hidden_own, hidden_own, 1)
        return jnp.concatenate(
            [x[:, c:c + chunk] for c in range(0, hidden_own, chunk) for x in (gate, up)], 1
        )

    gate_up_own = spread(gate_up_for)
    gate_up_full = fsdp_gather(gate_up_own)
    down_full = fsdp_gather(down_weight)
    own_upstream = after(cotangent[0], gate_up_own, *token_pieces)
    upstream = [own_upstream] + [swap(own_upstream, j) for j in range(1, seq_size)]

    qrot, kv, attended, mix, lse, inv_one = attend(
        order, rank, token_pieces, projections, cosine, sine, heads, kvs, span
    )
    branch = rows_of_product(attended, projections, piece_rows, into)
    branch, upstream = lax.optimization_barrier((branch, upstream))
    branch = seq_scatter(branch)[1]
    middle, inv_two, *own_pieces = call_own(
        functools.partial(middle_kernel, into, parts),
        (like((span, width), FULL), like((span, 1), FULL)) + (like((piece_rows, width)),) * parts,
        own_tokens, *branch, params=SMALL,
    )

    normed_pieces = seq_gather(own_pieces)
    slope, hidden, normed = hidden_of(normed_pieces, gate_up_full, chunk)
    part_down = grad_down_of(hidden, upstream)
    grad_down = fsdp_scatter(part_down)
    grad_gate_up = grad_gate_up_of([after(upstream[0], part_down), *upstream[1:]], down_full, slope, chunk)
    first, grad_pieces = seq_scatter(grad_rows_of(grad_gate_up, gate_up_full, piece_rows))
    place, core = (at.astype(jnp.int32).reshape(1) for at in (here, lax.axis_index("core")))
    part_gate_up = grad_weight_of(
        after(normed, *first), exchange(normed), grad_gate_up, exchange(grad_gate_up), core, fsdp_size // 2
    )
    part_gate_up, *grad_pieces = lax.optimization_barrier((part_gate_up, *grad_pieces))
    grad_gate_up_own = chip_scatter(part_gate_up)
    grad_pieces[0] = after(grad_pieces[0], grad_down)
    grad_middle, *own_pieces = call_own(
        functools.partial(grad_middle_kernel, back, parts),
        (like((span, width), FULL),) + (like((piece_rows, width)),) * parts,
        cotangent[0], middle, inv_two, *grad_pieces,
    )

    branch_pieces = seq_gather(own_pieces)
    out_pieces = rows_of_product(after(hidden, own_pieces[0]), down_full, piece_rows)
    out_pieces = lax.optimization_barrier((*out_pieces, *branch_pieces))[:len(out_pieces)]
    out_came = scatter_start(out_pieces)
    grad_qkv, grad_qkv_turned = attend_back(
        order, rank, branch_pieces, projections.reshape(fsdp_size, seq_size, own_rows, -1), qrot, kv, mix, lse,
        cosine, sine, inv_one, heads, kvs, span,
    )
    grad_qkv, grad_qkv_turned, *out_came = lax.optimization_barrier((grad_qkv, grad_qkv_turned, *out_came))
    part_projections = attention_weights_of(token_pieces, branch_pieces, grad_qkv, attended, into)
    grad_pieces = grad_rows_of(grad_qkv_turned, projections, piece_rows)
    first, grad_pieces = seq_scatter(grad_pieces)
    grad_projections = fsdp_scatter(after(part_projections, grad_gate_up_own, *first))
    got = collect(after(grad_gate_up_own, *grad_pieces))
    out_pieces = scatter_end(out_pieces, out_came)[1]
    block_out = call_own(functools.partial(block_out_kernel, parts), like((span, width)), middle, *out_pieces)


    def whole_rows(x):
        return x.swapaxes(0, 1).reshape(own_rows, -1)

    if chunk == 128:
        rows_like = like((own_rows, gate_weight.shape[1]), FULL)
        grad_gate, grad_up, grad_ffn_gain = call_own(
            finish_gate_up_kernel, (rows_like, rows_like, like((1, own_rows), FULL)),
            *got, gate_weight, up_weight, gain_two, scalars=(place,),
        )
    else:
        got = in_order(got).reshape(seq_size, own_rows, -1, 2, chunk)
        grad_gate, grad_up = whole_rows(got[:, :, :, 0]), whole_rows(got[:, :, :, 1])
        grad_ffn_gain = jnp.sum(grad_gate * gate_weight.astype(FULL) + grad_up * up_weight.astype(FULL), 1)
        grad_gate, grad_up = grad_gate * gain_two, grad_up * gain_two
    grad_tokens = call_own(
        functools.partial(grad_tokens_kernel, back, parts), like((span, width), FULL),
        own_tokens, grad_middle, *grad_pieces,
    )
    grad_projections = after(grad_projections, grad_tokens, block_out, grad_ffn_gain)
    got = collect(grad_projections[:, -qw - 2 * kw:])
    if shared == 1 and kvs == 1:
        grad_query, grad_key, grad_value, grad_output, grad_attn_gain = call_own(
            finish_projections_kernel,
            tuple(like(w.shape, FULL) for w in (query_weight, key_weight, value_weight, output_weight))
            + (like((1, own_rows), FULL),),
            *got, grad_projections, query_weight, key_weight, value_weight, gain_one, scalars=(place,), params=SMALL,
        )
    else:
        grad_output = grad_projections[:, :-qw - 2 * kw].reshape(seq_size, own_rows, -1).swapaxes(0, 1)
        grad_output = grad_output.reshape(own_rows, width).astype(FULL)
        got = in_order(got)
        grad_query = whole_rows(got[:, :, :qw])

        def of_heads(x):
            return whole_rows(x.reshape(seq_size // shared, shared, own_rows, kw).sum(1))

        grad_key, grad_value = of_heads(got[:, :, qw:qw + kw]), of_heads(got[:, :, qw + kw:])
        grads = (grad_query, grad_key, grad_value)
        grad_attn_gain = sum(
            jnp.sum(g * w.astype(FULL), 1) for g, w in zip(grads, (query_weight, key_weight, value_weight))
        )
        grad_query, grad_key, grad_value = (g * gain_one for g in grads)
    return (
        block_out[None],
        grad_tokens[None],
        grad_attn_gain.reshape(-1),
        grad_query,
        grad_key,
        grad_value,
        grad_output,
        grad_ffn_gain.reshape(-1),
        grad_gate,
        grad_up,
        grad_down.astype(FULL),
    )


def solution(mesh):
    seq_size, fsdp_size = mesh.shape["seq"], mesh.shape["fsdp"]
    split = Mesh(mesh.devices.reshape(seq_size, fsdp_size // 2, 2), ("seq", "chip", "core"))
    rows, vector, matrix = P(FSDP, "seq", None), P(("seq", *FSDP)), P(("seq", *FSDP), None)
    return jax.shard_map(
        functools.partial(layer, seq_size, fsdp_size),
        mesh=split,
        in_specs=(
            rows, P(FSDP, None), vector, matrix, matrix, matrix, matrix, vector, matrix, matrix, matrix, rows,
        ),
        out_specs=(rows, rows, vector, matrix, matrix, matrix, matrix, vector, matrix, matrix, matrix),
        check_vma=False,
    )
```

```python
import functools
import math

import jax
import jax.numpy as jnp
from jax import lax
from jax.experimental import pallas as pl
from jax.experimental.pallas import tpu as pltpu
from jax.sharding import Mesh
from jax.sharding import PartitionSpec as P

HEADS = 32
KV_HEADS = 4
HEAD_DIM = 64
HALF = HEAD_DIM // 2
GROUP = HEADS // KV_HEADS
EPSILON = 1e-05
SCALE = 1.0 / math.sqrt(HEAD_DIM)
FSDP = ("chip", "core")
LOW = jnp.bfloat16
FULL = jnp.float32
VMEM = pl.BlockSpec(memory_space=pltpu.VMEM)
ANY = pl.BlockSpec(memory_space=pltpu.HBM)
SMEM = pl.BlockSpec(memory_space=pltpu.SMEM)
PARAMS = pltpu.CompilerParams(vmem_limit_bytes=60 << 20)
SMALL = pltpu.CompilerParams(vmem_limit_bytes=20 << 20)
NN, NT, TN = ((1,), (0,)), ((1,), (1,)), ((0,), (0,))


def dot(a, b, dims=NN):
    return lax.dot_general(a, b, (dims, ((), ())), preferred_element_type=FULL)


def like(shape, dtype=LOW):
    return jax.ShapeDtypeStruct(shape, dtype)


def rope_tables(where_at):
    frequency = 1.0 / 10000.0 ** (jnp.arange(HALF, dtype=FULL) * 2.0 / HEAD_DIM)
    angles = frequency[:, None] * where_at.astype(FULL)[None, :]
    return jnp.cos(angles), jnp.sin(angles)


def regroup(x, outer, inner, rows):
    return jnp.concatenate(
        [x[:, (o * inner + i) * rows:(o * inner + i + 1) * rows] for i in range(inner) for o in range(outer)], 1
    )


def join(pieces, whole_ref):
    at = 0
    for piece in pieces:
        whole_ref[at:at + piece.shape[0], :] = piece[...]
        at += piece.shape[0]


def fetch(pieces, whole_ref, sems):
    copies, at = [], 0
    for i, piece in enumerate(pieces):
        rows = piece.shape[0]
        copies.append(pltpu.make_async_copy(piece, whole_ref.at[pl.ds(at, rows)], sems.at[i]))
        at += rows
    for copy in copies:
        copy.start()
    for copy in copies:
        copy.wait()


def arrivals(count):
    return pltpu.SemaphoreType.DMA((count,))


def call_own(kernel, out_shape, *args, scalars=(), params=PARAMS):
    return pl.pallas_call(
        kernel, out_shape=out_shape, in_specs=[SMEM] * len(scalars) + [VMEM] * len(args),
        out_specs=jax.tree.map(lambda _: VMEM, out_shape), compiler_params=params,
        name=getattr(kernel, "func", kernel).__name__,
    )(*scalars, *args)


def added(refs):
    total = refs[0][...].astype(FULL)
    for ref in refs[1:]:
        total = total + ref[...].astype(FULL)
    return total


def regroup_kernel(grid, x_ref, *out_refs):
    x = regroup(x_ref[...].astype(FULL), *grid).astype(LOW)
    rows = out_refs[0].shape[0]
    for i, ref in enumerate(out_refs):
        ref[...] = x[i * rows:(i + 1) * rows]


def middle_kernel(grid, parts, *refs):
    tokens_ref, refs = refs[0], refs[1:]
    per = (len(refs) - 2 - parts) // parts
    middle_ref, inv_ref, *normed_refs = refs[per * parts:]
    rows = normed_refs[0].shape[0]
    for i in range(parts):
        at = slice(i * rows, (i + 1) * rows)
        middle = tokens_ref[at, :].astype(FULL) + added(refs[i * per:(i + 1) * per])
        inv = lax.rsqrt(jnp.mean(middle * middle, -1, keepdims=True) + EPSILON)
        middle_ref[at, :] = middle
        inv_ref[at, :] = inv
        normed_refs[i][...] = regroup(middle * inv, *grid).astype(LOW)


def grad_middle_kernel(grid, parts, *refs):
    upstream_ref, middle_ref, inv_ref, refs = refs[0], refs[1], refs[2], refs[3:]
    out_ref, *low_refs = refs[-1 - parts:]
    per = (len(refs) - 1 - parts) // parts
    rows = low_refs[0].shape[0]
    for i in range(parts):
        at = slice(i * rows, (i + 1) * rows)
        inv = inv_ref[at, :]
        normed = middle_ref[at, :] * inv
        grad = regroup(added(refs[i * per:(i + 1) * per]), *grid)
        grad = upstream_ref[at, :].astype(FULL) + inv * (grad - normed * jnp.mean(grad * normed, -1, keepdims=True))
        out_ref[at, :] = grad
        low_refs[i][...] = grad.astype(LOW)


def grad_tokens_kernel(grid, parts, *refs):
    tokens_ref, grad_ref, refs, out_ref = refs[0], refs[1], refs[2:-1], refs[-1]
    per = len(refs) // parts
    rows = out_ref.shape[0] // parts
    for i in range(parts):
        at = slice(i * rows, (i + 1) * rows)
        tokens = tokens_ref[at, :].astype(FULL)
        normed = tokens * lax.rsqrt(jnp.mean(tokens * tokens, -1, keepdims=True) + EPSILON)
        grad = regroup(added(refs[i * per:(i + 1) * per]), *grid)
        out_ref[at, :] = grad_ref[at, :] + grad - normed * jnp.mean(grad * normed, -1, keepdims=True)


def block_out_kernel(parts, *refs):
    middle_ref, refs, out_ref = refs[0], refs[1:-1], refs[-1]
    per, rows = len(refs) // parts, out_ref.shape[0] // parts
    for i in range(parts):
        at = slice(i * rows, (i + 1) * rows)
        out_ref[at, :] = (middle_ref[at, :] + added(refs[i * per:(i + 1) * per])).astype(LOW)


def as_row(column):
    return jnp.broadcast_to(column, (column.shape[0], 128)).T[:1]


def finish_gate_up_kernel(here_ref, *refs):
    *pieces, gate_ref, up_ref, gain_ref, grad_gate_ref, grad_up_ref, grad_gain_ref = refs
    gain, total = gain_ref[...], 0.0
    across, chunk = gate_ref.shape[1] // len(pieces), 128
    for j, piece in enumerate(pieces):
        first = (here_ref[0] ^ j) * across
        for c in range(across // chunk):
            there = pl.ds(pl.multiple_of(first + c * chunk, chunk), chunk)
            for i, (weight_ref, out_ref) in enumerate(((gate_ref, grad_gate_ref), (up_ref, grad_up_ref))):
                grad = piece[:, (2 * c + i) * chunk:(2 * c + i + 1) * chunk].astype(FULL)
                out_ref[:, there] = grad * gain
                total = total + grad * weight_ref[:, there].astype(FULL)
    grad_gain_ref[...] = as_row(jnp.sum(total, 1, keepdims=True))


def finish_projections_kernel(here_ref, *refs):
    *pieces, own_ref, query_ref, key_ref, value_ref, gain_ref = refs[:-5]
    grad_query_ref, grad_key_ref, grad_value_ref, grad_output_ref, grad_gain_ref = refs[-5:]
    gain, count = gain_ref[...], len(pieces)
    rows = gain.shape[0]
    qw, kw = query_ref.shape[1] // count, key_ref.shape[1] // count
    total = 0.0
    for j, piece in enumerate(pieces):
        there = pl.ds(pl.multiple_of((here_ref[0] ^ j) * qw, qw), qw)
        grad = piece[:, :qw].astype(FULL)
        grad_query_ref[:, there] = grad * gain
        total = total + jnp.sum(grad * query_ref[:, there].astype(FULL), 1, keepdims=True)
    for first, weight_ref, out_ref in ((qw, key_ref, grad_key_ref), (qw + kw, value_ref, grad_value_ref)):
        grad = [jnp.zeros((rows, kw), FULL)] * count
        for j, piece in enumerate(pieces):
            mine = piece[:, first:first + kw].astype(FULL)
            for t in range(count):
                grad[t] = jnp.where(here_ref[0] == t ^ j, mine, grad[t])
        grad = jnp.concatenate(grad, 1)
        out_ref[...] = grad * gain
        total = total + jnp.sum(grad * weight_ref[...].astype(FULL), 1, keepdims=True)
    across = grad_output_ref.shape[1] // count
    for part in range(count):
        grad_output_ref[:, part * across:(part + 1) * across] = own_ref[part * rows:(part + 1) * rows, :across].astype(FULL)
    grad_gain_ref[...] = as_row(total)


def rows_of(pieces):
    return sum(p.shape[0] for p in pieces)


def whole(shape):
    return pl.BlockSpec(shape, lambda i: (0,) * len(shape))


def columns(rows, width):
    return pl.BlockSpec((rows, width), lambda i: (0, i))


def by_rows(height, width):
    return pl.BlockSpec((height, width), lambda i: (i, 0))


def hidden_kernel(count, chunk, *refs):
    pieces, refs = refs[:count], refs[count:]
    weight_ref, slope_ref, hidden_ref, out_ref, normed_ref, sems, out_sem = refs
    step = pl.program_id(0)
    out_copy = pltpu.make_async_copy(normed_ref, out_ref, out_sem)

    @pl.when(step == 0)
    def _():
        fetch(pieces, normed_ref, sems)
        out_copy.start()

    both = dot(normed_ref[...], weight_ref[...])
    gate, up = both[:, :chunk], both[:, chunk:]
    sigmoid = jax.nn.sigmoid(gate)
    silu = gate * sigmoid
    slope = up * sigmoid * (1.0 + gate * (1.0 - sigmoid))
    slope_ref[...] = jnp.concatenate([slope, silu], 1).astype(LOW)
    hidden_ref[...] = (silu * up).T.astype(LOW)

    @pl.when(step == pl.num_programs(0) - 1)
    def _():
        out_copy.wait()


def hidden_of(pieces, weight, chunk):
    tokens, (width, both) = rows_of(pieces), weight.shape
    return pl.pallas_call(
        functools.partial(hidden_kernel, len(pieces), chunk),
        grid=(both // (2 * chunk),),
        in_specs=[ANY] * len(pieces) + [columns(width, 2 * chunk)],
        out_specs=(columns(tokens, 2 * chunk), by_rows(chunk, tokens), ANY),
        out_shape=(like((tokens, both)), like((both // 2, tokens)), like((tokens, width))),
        scratch_shapes=[pltpu.VMEM((tokens, width), LOW), arrivals(len(pieces)), pltpu.SemaphoreType.DMA],
        compiler_params=PARAMS,
        name="hidden_of",
    )(*pieces, weight)


def grad_down_kernel(count, *refs):
    pieces, (hidden_ref, out_ref, block_ref) = refs[:count], refs[count:]
    join(pieces, block_ref)
    out_ref[...] = dot(hidden_ref[...], block_ref[...]).astype(LOW)


def grad_down_of(hidden, pieces, block=256):
    tokens, width = rows_of(pieces), pieces[0].shape[1]
    return pl.pallas_call(
        functools.partial(grad_down_kernel, len(pieces)),
        grid=(width // block,),
        in_specs=[columns(p.shape[0], block) for p in pieces] + [whole(hidden.shape)],
        out_specs=columns(hidden.shape[0], block),
        out_shape=like((hidden.shape[0], width)),
        scratch_shapes=[pltpu.VMEM((tokens, block), LOW)],
        compiler_params=PARAMS,
        name="grad_down_of",
    )(*pieces, hidden)


def grad_gate_up_kernel(count, chunk, odd, *refs):
    pieces, (down_ref, slope_ref, out_ref, upstream_ref, sems) = refs[:count], refs[count:]
    step, steps = pl.program_id(0), pl.num_programs(0)

    @pl.when(step == 0)
    def _():
        fetch(pieces, upstream_ref, sems)

    def work(chunks):
        grad = dot(upstream_ref[...], down_ref[:chunks * chunk, :], NT)
        each = [grad[:, c * chunk:(c + 1) * chunk] for c in range(chunks) for _ in range(2)]
        width = chunks * 2 * chunk
        out_ref[:, :width] = (jnp.concatenate(each, 1) * slope_ref[:, :width].astype(FULL)).astype(LOW)

    @pl.when(step < steps - odd)
    def _():
        work(2)

    if odd:

        @pl.when(step == steps - 1)
        def _():
            work(1)


def grad_gate_up_of(pieces, down, slope, chunk):
    (tokens, width), depth = (rows_of(pieces), pieces[0].shape[1]), down.shape[0]
    return pl.pallas_call(
        functools.partial(grad_gate_up_kernel, len(pieces), chunk, depth // chunk % 2),
        grid=(pl.cdiv(depth, 2 * chunk),),
        in_specs=[ANY] * len(pieces) + [by_rows(2 * chunk, width), columns(tokens, 4 * chunk)],
        out_specs=columns(tokens, 4 * chunk),
        out_shape=like(slope.shape),
        scratch_shapes=[pltpu.VMEM((tokens, width), LOW), arrivals(len(pieces))],
        compiler_params=PARAMS,
        name="grad_gate_up_of",
    )(*pieces, down, slope)


def grad_rows_kernel(first, grad_ref, weight_ref, *out_refs):
    grad = dot(grad_ref[...], weight_ref[:, first:], NT).astype(LOW)
    rows = out_refs[0].shape[0]
    for i, ref in enumerate(out_refs):
        ref[...] = grad[i * rows:(i + 1) * rows]


def grad_rows_of(grad, weight, piece_rows, block=512):
    tokens, width = grad.shape[0], weight.shape[0]
    count = tokens // piece_rows
    return pl.pallas_call(
        functools.partial(grad_rows_kernel, weight.shape[1] - grad.shape[1]),
        grid=(width // block,),
        in_specs=[whole(grad.shape), by_rows(block, weight.shape[1])],
        out_specs=(columns(piece_rows, block),) * count,
        out_shape=(like((piece_rows, width)),) * count,
        compiler_params=PARAMS,
        name="grad_rows_of",
    )(grad, weight)


def grad_weight_kernel(core_ref, left_ref, other_left_ref, grad_ref, other_grad_ref, out_ref):
    got = dot(left_ref[...], grad_ref[...], TN) + dot(other_left_ref[...], other_grad_ref[...], TN)
    out_ref[...] = got.astype(LOW)


def grad_weight_of(left, other_left, grad, other_grad, core, chips):
    tokens, width = left.shape
    block = width // chips // 2
    mine = pl.BlockSpec((tokens, block), lambda i, core_ref: (0, i * 2 + core_ref[0]))
    every = pl.BlockSpec(grad.shape, lambda i, core_ref: (0, 0))
    return pl.pallas_call(
        grad_weight_kernel,
        grid_spec=pltpu.PrefetchScalarGridSpec(
            num_scalar_prefetch=1,
            grid=(chips,),
            in_specs=[mine, mine, every, every],
            out_specs=pl.BlockSpec((block, grad.shape[1]), lambda i, core_ref: (i, 0)),
        ),
        out_shape=like((width // 2, grad.shape[1])),
        compiler_params=PARAMS,
        name="grad_weight_of",
    )(core, left, other_left, grad, other_grad)


def rows_kernel(left_ref, weight_ref, *refs):
    *out_refs, turned_ref = refs

    @pl.when(pl.program_id(0) == 0)
    def _():
        turned_ref[...] = left_ref[...].T

    weight = weight_ref[...].reshape(turned_ref.shape[1], weight_ref.shape[-1])
    out = dot(turned_ref[...], weight).astype(LOW)
    rows = out_refs[0].shape[0]
    for i, ref in enumerate(out_refs):
        ref[...] = out[i * rows:(i + 1) * rows]


def rows_of_product(left, weight, piece_rows, inner=None, block=512):
    depth, tokens = left.shape
    count = tokens // piece_rows
    if inner is None:
        width, spec = weight.shape[1], columns(depth, block)
    else:
        seq_size, fsdp_size, own_rows = inner
        width = weight.shape[0]
        block = min(block, width // seq_size)
        per = width // seq_size // block
        weight = weight.reshape(fsdp_size, seq_size, own_rows, -1)
        spec = pl.BlockSpec((fsdp_size, 1, own_rows, block), lambda i: (0, i // per, 0, i % per))
    return pl.pallas_call(
        rows_kernel,
        grid=(width // block,),
        in_specs=[whole(left.shape), spec],
        out_specs=(columns(piece_rows, block),) * count,
        out_shape=(like((piece_rows, width)),) * count,
        scratch_shapes=[pltpu.VMEM((tokens, depth), LOW)],
        compiler_params=PARAMS,
        name="rows_of_product",
    )(left, weight)


def attention_weights_kernel(count, inner, *refs):
    tokens, grads = refs[:count], refs[count:2 * count]
    grad_qkv_ref, attended_ref, out_ref, block_ref = refs[2 * count:]
    seq_size, fsdp_size, own_rows = inner
    step, block = pl.program_id(0), block_ref.shape[1]
    across = out_ref.shape[1] - grad_qkv_ref.shape[0]
    join(tokens, block_ref)
    there = pl.ds(pl.multiple_of(step * block, block), block)
    out_ref[there, across:] = dot(grad_qkv_ref[...], block_ref[...]).T.astype(LOW)
    join(grads, block_ref)
    got = dot(attended_ref[...], block_ref[...]).astype(LOW)
    part = step * block // across
    first = step * block % across
    for f in range(fsdp_size):
        rows = pl.ds(pl.multiple_of((f * seq_size + part) * own_rows, own_rows), own_rows)
        out_ref[rows, pl.ds(pl.multiple_of(first, 128), block)] = got[f * own_rows:(f + 1) * own_rows]


def attention_weights_of(tokens, grads, grad_qkv, attended, inner, block=512):
    count, width = len(tokens), tokens[0].shape[1]
    block = min(block, width // inner[0])
    shape = (width, grad_qkv.shape[0] + width // inner[0])
    return pl.pallas_call(
        functools.partial(attention_weights_kernel, count, inner),
        grid=(width // block,),
        in_specs=[columns(p.shape[0], block) for p in (*tokens, *grads)]
        + [whole(grad_qkv.shape), whole(attended.shape)],
        out_specs=whole(shape),
        out_shape=like(shape),
        scratch_shapes=[pltpu.VMEM((rows_of(tokens), block), LOW)],
        compiler_params=PARAMS,
        name="attention_weights_of",
    )(*tokens, *grads, grad_qkv, attended)


def attend_kernel(heads, kvs, span, pieces, order_ref, rank_ref, *refs):
    token_refs, refs = refs[:pieces], refs[pieces:]
    weight_ref, cos_ref, sin_ref, qrot_ref, kv_ref, att_ref, mix_ref, lse_ref, inv_ref, *scratch = refs
    keys_ref, qkv_ref, tokens_ref, sems = scratch
    fetch(token_refs, tokens_ref, sems)
    count = cos_ref.shape[1] // span
    for at in range(0, tokens_ref.shape[0], span):
        there = slice(at, at + span)
        values = tokens_ref[there, :].astype(FULL)
        inv = lax.rsqrt(jnp.mean(values * values, -1, keepdims=True) + EPSILON)
        qkv_ref[:, there] = (dot(tokens_ref[there, :], weight_ref[:, -qkv_ref.shape[0]:]) * inv).T
        inv_ref[:, there] = jnp.broadcast_to(inv, (span, 128)).T[:1]
    qw, kw = heads * HEAD_DIM, kvs * HEAD_DIM
    cosine, sine = cos_ref[...], sin_ref[...]

    def rotated(row):
        one, two = qkv_ref[row:row + HALF, :], qkv_ref[row + HALF:row + HEAD_DIM, :]
        return jnp.concatenate([one * cosine - two * sine, two * cosine + one * sine], 0)

    for h in range(heads):
        qrot_ref[h * HEAD_DIM:(h + 1) * HEAD_DIM, :] = rotated(h * HEAD_DIM).astype(LOW)
    for k in range(kvs):
        turned = rotated(qw + k * HEAD_DIM).astype(LOW)
        kv_ref[k * HEAD_DIM:(k + 1) * HEAD_DIM, :] = turned
        keys_ref[k] = (turned.astype(FULL) * SCALE).T.astype(LOW)
    kv_ref[kw:, :] = qkv_ref[qw + kw:, :].astype(LOW)

    def one_block(qb, _):
        cols = pl.ds(pl.multiple_of(qb * span, span), span)
        rank = rank_ref[qb]

        def step(at, state, diagonal):
            rows = pl.ds(pl.multiple_of(order_ref[at] * span, span), span)
            out = []
            for h in range(heads):
                top, total, mixed = state[h]
                k = h * kvs // heads
                scores = dot(keys_ref[k, rows, :], qrot_ref[h * HEAD_DIM:(h + 1) * HEAD_DIM, cols])
                if diagonal:
                    key_at = lax.broadcasted_iota(jnp.int32, (span, span), 0)
                    query_at = lax.broadcasted_iota(jnp.int32, (span, span), 1)
                    scores = jnp.where(key_at <= query_at, scores, -1e30)
                new_top = jnp.maximum(top, jnp.max(scores, 0, keepdims=True))
                weights = jnp.exp(scores - new_top)
                fade = jnp.exp(top - new_top)
                total = total * fade + jnp.sum(weights, 0, keepdims=True)
                values = kv_ref[kw + k * HEAD_DIM:kw + (k + 1) * HEAD_DIM, rows]
                mixed = mixed * fade + dot(values, weights.astype(LOW))
                out.append((new_top, total, mixed))
            return out

        start = [(jnp.full((1, span), -1e30, FULL), jnp.zeros((1, span), FULL),
                  jnp.zeros((HEAD_DIM, span), FULL)) for _ in range(heads)]
        state = lax.fori_loop(0, rank, lambda at, st: step(at, st, False), start)
        state = step(rank, state, True)
        for h in range(heads):
            top, total, mixed = state[h]
            mixed = mixed / total
            mix_ref[h * HEAD_DIM:(h + 1) * HEAD_DIM, cols] = mixed
            att_ref[h * HEAD_DIM:(h + 1) * HEAD_DIM, cols] = mixed.astype(LOW)
            lse_ref[h:h + 1, cols] = top + jnp.log(total)
        return 0

    lax.fori_loop(0, count, one_block, 0)


def attend(order, rank, pieces, weight, cosine, sine, heads, kvs, span):
    tokens = cosine.shape[1]
    qw, kw = heads * HEAD_DIM, kvs * HEAD_DIM
    return pl.pallas_call(
        functools.partial(attend_kernel, heads, kvs, span, len(pieces)),
        out_shape=(
            like((qw, tokens)), like((2 * kw, tokens)), like((qw, tokens)), like((qw, tokens), FULL),
            like((heads, tokens), FULL), like((1, tokens), FULL),
        ),
        in_specs=[SMEM, SMEM] + [ANY] * len(pieces) + [VMEM] * 3,
        out_specs=(VMEM,) * 6,
        scratch_shapes=[
            pltpu.VMEM((kvs, tokens, HEAD_DIM), LOW),
            pltpu.VMEM((qw + 2 * kw, tokens), FULL),
            pltpu.VMEM((tokens, weight.shape[0]), LOW),
            arrivals(len(pieces)),
        ],
        compiler_params=PARAMS,
        name="attend",
    )(order, rank, *pieces, weight, cosine, sine)


def attend_back_kernel(heads, kvs, span, pieces, order_ref, rank_ref, *refs):
    branch_refs, refs = refs[:pieces], refs[pieces:]
    output_ref, qrot_ref, kv_ref, mix_ref, lse_ref, cos_ref, sin_ref, inv_ref, out_ref, turned_ref, *scratch = refs
    keys_ref, values_ref, delta_ref, dkv_ref, grad_ref, branch_ref, sems = scratch
    count = cos_ref.shape[1] // span
    qw, kw = heads * HEAD_DIM, kvs * HEAD_DIM
    fetch(branch_refs, branch_ref, sems)
    seq_size, across = output_ref.shape[1], branch_ref.shape[1] // output_ref.shape[1]
    for at in range(0, branch_ref.shape[0], span):
        total = 0.0
        for part in range(seq_size):
            weight = output_ref[:, part, :, :across].reshape(qw, across)
            total = total + dot(weight, branch_ref[at:at + span, part * across:(part + 1) * across], NT)
        grad_ref[:, at:at + span] = total.astype(LOW)
    qw, kw = heads * HEAD_DIM, kvs * HEAD_DIM
    for k in range(kvs):
        keys_ref[k] = (kv_ref[k * HEAD_DIM:(k + 1) * HEAD_DIM, :].astype(FULL) * SCALE).T.astype(LOW)
        values_ref[k] = kv_ref[kw + k * HEAD_DIM:kw + (k + 1) * HEAD_DIM, :].astype(FULL).T.astype(LOW)
    for h in range(heads):
        rows = slice(h * HEAD_DIM, (h + 1) * HEAD_DIM)
        delta_ref[h:h + 1, :] = jnp.sum(grad_ref[rows, :].astype(FULL) * mix_ref[rows, :], 0, keepdims=True)
    dkv_ref[...] = jnp.zeros_like(dkv_ref)

    def one_block(qb, _):
        cols = pl.ds(pl.multiple_of(qb * span, span), span)
        rank = rank_ref[qb]

        def step(at, state, diagonal):
            rows = pl.ds(pl.multiple_of(order_ref[at] * span, span), span)
            out = []
            dkeys = [None] * kvs
            dvalues = [None] * kvs
            for h in range(heads):
                k = h * kvs // heads
                mine = slice(h * HEAD_DIM, (h + 1) * HEAD_DIM)
                query = qrot_ref[mine, cols]
                grad = grad_ref[mine, cols]
                scores = dot(keys_ref[k, rows, :], query)
                weights = jnp.exp(scores - lse_ref[h:h + 1, cols])
                if diagonal:
                    key_at = lax.broadcasted_iota(jnp.int32, (span, span), 0)
                    query_at = lax.broadcasted_iota(jnp.int32, (span, span), 1)
                    weights = jnp.where(key_at <= query_at, weights, 0.0)
                grad_probs = dot(values_ref[k, rows, :], grad)
                grad_scores = (weights * (grad_probs - delta_ref[h:h + 1, cols])).astype(LOW)
                key_t = kv_ref[k * HEAD_DIM:(k + 1) * HEAD_DIM, rows]
                out.append(state[h] + dot(key_t, grad_scores))
                dk = dot(query, grad_scores, NT)
                dv = dot(grad, weights.astype(LOW), NT)
                dkeys[k] = dk if dkeys[k] is None else dkeys[k] + dk
                dvalues[k] = dv if dvalues[k] is None else dvalues[k] + dv
            for k in range(kvs):
                mine = slice(k * HEAD_DIM, (k + 1) * HEAD_DIM)
                dkv_ref[mine, rows] += dkeys[k]
                mine = slice(kw + k * HEAD_DIM, kw + (k + 1) * HEAD_DIM)
                dkv_ref[mine, rows] += dvalues[k]
            return out

        state = [jnp.zeros((HEAD_DIM, span), FULL) for _ in range(heads)]
        state = lax.fori_loop(0, rank, lambda at, st: step(at, st, False), state)
        state = step(rank, state, True)
        scale = inv_ref[:, cols] * SCALE
        cosine, sine = cos_ref[:, cols], sin_ref[:, cols]
        for h in range(heads):
            one, two = state[h][:HALF] * scale, state[h][HALF:] * scale
            out_ref[h * HEAD_DIM:h * HEAD_DIM + HALF, cols] = (one * cosine + two * sine).astype(LOW)
            out_ref[h * HEAD_DIM + HALF:(h + 1) * HEAD_DIM, cols] = (two * cosine - one * sine).astype(LOW)
        return 0

    lax.fori_loop(0, count, one_block, 0)
    cosine, sine = cos_ref[...], sin_ref[...]
    scale = inv_ref[...] * SCALE
    for k in range(kvs):
        top = k * HEAD_DIM
        one, two = dkv_ref[top:top + HALF, :] * scale, dkv_ref[top + HALF:top + HEAD_DIM, :] * scale
        out_ref[qw + top:qw + top + HALF, :] = (one * cosine + two * sine).astype(LOW)
        out_ref[qw + top + HALF:qw + top + HEAD_DIM, :] = (two * cosine - one * sine).astype(LOW)
    out_ref[qw + kw:, :] = (dkv_ref[kw:, :] * inv_ref[...]).astype(LOW)
    turned_ref[...] = out_ref[...].T


def attend_back(order, rank, pieces, output, qrot, kv, mix, lse, cosine, sine, inv, heads, kvs, span):
    tokens = cosine.shape[1]
    qw, kw = heads * HEAD_DIM, kvs * HEAD_DIM
    return pl.pallas_call(
        functools.partial(attend_back_kernel, heads, kvs, span, len(pieces)),
        out_shape=(like((qw + 2 * kw, tokens)), like((tokens, qw + 2 * kw))),
        in_specs=[SMEM, SMEM] + [ANY] * len(pieces) + [VMEM] * 8,
        out_specs=(VMEM, VMEM),
        scratch_shapes=[
            pltpu.VMEM((kvs, tokens, HEAD_DIM), LOW),
            pltpu.VMEM((kvs, tokens, HEAD_DIM), LOW),
            pltpu.VMEM((heads, tokens), FULL),
            pltpu.VMEM((2 * kw, tokens), FULL),
            pltpu.VMEM((qw, tokens), LOW),
            pltpu.VMEM((tokens, pieces[0].shape[1]), LOW),
            arrivals(len(pieces)),
        ],
        compiler_params=PARAMS,
        name="attend_back",
    )(order, rank, *pieces, output, qrot, kv, mix, lse, cosine, sine, inv)


def layer(seq_size, fsdp_size, tokens, positions, attn_gain, query_weight, key_weight, value_weight, output_weight,
          ffn_gain, gate_weight, up_weight, down_weight, cotangent):
    span, width = tokens.shape[1:]
    heads = HEADS // seq_size
    kvs = max(1, KV_HEADS // seq_size)
    shared = max(1, seq_size // KV_HEADS)
    qw, kw = heads * HEAD_DIM, kvs * HEAD_DIM
    own_rows = query_weight.shape[0]
    hidden_own = gate_weight.shape[1] // seq_size
    chunk = 128 if hidden_own % 128 == 0 else 64
    parts = 2 if seq_size == 4 else 1
    piece_rows = span // parts
    into, back = (seq_size, fsdp_size, own_rows), (fsdp_size, seq_size, own_rows)
    here = lax.axis_index("seq")

    def after(x, *others):
        return lax.optimization_barrier((x, *others))[0]

    def swap(x, j):
        return lax.ppermute(x, "seq", [(i, i ^ j) for i in range(seq_size)])

    def seq_gather(own):
        if parts == 1:
            return [own[0]] + [swap(own[0], j) for j in range(1, seq_size)]
        a, b = own
        ax, by = swap(a, 1), swap(b, 2)
        ay, bx = swap(a, 2), swap(b, 1)
        ad, bd = swap(ax, 2), swap(by, 1)
        return [a, b, ax, bx, ay, by, ad, bd]

    def scatter_start(pieces):
        if parts == 1:
            return [swap(pieces[j], j) for j in range(1, seq_size)]
        a, b = pieces[::2], pieces[1::2]
        return [swap(a[3], 2), swap(b[3], 1), swap(a[2], 2), swap(b[1], 1)]

    def scatter_end(pieces, came):
        if parts == 1:
            return (), [pieces[0], *came]
        a, b, (da, db, ya, xb) = pieces[::2], pieces[1::2], came
        da = (a[1].astype(FULL) + da.astype(FULL)).astype(LOW)
        db = (b[2].astype(FULL) + db.astype(FULL)).astype(LOW)
        return (da, db), [a[0], ya, swap(da, 1), b[0], xb, swap(db, 2)]

    def seq_scatter(pieces):
        return scatter_end(pieces, scatter_start(pieces))

    def spread(pieces_for):
        got = [pieces_for(here)] + [swap(pieces_for(here ^ j), j) for j in range(1, seq_size)]
        stack = jnp.stack(got)
        return jnp.concatenate(
            [lax.dynamic_index_in_dim(stack, here ^ t, 0, False) for t in range(seq_size)], 0
        )

    def collect(x):
        blocks = x.reshape(seq_size, own_rows, x.shape[1])
        return [lax.dynamic_index_in_dim(blocks, here, 0, False)] + [
            swap(lax.dynamic_index_in_dim(blocks, here ^ j, 0, False), j) for j in range(1, seq_size)
        ]

    def in_order(got):
        got = jnp.stack(got)
        return jnp.stack([lax.dynamic_index_in_dim(got, here ^ t, 0, False) for t in range(seq_size)]).astype(FULL)

    def fsdp_gather(x):
        return lax.all_gather(x, FSDP, axis=0, tiled=True)

    def exchange(x):
        return lax.ppermute(x, "core", [(0, 1), (1, 0)])

    def chip_scatter(x):
        return lax.psum_scatter(x.reshape(-1, x.shape[-1]), "chip", scatter_dimension=0, tiled=True)

    def fsdp_scatter(x):
        return lax.psum_scatter(x, FSDP, scatter_dimension=0, tiled=True)

    gain_one, gain_two = attn_gain.astype(FULL)[:, None], ffn_gain.astype(FULL)[:, None]

    def with_gain(weight, gain):
        return (weight.astype(FULL) * gain).astype(LOW)

    query_low, key_low, value_low = (with_gain(w, gain_one) for w in (query_weight, key_weight, value_weight))

    def qkv_for(t):
        first = (t * heads // GROUP) * HEAD_DIM
        return jnp.concatenate([
            lax.dynamic_slice_in_dim(query_low, t * qw, qw, 1),
            lax.dynamic_slice_in_dim(key_low, first, kw, 1),
            lax.dynamic_slice_in_dim(value_low, first, kw, 1),
        ], 1)

    count = positions.shape[1] // span
    where_at = positions[0].reshape(count, span)
    where_at = jnp.stack([lax.dynamic_index_in_dim(where_at, here ^ j, 0, False) for j in range(count)])
    rank = where_at[:, 0] // span
    order = jnp.argsort(rank).astype(jnp.int32)
    cosine, sine = rope_tables(where_at.reshape(-1))

    own_tokens = tokens[0]
    own_pieces = call_own(
        functools.partial(regroup_kernel, into), (like((piece_rows, width)),) * parts, own_tokens
    )
    token_pieces = seq_gather(own_pieces)
    output_own = output_weight.reshape(own_rows, seq_size, -1).swapaxes(0, 1).reshape(seq_size * own_rows, -1)
    projections = fsdp_gather(jnp.concatenate([output_own, spread(qkv_for)], 1))
    gate_weight, up_weight = lax.optimization_barrier((gate_weight, up_weight, *own_pieces, order, cosine, sine))[:2]
    gate_low, up_low = with_gain(gate_weight, gain_two), with_gain(up_weight, gain_two)

    def gate_up_for(t):
        gate = lax.dynamic_slice_in_dim(gate_low, t * hidden_own, hidden_own, 1)
        up = lax.dynamic_slice_in_dim(up_low, t * hidden_own, hidden_own, 1)
        return jnp.concatenate(
            [x[:, c:c + chunk] for c in range(0, hidden_own, chunk) for x in (gate, up)], 1
        )

    gate_up_own = spread(gate_up_for)
    gate_up_full = fsdp_gather(gate_up_own)
    down_full = fsdp_gather(down_weight)
    own_upstream = after(cotangent[0], gate_up_own, *token_pieces)
    upstream = [own_upstream] + [swap(own_upstream, j) for j in range(1, seq_size)]

    qrot, kv, attended, mix, lse, inv_one = attend(
        order, rank, token_pieces, projections, cosine, sine, heads, kvs, span
    )
    branch = rows_of_product(attended, projections, piece_rows, into)
    branch, upstream = lax.optimization_barrier((branch, upstream))
    branch = seq_scatter(branch)[1]
    middle, inv_two, *own_pieces = call_own(
        functools.partial(middle_kernel, into, parts),
        (like((span, width), FULL), like((span, 1), FULL)) + (like((piece_rows, width)),) * parts,
        own_tokens, *branch, params=SMALL,
    )

    normed_pieces = seq_gather(own_pieces)
    slope, hidden, normed = hidden_of(normed_pieces, gate_up_full, chunk)
    part_down = grad_down_of(hidden, upstream)
    grad_down = fsdp_scatter(part_down)
    grad_gate_up = grad_gate_up_of([after(upstream[0], part_down), *upstream[1:]], down_full, slope, chunk)
    first, grad_pieces = seq_scatter(grad_rows_of(grad_gate_up, gate_up_full, piece_rows))
    place, core = (at.astype(jnp.int32).reshape(1) for at in (here, lax.axis_index("core")))
    part_gate_up = grad_weight_of(
        after(normed, *first), exchange(normed), grad_gate_up, exchange(grad_gate_up), core, fsdp_size // 2
    )
    part_gate_up, *grad_pieces = lax.optimization_barrier((part_gate_up, *grad_pieces))
    grad_gate_up_own = chip_scatter(part_gate_up)
    grad_pieces[0] = after(grad_pieces[0], grad_down)
    grad_middle, *own_pieces = call_own(
        functools.partial(grad_middle_kernel, back, parts),
        (like((span, width), FULL),) + (like((piece_rows, width)),) * parts,
        cotangent[0], middle, inv_two, *grad_pieces,
    )

    branch_pieces = seq_gather(own_pieces)
    out_pieces = rows_of_product(after(hidden, own_pieces[0]), down_full, piece_rows)
    out_pieces = lax.optimization_barrier((*out_pieces, *branch_pieces))[:len(out_pieces)]
    out_came = scatter_start(out_pieces)
    grad_qkv, grad_qkv_turned = attend_back(
        order, rank, branch_pieces, projections.reshape(fsdp_size, seq_size, own_rows, -1), qrot, kv, mix, lse,
        cosine, sine, inv_one, heads, kvs, span,
    )
    grad_qkv, grad_qkv_turned, *out_came = lax.optimization_barrier((grad_qkv, grad_qkv_turned, *out_came))
    part_projections = attention_weights_of(token_pieces, branch_pieces, grad_qkv, attended, into)
    grad_pieces = grad_rows_of(grad_qkv_turned, projections, piece_rows)
    came = scatter_start(grad_pieces)
    grad_projections = fsdp_scatter(after(part_projections, grad_gate_up_own, *came[:2]))
    grad_pieces = scatter_end(grad_pieces, came)[1]
    got = collect(after(grad_gate_up_own, *grad_pieces))
    out_pieces = scatter_end(out_pieces, out_came)[1]
    block_out = call_own(functools.partial(block_out_kernel, parts), like((span, width)), middle, *out_pieces)


    def whole_rows(x):
        return x.swapaxes(0, 1).reshape(own_rows, -1)

    if chunk == 128:
        rows_like = like((own_rows, gate_weight.shape[1]), FULL)
        grad_gate, grad_up, grad_ffn_gain = call_own(
            finish_gate_up_kernel, (rows_like, rows_like, like((1, own_rows), FULL)),
            *got, gate_weight, up_weight, gain_two, scalars=(place,),
        )
    else:
        got = in_order(got).reshape(seq_size, own_rows, -1, 2, chunk)
        grad_gate, grad_up = whole_rows(got[:, :, :, 0]), whole_rows(got[:, :, :, 1])
        grad_ffn_gain = jnp.sum(grad_gate * gate_weight.astype(FULL) + grad_up * up_weight.astype(FULL), 1)
        grad_gate, grad_up = grad_gate * gain_two, grad_up * gain_two
    grad_tokens = call_own(
        functools.partial(grad_tokens_kernel, back, parts), like((span, width), FULL),
        own_tokens, grad_middle, *grad_pieces,
    )
    grad_projections = after(grad_projections, grad_tokens, block_out, grad_ffn_gain)
    got = collect(grad_projections[:, -qw - 2 * kw:])
    if shared == 1 and kvs == 1:
        grad_query, grad_key, grad_value, grad_output, grad_attn_gain = call_own(
            finish_projections_kernel,
            tuple(like(w.shape, FULL) for w in (query_weight, key_weight, value_weight, output_weight))
            + (like((1, own_rows), FULL),),
            *got, grad_projections, query_weight, key_weight, value_weight, gain_one, scalars=(place,), params=SMALL,
        )
    else:
        grad_output = grad_projections[:, :-qw - 2 * kw].reshape(seq_size, own_rows, -1).swapaxes(0, 1)
        grad_output = grad_output.reshape(own_rows, width).astype(FULL)
        got = in_order(got)
        grad_query = whole_rows(got[:, :, :qw])

        def of_heads(x):
            return whole_rows(x.reshape(seq_size // shared, shared, own_rows, kw).sum(1))

        grad_key, grad_value = of_heads(got[:, :, qw:qw + kw]), of_heads(got[:, :, qw + kw:])
        grads = (grad_query, grad_key, grad_value)
        grad_attn_gain = sum(
            jnp.sum(g * w.astype(FULL), 1) for g, w in zip(grads, (query_weight, key_weight, value_weight))
        )
        grad_query, grad_key, grad_value = (g * gain_one for g in grads)
    return (
        block_out[None],
        grad_tokens[None],
        grad_attn_gain.reshape(-1),
        grad_query,
        grad_key,
        grad_value,
        grad_output,
        grad_ffn_gain.reshape(-1),
        grad_gate,
        grad_up,
        grad_down.astype(FULL),
    )


def solution(mesh):
    seq_size, fsdp_size = mesh.shape["seq"], mesh.shape["fsdp"]
    split = Mesh(mesh.devices.reshape(seq_size, fsdp_size // 2, 2), ("seq", "chip", "core"))
    rows, vector, matrix = P(FSDP, "seq", None), P(("seq", *FSDP)), P(("seq", *FSDP), None)
    return jax.shard_map(
        functools.partial(layer, seq_size, fsdp_size),
        mesh=split,
        in_specs=(
            rows, P(FSDP, None), vector, matrix, matrix, matrix, matrix, vector, matrix, matrix, matrix, rows,
        ),
        out_specs=(rows, rows, vector, matrix, matrix, matrix, matrix, vector, matrix, matrix, matrix),
        check_vma=False,
    )
```
